32 devices in a mesh: section: 2 (over x), dp: 16 (over z, y, core).
Axes of the slice: x: 2, y: 2, z: 4, core: 2. Of those that a mesh axis runs over, the one named last changes fastest.
Arguments:
- tokens: bfloat16 [64, 256, 640], P('dp'), may hold values from -6 to 6
- lengths: int32 [64], P('dp'), may hold values from 64 to 256
- cotangent: bfloat16 [64, 256, 640], P('dp'), may hold values from -6 to 6
- w_qkv: bfloat16 [2, 640, 1920], P('section', 'dp'), may hold values from -0.25 to 0.25
- w_out: bfloat16 [2, 640, 640], P('section', 'dp'), may hold values from -1 to 1
- w_up: bfloat16 [2, 640, 5120], P('section', 'dp'), may hold values from -0.25 to 0.25
- w_down: bfloat16 [2, 5120, 640], P('section', 'dp'), may hold values from -0.078125 to 0.078125
- norm_gain: bfloat16 [2, 2, 640], P('section', None, 'dp'), may hold values from 0.25 to 1.75
- norm_bias: bfloat16 [2, 2, 640], P('section', None, 'dp'), may hold values from -1 to 1
- bias_vec: bfloat16 [2, 4, 640], P('section', None, 'dp'), may hold values from -1 to 1
- up_bias: bfloat16 [2, 5120], P('section', 'dp'), may hold values from -1 to 1
Outputs:
- hidden_out: bfloat16 [2, 64, 256, 640], P('section', 'dp')
- input_grads: float32 [2, 64, 256, 640], P('section', 'dp')
- grad_qkv: float32 [2, 640, 1920], P('section', 'dp')
- grad_out: float32 [2, 640, 640], P('section', 'dp')
- grad_up: float32 [2, 640, 5120], P('section', 'dp')
- grad_down: float32 [2, 5120, 640], P('section', 'dp')
- grad_gain: float32 [2, 2, 640], P('section', None, 'dp')
- grad_norm_bias: float32 [2, 2, 640], P('section', None, 'dp')
- grad_bias_vec: float32 [2, 4, 640], P('section', None, 'dp')
- grad_up_bias: float32 [2, 5120], P('section', 'dp')
The draws below stay inside these ranges and needn't reach their ends.
All inputs are finite; a program needn't handle non-finite values.
Results may differ from the reference program's by a relative error of at most 0.015.
Values may be sent and summed in bfloat16 or wider, within the bound.
No kernel may reach another device: no remote copies, remote signals or barrier semaphores. Data moves between devices by JAX's collectives and lax.ppermute only.
A program may use at most 320 MiB of HBM per device.

```python
import math
import jax
import jax.numpy as jnp
from jax import lax

D = 640
HEADS = 20
HEAD_DIM = 32
FF = 5120
SLOT = 256
SEQS = 64


def plant(array, key, low, high):
    shape = array.shape
    place = [jax.random.randint(jax.random.fold_in(key, axis), (), 0, shape[axis]) for axis in range(len(shape))]
    array = array.at[tuple(place)].set(low)
    longest = shape.index(max(shape))
    place[longest] = (place[longest] + 1) % shape[longest]
    return array.at[tuple(place)].set(high)


def with_spikes(drawn, key, source, target, parts, factor):
    def block_of(axis_at):
        return (jnp.arange(drawn.shape[axis_at]) // (drawn.shape[axis_at] // parts)).reshape((-1,) + (1,) * (drawn.ndim - 1 - axis_at))

    near = jax.random.permutation(key, parts)[block_of(target)]
    other_side = (block_of(target) + parts // 2) % parts
    return jnp.where((block_of(source) == near) | (block_of(source) == other_side), factor * drawn, drawn)


def block_levels(key, dims, shards, least, top_value):
    def one(position, parts):
        draws = jax.random.uniform(jax.random.fold_in(jax.random.fold_in(key, 6), position), (parts,), jnp.float32, least / len(shards), top_value / len(shards))
        return jnp.repeat(jnp.exp(draws), dims[position] // parts).reshape((-1,) + (1,) * (len(dims) - position - 1))

    level = one(*shards[0])
    for cut in shards[1:]:
        level = level * one(*cut)
    return level


def centred(key, extent, scale, bound, cuts=(), kind=jnp.bfloat16):
    array = jax.random.normal(key, extent, jnp.float32) * scale
    if len(cuts) > 0:
        array = block_levels(key, extent, cuts, -0.22, 0.18) * array
    return jnp.clip(array, min=-bound, max=bound).astype(kind)


def noise_with(key, extent, scale, reach, pieces, heavy, kind=jnp.bfloat16):
    array = scale * jax.random.normal(key, extent, jnp.float32)
    if pieces:
        array = array * block_levels(key, extent, pieces, -0.22, 0.18)
    return jnp.clip(with_spikes(array, jax.random.fold_in(key, 3), *heavy), -reach, reach).astype(kind)


def setup_inputs(seed: int = 0) -> dict:
    streams_of = jax.random.split(jax.random.key(seed), 12)
    return {
        "tokens": centred(streams_of[0], (SEQS, SLOT, D), 1.0, 6.0, ((0, 16),)),
        "lengths": plant(jax.random.randint(streams_of[1], (SEQS,), SLOT // 4, SLOT + 1), jax.random.fold_in(streams_of[1], 1), SLOT // 4, SLOT).astype(jnp.int32),
        "cotangent": noise_with(streams_of[2], (SEQS, SLOT, D), 1.0, 6.0, ((0, 16),), (0, 2, 16, 2.0)),
        "w_qkv": centred(streams_of[3], (2, D, 3 * D), D ** -0.5, 0.25, ((0, 2), (1, 16))),
        "w_out": centred(streams_of[4], (2, D, D), (D // 16) ** -0.5, 1.0, ((0, 2), (1, 16))),
        "w_up": centred(streams_of[5], (2, D, FF), D ** -0.5, 0.25, ((0, 2), (1, 16))),
        "w_down": centred(streams_of[6], (2, FF, D), FF ** -0.5, 0.078125, ((0, 2), (1, 16))),
        "norm_gain": jnp.clip(1.0 + 0.15 * jax.random.normal(streams_of[7], (2, 2, D), jnp.float32), 0.25, 1.75).astype(jnp.bfloat16),
        "norm_bias": centred(streams_of[8], (2, 2, D), 0.2, 1.0, ((0, 2), (2, 16))),
        "bias_vec": centred(streams_of[9], (2, 4, D), 0.2, 1.0, ((0, 2), (2, 16))),
        "up_bias": centred(streams_of[10], (2, FF), 0.2, 1.0, ((0, 2), (1, 16))),
    }


@jax.custom_vjp
def low(v):
    return lax.optimization_barrier(v.astype(jnp.bfloat16)).astype(jnp.float32)

@jax.custom_vjp
def low_back(v):
    return v

def low_keep(v):
    return (low(v), None)

def low_pass(kept, grad):
    return (grad,)

def back_keep(v):
    return (v, None)

def back_low(kept, grad):
    return (low(grad),)
low.defvjp(low_keep, low_pass)
low_back.defvjp(back_keep, back_low)

def layer_norm(values, gain, shift):
    centered = values - lax.optimization_barrier(jnp.mean(values, axis=-1, keepdims=True))
    spread = lax.optimization_barrier(jnp.mean(centered * centered, axis=-1, keepdims=True))
    return centered * lax.rsqrt(spread + 1e-05) * gain + shift

def encoder_layer(hidden, window_len, params):
    w_qkv, w_out, w_up, w_down, gains, shifts, biases, up_bias = params
    top = lax.Precision.HIGHEST
    groups, seq_len, width = hidden.shape
    normed = low(layer_norm(hidden, gains[0], shifts[0]))
    bias_qkv = jnp.concatenate([biases[0], jnp.zeros_like(biases[0]), biases[1]])
    qkv = low_back(low(jnp.einsum('bsd,de->bse', normed, w_qkv, precision=top) + bias_qkv))
    query = qkv[..., :width].reshape(groups, seq_len, HEADS, HEAD_DIM)
    key_part = qkv[..., width:2 * width].reshape(groups, seq_len, HEADS, HEAD_DIM)
    value = qkv[..., 2 * width:].reshape(groups, seq_len, HEADS, HEAD_DIM)
    raw = low_back(jnp.einsum('bqhe,bkhe->bhqk', query, key_part, precision=top))
    valid = (jnp.arange(seq_len)[None, :] < window_len[:, None])[:, None, None, :]
    scores = jnp.where(valid, raw * HEAD_DIM ** (-0.5), -1e+30)
    highest = lax.optimization_barrier(jnp.max(scores, axis=-1, keepdims=True))
    expo = jnp.exp(scores - highest)
    probs = expo / lax.optimization_barrier(jnp.sum(expo, axis=-1, keepdims=True))
    probs_low = low(probs)
    mixed = jnp.einsum('bhqk,bkhe->bqhe', probs_low, value, precision=top).reshape(groups, seq_len, width)
    mixed = low_back(low(mixed))
    middle = hidden + low_back(jnp.einsum('bsd,de->bse', mixed, w_out, precision=top) + biases[2])
    normed_two = low(layer_norm(middle, gains[1], shifts[1]))
    pre = low_back(jnp.einsum('bsd,df->bsf', normed_two, w_up, precision=top) + up_bias)
    act = low(jax.nn.gelu(pre, approximate=False))
    return middle + low_back(jnp.einsum('bsf,fd->bsd', act, w_down, precision=top) + biases[3])

def reference(tokens, lengths, cotangent, w_qkv, w_out, w_up, w_down, norm_gain, norm_bias, bias_vec, up_bias):
    params = tuple((a.astype(jnp.float32) for a in (w_qkv, w_out, w_up, w_down, norm_gain, norm_bias, bias_vec, up_bias)))
    per_group = math.gcd(SEQS, 8)
    count = SEQS // per_group
    inputs = tokens.astype(jnp.float32).reshape(count, per_group, SLOT, D)
    grouped_len = lengths.reshape(count, per_group)
    extra = jnp.zeros((count, per_group, SLOT, D), jnp.float32)

    def two_layers(weights, window, window_len, added):
        first = tuple((a[0] for a in weights))
        second = tuple((a[1] for a in weights))
        middle_out = low_back(low(encoder_layer(window, window_len, first))) + added
        return (middle_out, encoder_layer(middle_out, window_len, second))
    checked = jax.checkpoint(two_layers)

    def whole(weights, windows, added_all):

        def scan_step(carry, items):
            return (carry, checked(weights, items[0], items[1], items[2]))
        _, results = lax.scan(scan_step, jnp.zeros((), jnp.float32), (windows, grouped_len, added_all))
        return results
    (first_out, second_out), pull = jax.vjp(whole, params, inputs, extra)
    upstream_grads = (jnp.zeros_like(first_out), cotangent.astype(jnp.float32).reshape(count, per_group, SLOT, D))
    grads, grad_tokens, grad_middle = pull(upstream_grads)
    hidden_out = jnp.stack([first_out, second_out]).reshape(2, SEQS, SLOT, D).astype(jnp.bfloat16)
    input_grads = jnp.stack([grad_tokens, grad_middle]).reshape(2, SEQS, SLOT, D)
    return (hidden_out, input_grads, grads[0], grads[1], grads[2], grads[3], grads[4], grads[5], grads[6], grads[7])
```

```python
import jax
import jax.numpy as jnp
from jax import lax
from jax.experimental import pallas as pl
from jax.experimental.pallas import tpu as pltpu
from jax.sharding import PartitionSpec as P

HEADS = 20
HEAD_DIM = 32
GROUP = 128 // HEAD_DIM
SCALE = HEAD_DIM ** -0.5
VMEM_LIMIT = 56 * 1024 * 1024
F32 = jnp.float32
BF16 = jnp.bfloat16


def dot(a, b, dims=((1,), (0,))):
    return lax.dot_general(a, b, (dims, ((), ())), preferred_element_type=F32)


def gelu_pair(u):
    mag = jnp.abs(u)
    t = 1.0 / (1.0 + (0.3275911 * 0.7071067811865476) * mag)
    e = jnp.exp(-0.5 * (u * u))
    poly = t * (0.5 * 0.254829592 + t * (0.5 * -0.284496736 + t * (0.5 * 1.421413741 + t * (0.5 * -1.453152027 + t * (0.5 * 1.061405429)))))
    tail = poly * e
    phi_cap = jnp.where(u < 0, tail, 1.0 - tail)
    return u * phi_cap, phi_cap + (0.3989422804014327 * u) * e


def normed(v, gain, shift):
    centered = v - jnp.mean(v, axis=-1, keepdims=True)
    spread = jnp.mean(centered * centered, axis=-1, keepdims=True)
    hat = centered * lax.rsqrt(spread + 1e-05)
    return hat * gain + shift


def norm_back(v, gain, grad):
    centered = v - jnp.mean(v, axis=-1, keepdims=True)
    spread = jnp.mean(centered * centered, axis=-1, keepdims=True)
    inv = lax.rsqrt(spread + 1e-05)
    hat = centered * inv
    g = grad * gain
    back = inv * (g - jnp.mean(g, axis=-1, keepdims=True) - hat * jnp.mean(g * hat, axis=-1, keepdims=True))
    return back, jnp.sum(grad * hat, axis=0, keepdims=True), jnp.sum(grad, axis=0, keepdims=True)


def attn_fwd_body(save, len_ref, h_ref, wqkv_ref, vec_ref, *outs):
    if save:
        m_ref, c_ref, qkv_ref, p_ref, o_ref, a_ref = outs
    else:
        m_ref, c_ref = outs
    width = h_ref.shape[2]
    seq = h_ref.shape[1]
    length = len_ref[pl.program_id(0)]
    h = h_ref[0].astype(F32)
    vec = vec_ref[...]
    a = normed(h, vec[0:1], vec[2:3]).astype(BF16)
    q_all = (dot(a, wqkv_ref[:, :width]) + vec[4:5]).astype(BF16)
    k_all = dot(a, wqkv_ref[:, width:2 * width]).astype(BF16)
    v_all = (dot(a, wqkv_ref[:, 2 * width:3 * width]) + vec[5:6]).astype(BF16)
    if save:
        a_ref[0] = a
        qkv_ref[0, :, :width] = q_all
        qkv_ref[0, :, width:2 * width] = k_all
        qkv_ref[0, :, 2 * width:] = v_all
    valid = lax.broadcasted_iota(jnp.int32, (1, seq), 1) < length
    head_of = lax.broadcasted_iota(jnp.int32, (1, 128), 1) // HEAD_DIM
    mixed = []
    for g in range(width // 128):
        at = slice(128 * g, 128 * g + 128)
        q, k, v = q_all[:, at], k_all[:, at], v_all[:, at]
        acc = None
        for j in range(GROUP):
            mine = head_of == j
            s = dot(jnp.where(mine, q, jnp.zeros_like(q)), k, ((1,), (1,)))
            s = jnp.where(valid, s * SCALE, -1e30)
            e = jnp.exp(s - jnp.max(s, axis=1, keepdims=True))
            pb = (e * (1.0 / jnp.sum(e, axis=1, keepdims=True))).astype(BF16)
            if save:
                p_ref[0, GROUP * g + j] = pb
            part = dot(pb, jnp.where(mine, v, jnp.zeros_like(v)))
            acc = part if acc is None else acc + part
        mixed.append(acc.astype(BF16))
    o = jnp.concatenate(mixed, axis=1)
    if save:
        o_ref[0] = o
    m = h + dot(o, wqkv_ref[:, 3 * width:4 * width]) + vec[6:7]
    m_ref[0] = m
    c_ref[0] = normed(m, vec[1:2], vec[3:4]).astype(BF16)


def whole(shape):
    return pl.BlockSpec(shape, lambda *_: (0,) * len(shape))


def attn_fwd(h, lengths, proj, vec, save):
    n, seq, width = h.shape
    row = lambda *tail: pl.BlockSpec((1,) + tail, lambda i, *_: (i,) + (0,) * len(tail))
    shapes = [((seq, width), F32), ((seq, width), BF16)]
    if save:
        shapes += [((seq, 3 * width), BF16), ((HEADS, seq, seq), BF16), ((seq, width), BF16), ((seq, width), BF16)]
    return pl.pallas_call(
        lambda *refs: attn_fwd_body(save, *refs),
        grid_spec=pltpu.PrefetchScalarGridSpec(
            num_scalar_prefetch=1,
            grid=(n,),
            in_specs=[row(seq, width), whole(proj.shape), whole(vec.shape)],
            out_specs=[row(*s) for s, _ in shapes],
        ),
        out_shape=[jax.ShapeDtypeStruct((n,) + s, d) for s, d in shapes],
        compiler_params=pltpu.CompilerParams(vmem_limit_bytes=VMEM_LIMIT),
        name="attention_forward",
    )(lengths, h, proj, vec)


def mlp_fwd_body(save, rows, c_ref, m_ref, wup_ref, wdown_ref, bup_ref, vec_ref, *outs):
    if save:
        y_ref, g_ref, gp_ref, acc_ref = outs
    else:
        y_ref, acc_ref = outs
    step = pl.program_id(0)

    @pl.when(step == 0)
    def _():
        acc_ref[...] = m_ref[...] + vec_ref[7:8]

    for r in range(c_ref.shape[0] // rows):
        at = slice(r * rows, r * rows + rows)
        u = dot(c_ref[at], wup_ref[...]) + bup_ref[...]
        act, slope = gelu_pair(u)
        act = act.astype(BF16)
        if save:
            g_ref[at] = act
            gp_ref[at] = slope.astype(BF16)
        acc_ref[at] += dot(act, wdown_ref[...])

    @pl.when(step == pl.num_programs(0) - 1)
    def _():
        y_ref[...] = acc_ref[...].astype(BF16)


def mlp_fwd(c, m, wup, wdown, bup, vec, save, chunk=512, rows=256):
    n, width = c.shape
    ff = wup.shape[1]
    outs = [jax.ShapeDtypeStruct((n, width), BF16)]
    specs = [whole((n, width))]
    if save:
        outs += [jax.ShapeDtypeStruct((n, ff), BF16)] * 2
        specs += [pl.BlockSpec((n, chunk), lambda i: (0, i))] * 2
    return pl.pallas_call(
        lambda *refs: mlp_fwd_body(save, rows, *refs),
        grid=(ff // chunk,),
        in_specs=[whole(c.shape), whole(m.shape), pl.BlockSpec((width, chunk), lambda i: (0, i)),
                  pl.BlockSpec((chunk, width), lambda i: (i, 0)), pl.BlockSpec((1, chunk), lambda i: (0, i)), whole(vec.shape)],
        out_specs=specs,
        out_shape=outs,
        scratch_shapes=[pltpu.VMEM((n, width), F32)],
        compiler_params=pltpu.CompilerParams(vmem_limit_bytes=VMEM_LIMIT),
        name="feed_forward",
    )(c, m, wup, wdown, bup, vec)


def mlp_bwd_body(grads, rows, dz_ref, gp_ref, wup_ref, wdown_ref, *rest):
    if grads:
        g_ref, c_ref, dc_ref, gup_ref, gdown_ref, gbu_ref, du_ref, ct_ref = rest
    else:
        dc_ref, = rest
    step = pl.program_id(0)
    n = dz_ref.shape[0]
    width = dz_ref.shape[1]

    @pl.when(step == 0)
    def _():
        dc_ref[...] = jnp.zeros_like(dc_ref)
        if grads:
            ct_ref[:width] = c_ref[...].T
            ct_ref[width:] = jnp.ones_like(ct_ref[width:])

    for r in range(n // rows):
        at = slice(r * rows, r * rows + rows)
        dg = dot(dz_ref[at], wdown_ref[...], ((1,), (1,)))
        du = (dg * gp_ref[at].astype(F32)).astype(BF16)
        if grads:
            du_ref[at] = du
        dc_ref[at] += dot(du, wup_ref[...], ((1,), (1,)))
    if grads:
        gup = dot(ct_ref[...], du_ref[...])
        gup_ref[...] = gup[:width].astype(BF16)
        gbu_ref[...] = gup[width:width + 8]
        gdown_ref[...] = dot(g_ref[...], dz_ref[...], ((0,), (0,))).astype(BF16)


def mlp_bwd(dz, gp, wup, wdown, g=None, c=None, chunk=512, rows=256):
    n, width = dz.shape
    ff = wup.shape[1]
    grads = g is not None
    col = pl.BlockSpec((n, chunk), lambda i: (0, i))
    args = [dz, gp, wup, wdown]
    in_specs = [whole(dz.shape), col, pl.BlockSpec((width, chunk), lambda i: (0, i)), pl.BlockSpec((chunk, width), lambda i: (i, 0))]
    outs = [jax.ShapeDtypeStruct((n, width), F32)]
    specs = [whole((n, width))]
    scratch = []
    if grads:
        args += [g, c]
        in_specs += [col, whole(c.shape)]
        outs += [jax.ShapeDtypeStruct((width, ff), BF16), jax.ShapeDtypeStruct((ff, width), BF16), jax.ShapeDtypeStruct((8, ff), F32)]
        specs += [pl.BlockSpec((width, chunk), lambda i: (0, i)), pl.BlockSpec((chunk, width), lambda i: (i, 0)), pl.BlockSpec((8, chunk), lambda i: (0, i))]
        scratch = [pltpu.VMEM((n, chunk), BF16), pltpu.VMEM((width + 16, n), BF16)]
    return pl.pallas_call(
        lambda *refs: mlp_bwd_body(grads, rows, *refs),
        grid=(ff // chunk,),
        in_specs=in_specs,
        out_specs=specs,
        out_shape=outs,
        scratch_shapes=scratch,
        compiler_params=pltpu.CompilerParams(vmem_limit_bytes=VMEM_LIMIT),
        name="feed_forward_back",
    )(*args)


def attn_bwd_body(dc_ref, dz_ref, m_ref, h_ref, qkv_ref, p_ref, proj_ref, vec_ref, dh_ref, dr_ref, dqkv_ref, small_ref):
    width = h_ref.shape[2]
    vec = vec_ref[...]

    @pl.when(pl.program_id(0) == 0)
    def _():
        small_ref[...] = jnp.zeros_like(small_ref)

    dz = dz_ref[0].astype(F32)
    back, g_gain1, g_shift1 = norm_back(m_ref[0], vec[1:2], dc_ref[0])
    dm = dz + back
    dr = dm.astype(BF16)
    dr_ref[0] = dr
    do_all = dot(dr, proj_ref[:, 3 * width:4 * width], ((1,), (1,))).astype(BF16)
    head_of = lax.broadcasted_iota(jnp.int32, (1, 128), 1) // HEAD_DIM
    dq_all, dk_all, dv_all = [], [], []
    for g in range(width // 128):
        at = slice(128 * g, 128 * g + 128)
        q = qkv_ref[0, :, 128 * g:128 * g + 128]
        k = qkv_ref[0, :, width + 128 * g:width + 128 * g + 128]
        v = qkv_ref[0, :, 2 * width + 128 * g:2 * width + 128 * g + 128]
        do = do_all[:, at]
        do_t, q_t = do.T, q.T
        dq = None
        dk_t, dv_t = [], []
        for j in range(GROUP):
            mine = head_of == j
            zero = jnp.zeros_like(do)
            pb = p_ref[0, GROUP * g + j]
            rows = slice(HEAD_DIM * j, HEAD_DIM * j + HEAD_DIM)
            dv_t.append(dot(do_t[rows], pb))
            dp = dot(jnp.where(mine, do, zero), v, ((1,), (1,)))
            p = pb.astype(F32)
            t = p * dp
            ds = ((t - p * jnp.sum(t, axis=1, keepdims=True)) * SCALE).astype(BF16)
            part = dot(ds, jnp.where(mine, k, zero))
            dq = part if dq is None else dq + part
            dk_t.append(dot(q_t[rows], ds))
        dq_all.append(dq.astype(BF16))
        dk_all.append(jnp.concatenate(dk_t, axis=0).astype(BF16).T)
        dv_all.append(jnp.concatenate(dv_t, axis=0).astype(BF16).T)
    dqkv = jnp.concatenate(dq_all + dk_all + dv_all, axis=1)
    dqkv_ref[0] = dqkv
    da = dot(dqkv, proj_ref[:, :3 * width], ((1,), (1,)))
    back, g_gain0, g_shift0 = norm_back(h_ref[0].astype(F32), vec[0:1], da)
    dh_ref[0] = dm + back
    total = lambda x: jnp.sum(x.astype(F32), axis=0, keepdims=True)
    small_ref[...] += jnp.concatenate(
        [g_gain0, g_gain1, g_shift0, g_shift1, total(dqkv[:, :width]), total(dqkv[:, 2 * width:]), total(dr), total(dz)], axis=0)


def attn_bwd(dc, dz, m, h, qkv, p, proj, vec):
    n, seq, width = h.shape
    row = lambda *tail: pl.BlockSpec((1,) + tail, lambda i, *_: (i,) + (0,) * len(tail))
    shapes = [((seq, width), F32), ((seq, width), BF16), ((seq, 3 * width), BF16)]
    return pl.pallas_call(
        attn_bwd_body,
        grid=(n,),
        in_specs=[row(seq, width), row(seq, width), row(seq, width), row(seq, width), row(seq, 3 * width), row(HEADS, seq, seq),
                  whole(proj.shape), whole(vec.shape)],
        out_specs=[row(*s) for s, _ in shapes] + [whole((8, width))],
        out_shape=[jax.ShapeDtypeStruct((n,) + s, d) for s, d in shapes] + [jax.ShapeDtypeStruct((8, width), F32)],
        compiler_params=pltpu.CompilerParams(vmem_limit_bytes=VMEM_LIMIT),
        name="attention_back",
    )(dc, dz, m, h, qkv, p, proj, vec)


def proj_grad_body(a_ref, dqkv_ref, o_ref, dr_ref, table_ref, out_ref, at_ref):
    step = pl.program_id(0)
    width = a_ref.shape[1]

    @pl.when(step == 0)
    def _():
        at_ref[...] = a_ref[...].T
        out_ref[:, 3 * width:4 * width] = dot(o_ref[...], dr_ref[...], ((0,), (0,))).astype(BF16)
        out_ref[:, 4 * width:] = table_ref[...].astype(BF16)

    out_ref[:, pl.ds(pl.multiple_of(step * width, 128), width)] = dot(at_ref[...], dqkv_ref[...]).astype(BF16)


def proj_grad(a, dqkv, o, dr, table):
    n, width = a.shape
    shape = (width, 4 * width + table.shape[1])
    return pl.pallas_call(
        proj_grad_body,
        grid=(3,),
        in_specs=[whole(a.shape), pl.BlockSpec((n, width), lambda i: (0, i)), whole(o.shape), whole(dr.shape), whole(table.shape)],
        out_specs=whole(shape),
        out_shape=jax.ShapeDtypeStruct(shape, BF16),
        scratch_shapes=[pltpu.VMEM((width, n), BF16)],
        compiler_params=pltpu.CompilerParams(vmem_limit_bytes=VMEM_LIMIT),
        name="projection_gradients",
    )(a, dqkv, o, dr, table)


def places(count):
    return count // 4, 2, 2


def hop(value, kind, step=1):
    zs, ys, cores = places(lax.axis_size("dp"))
    pairs = []
    for z in range(zs):
        for y in range(ys):
            for c in range(cores):
                to = {"core": (z, y, c ^ 1), "y": (z, y ^ 1, c), "z": ((z + step) % zs, y, c)}[kind]
                pairs.append(((z * ys + y) * cores + c, (to[0] * ys + to[1]) * cores + to[2]))
    return lax.ppermute(value, "dp", pairs)


def pick(value, index, axis):
    return lax.dynamic_index_in_dim(value, index, axis, keepdims=False)


def scatter_sum(grad, rows):
    count = lax.axis_size("dp")
    zs, ys, cores = places(count)
    me = lax.axis_index("dp")
    c, y, z = me % cores, (me // cores) % ys, me // (cores * ys)
    columns = grad.shape[1]
    parts = grad.reshape(zs, ys, cores, rows, columns)
    got = hop(pick(parts, 1 - c, 2), "core")
    parts = (pick(parts, c, 2).astype(F32) + got.astype(F32)).astype(BF16)
    got = hop(pick(parts, 1 - y, 1), "y")
    parts = (pick(parts, y, 1).astype(F32) + got.astype(F32)).astype(BF16)
    total = pick(parts, z, 0).astype(F32)
    for step in range(1, zs):
        total = total + hop(pick(parts, (z + step) % zs, 0), "z", step).astype(F32)
    return total


def on_device(tokens, lengths, cotangent, w_qkv, w_out, w_up, w_down, norm_gain, norm_bias, bias_vec, up_bias):
    section = lax.axis_index("section")
    windows, seq, width = tokens.shape
    n = windows * seq
    shard = w_qkv.shape[1]
    per_row = up_bias.shape[1] // shard
    ff = w_up.shape[2]
    table = jnp.concatenate([norm_gain[0], norm_bias[0], bias_vec[0]], axis=0).T
    table = jnp.concatenate([table, up_bias.reshape(shard, per_row)], axis=1)
    used = table.shape[1]
    table = jnp.pad(table, ((0, 0), (0, 128 - used)))
    packed = jnp.concatenate([w_qkv[0], w_out[0], table], axis=1)
    proj = lax.all_gather(packed, "dp", axis=0, tiled=True)
    wup = lax.all_gather(w_up[0], "dp", axis=0, tiled=True)
    wdown = lax.all_gather(w_down[0], "dp", axis=0, tiled=True)
    small = proj[:, 4 * width:4 * width + used]
    vec = small[:, :8].T.astype(F32)
    bup = small[:, 8:].reshape(1, ff).astype(F32)

    m, c = attn_fwd(tokens, lengths, proj, vec, False)
    first, = mlp_fwd(c.reshape(n, width), m.reshape(n, width), wup, wdown, bup, vec, False)
    arrived = lax.ppermute(first.reshape(tokens.shape), "section", [(0, 1)])
    h = jnp.where(section == 0, tokens, arrived)

    m, c, qkv, p, o, a = attn_fwd(h, lengths, proj, vec, True)
    c = c.reshape(n, width)
    y, g, gp = mlp_fwd(c, m.reshape(n, width), wup, wdown, bup, vec, True)

    dc, = mlp_bwd(cotangent.reshape(n, width), gp, wup, wdown)
    dh = attn_bwd(dc.reshape(windows, seq, width), cotangent, m, h, qkv, p, proj, vec)[0]
    arrived = lax.ppermute(dh.astype(BF16), "section", [(1, 0)])
    dz = jnp.where(section == 1, cotangent, arrived)

    dc, g_up, g_down, g_bup = mlp_bwd(dz.reshape(n, width), gp, wup, wdown, g, c)
    sum_down = scatter_sum(g_down, w_down.shape[1])
    sum_up = scatter_sum(g_up, shard)
    dh, dr, dqkv, smalls = attn_bwd(dc.reshape(windows, seq, width), dz, m, h, qkv, p, proj, vec)
    g_table = jnp.concatenate([smalls.T, g_bup[0].reshape(width, per_row)], axis=1)
    g_table = jnp.pad(g_table, ((0, 0), (0, 128 - used)))
    g_proj = proj_grad(a.reshape(n, width), dqkv.reshape(n, 3 * width), o.reshape(n, width), dr.reshape(n, width), g_table)
    sum_proj = scatter_sum(g_proj, shard)
    vectors = sum_proj[:, 4 * width:4 * width + 8].T
    return (
        y.reshape((1,) + tokens.shape),
        dh[None],
        sum_proj[None, :, :3 * width],
        sum_proj[None, :, 3 * width:4 * width],
        sum_up[None],
        sum_down[None],
        vectors[None, 0:2],
        vectors[None, 2:4],
        vectors[None, 4:8],
        sum_proj[:, 4 * width + 8:4 * width + used].reshape(1, -1),
    )


def solution(mesh):
    sharded = [P("section", "dp", None)] * 4 + [P("section", None, "dp")] * 3 + [P("section", "dp")]
    windows = P("dp", None, None)
    out = P("section", "dp", None, None)
    return jax.shard_map(
        on_device, mesh=mesh, in_specs=(windows, P("dp"), windows, *sharded), out_specs=(out, out, *sharded), check_vma=False
    )
```

```python
import jax
import jax.numpy as jnp
from jax import lax
from jax.experimental import pallas as pl
from jax.experimental.pallas import tpu as pltpu
from jax.sharding import PartitionSpec as P

HEADS = 20
HEAD_DIM = 32
GROUP = 128 // HEAD_DIM
SCALE = HEAD_DIM ** -0.5
LOG2E = 1.4426950408889634
VMEM_LIMIT = 56 * 1024 * 1024
F32 = jnp.float32
BF16 = jnp.bfloat16


def cost(us):
    return pl.CostEstimate(flops=int(us * 1.1e9), bytes_accessed=1024, transcendentals=0)


def tied(count):
    return [pl.BlockSpec(memory_space=pl.ANY)] * count


def dot(a, b, dims=((1,), (0,))):
    return lax.dot_general(a, b, (dims, ((), ())), preferred_element_type=F32)


def gelu_pair(u):
    below = 0.5 + 0.5 * lax.erf(u * 0.7071067811865476)
    return u * below, below + (0.3989422804014327 * u) * jnp.exp(-0.5 * (u * u))


def normed(v, gain, shift):
    centered = v - jnp.mean(v, axis=-1, keepdims=True)
    spread = jnp.mean(centered * centered, axis=-1, keepdims=True)
    hat = centered * lax.rsqrt(spread + 1e-05)
    return hat * gain + shift


def norm_back(v, gain, grad):
    centered = v - jnp.mean(v, axis=-1, keepdims=True)
    spread = jnp.mean(centered * centered, axis=-1, keepdims=True)
    inv = lax.rsqrt(spread + 1e-05)
    hat = centered * inv
    g = grad * gain
    back = inv * (g - jnp.mean(g, axis=-1, keepdims=True) - hat * jnp.mean(g * hat, axis=-1, keepdims=True))
    return back, jnp.sum(grad * hat, axis=0, keepdims=True), jnp.sum(grad, axis=0, keepdims=True)


def attn_fwd_body(save, len_ref, h_ref, wqkv_ref, vec_ref, *outs):
    if save:
        m_ref, c_ref, qkv_ref, e_ref, o_ref, a_ref, inv_ref = outs
    else:
        m_ref, c_ref = outs
    width = h_ref.shape[2]
    seq = h_ref.shape[1]
    length = len_ref[pl.program_id(0)]
    h = h_ref[0].astype(F32)
    vec = vec_ref[...]
    a = normed(h, vec[0:1], vec[2:3]).astype(BF16)
    q_all = (dot(a, wqkv_ref[:, :width]) + vec[4:5]).astype(BF16)
    k_all = dot(a, wqkv_ref[:, width:2 * width]).astype(BF16)
    v_all = (dot(a, wqkv_ref[:, 2 * width:3 * width]) + vec[5:6]).astype(BF16)
    if save:
        a_ref[0] = a
        qkv_ref[0, :, :width] = q_all
        qkv_ref[0, :, width:2 * width] = k_all
        qkv_ref[0, :, 2 * width:] = v_all
    head_of = lax.broadcasted_iota(jnp.int32, (1, 128), 1) // HEAD_DIM
    key_at = lax.broadcasted_iota(jnp.int32, (seq, 128), 0)
    lane = lax.broadcasted_iota(jnp.int32, (seq, 128), 1)
    past = jnp.where((lane == 0) & (key_at >= length), -1e30, 0.0).astype(BF16)
    first = jnp.where(lane == 0, 1.0, 0.0).astype(BF16)
    ones = jnp.ones((seq, 128), BF16)
    zero = jnp.zeros((seq, 128), BF16)
    mixed = []
    for g in range(width // 128):
        at = slice(128 * g, 128 * g + 128)
        q, v = q_all[:, at], v_all[:, at]
        k = jnp.concatenate([k_all[:, at], past], axis=1)
        acc, inv = None, None
        for j in range(GROUP):
            mine = head_of == j
            s = dot(jnp.concatenate([jnp.where(mine, q, zero), first], axis=1), k, ((1,), (1,)))
            e = jnp.exp2((s - jnp.max(s, axis=1, keepdims=True)) * (SCALE * LOG2E)).astype(BF16)
            if save:
                e_ref[0, GROUP * g + j] = e
            both_parts = dot(e, jnp.concatenate([jnp.where(mine, v, zero), ones], axis=1))
            one_over = 1.0 / both_parts[:, 128:]
            part = both_parts[:, :128] * one_over
            acc = part if acc is None else acc + part
            inv = one_over if inv is None else jnp.where(mine, one_over, inv)
        mixed.append(acc.astype(BF16))
        if save:
            inv_ref[0, :, at] = inv
    o = jnp.concatenate(mixed, axis=1)
    if save:
        o_ref[0] = o
    m = h + dot(o, wqkv_ref[:, 3 * width:4 * width]) + vec[6:7]
    m_ref[0] = m
    c_ref[0] = normed(m, vec[1:2], vec[3:4]).astype(BF16)


def whole(shape):
    return pl.BlockSpec(shape, lambda *_: (0,) * len(shape))


def attn_fwd(h, lengths, proj, vec, save, after=()):
    n, seq, width = h.shape
    row = lambda *tail: pl.BlockSpec((1,) + tail, lambda i, *_: (i,) + (0,) * len(tail))
    shapes = [((seq, width), F32), ((seq, width), BF16)]
    if save:
        shapes += [((seq, 3 * width), BF16), ((HEADS, seq, seq), BF16), ((seq, width), BF16), ((seq, width), BF16), ((seq, width), F32)]
    waits = len(after)
    return pl.pallas_call(
        lambda *refs: attn_fwd_body(save, *refs[:4], *refs[4 + waits:]),
        grid_spec=pltpu.PrefetchScalarGridSpec(
            num_scalar_prefetch=1,
            grid=(n,),
            in_specs=[row(seq, width), whole(proj.shape), whole(vec.shape)] + tied(waits),
            out_specs=[row(*s) for s, _ in shapes],
        ),
        out_shape=[jax.ShapeDtypeStruct((n,) + s, d) for s, d in shapes],
        compiler_params=pltpu.CompilerParams(vmem_limit_bytes=VMEM_LIMIT),
        cost_estimate=cost(7 * n),
        name="attention_forward",
    )(lengths, h, proj, vec, *after)


def mlp_fwd_body(save, rows, c_ref, m_ref, wup_ref, wdown_ref, bup_ref, vec_ref, *outs):
    if save:
        y_ref, g_ref, gp_ref, acc_ref = outs
    else:
        y_ref, acc_ref = outs
    step = pl.program_id(0)

    @pl.when(step == 0)
    def _():
        acc_ref[...] = m_ref[...] + vec_ref[7:8]

    for r in range(c_ref.shape[0] // rows):
        at = slice(r * rows, r * rows + rows)
        u = dot(c_ref[at], wup_ref[...]) + bup_ref[...]
        act, slope = gelu_pair(u)
        act = act.astype(BF16)
        if save:
            g_ref[at] = act
            gp_ref[at] = slope.astype(BF16)
        acc_ref[at] += dot(act, wdown_ref[...])

    @pl.when(step == pl.num_programs(0) - 1)
    def _():
        y_ref[...] = acc_ref[...].astype(BF16)


def mlp_fwd(c, m, wup, wdown, bup, vec, save, chunk=1280, rows=256):
    n, width = c.shape
    ff = wup.shape[1]
    outs = [jax.ShapeDtypeStruct((n, width), BF16)]
    specs = [whole((n, width))]
    if save:
        outs += [jax.ShapeDtypeStruct((n, ff), BF16)] * 2
        specs += [pl.BlockSpec((n, chunk), lambda i: (0, i))] * 2
    return pl.pallas_call(
        lambda *refs: mlp_fwd_body(save, rows, *refs),
        grid=(ff // chunk,),
        in_specs=[whole(c.shape), whole(m.shape), pl.BlockSpec((width, chunk), lambda i: (0, i)),
                  pl.BlockSpec((chunk, width), lambda i: (i, 0)), pl.BlockSpec((1, chunk), lambda i: (0, i)), whole(vec.shape)],
        out_specs=specs,
        out_shape=outs,
        scratch_shapes=[pltpu.VMEM((n, width), F32)],
        compiler_params=pltpu.CompilerParams(vmem_limit_bytes=VMEM_LIMIT),
        cost_estimate=cost(38),
        name="feed_forward",
    )(c, m, wup, wdown, bup, vec)


def mlp_up_body(rows, c_ref, wup_ref, bup_ref, g_ref):
    for r in range(c_ref.shape[0] // rows):
        at = slice(r * rows, r * rows + rows)
        g_ref[at] = gelu_pair(dot(c_ref[at], wup_ref[...]) + bup_ref[...])[0].astype(BF16)


def mlp_up(c, wup, bup, after=(), chunk=1280, rows=256):
    n, width = c.shape
    ff = wup.shape[1]
    waits = len(after)
    return pl.pallas_call(
        lambda *refs: mlp_up_body(rows, *refs[:3], *refs[3 + waits:]),
        grid=(ff // chunk,),
        in_specs=[whole(c.shape), pl.BlockSpec((width, chunk), lambda i: (0, i)), pl.BlockSpec((1, chunk), lambda i: (0, i))] + tied(waits),
        out_specs=pl.BlockSpec((n, chunk), lambda i: (0, i)),
        out_shape=jax.ShapeDtypeStruct((n, ff), BF16),
        compiler_params=pltpu.CompilerParams(vmem_limit_bytes=VMEM_LIMIT),
        cost_estimate=cost(0.027 * n),
        name="feed_forward_up",
    )(c, wup, bup, *after)


def mlp_down_body(g_ref, m_ref, wdown_ref, vec_ref, y_ref, acc_ref):
    step = pl.program_id(0)

    @pl.when(step == 0)
    def _():
        acc_ref[...] = m_ref[...] + vec_ref[7:8]

    acc_ref[...] += dot(g_ref[...], wdown_ref[...])

    @pl.when(step == pl.num_programs(0) - 1)
    def _():
        y_ref[...] = acc_ref[...].astype(BF16)


def mlp_down(g, m, wdown, vec, at, parts, after=(), chunk=1280):
    ff, width = wdown.shape
    rows = g.shape[0] // parts
    waits = len(after)
    return pl.pallas_call(
        lambda *refs: mlp_down_body(*refs[:4], *refs[4 + waits:]),
        grid=(ff // chunk,),
        in_specs=[pl.BlockSpec((rows, chunk), lambda i: (at, i)), pl.BlockSpec((rows, width), lambda i: (at, 0)),
                  pl.BlockSpec((chunk, width), lambda i: (i, 0)), whole(vec.shape)] + tied(waits),
        out_specs=whole((rows, width)),
        out_shape=jax.ShapeDtypeStruct((rows, width), BF16),
        scratch_shapes=[pltpu.VMEM((rows, width), F32)],
        compiler_params=pltpu.CompilerParams(vmem_limit_bytes=VMEM_LIMIT),
        cost_estimate=cost(6),
        name="feed_forward_down",
    )(g, m, wdown, vec, *after)


def mlp_bwd_body(grads, rows, base_ref, dz_ref, gp_ref, wup_ref, wdown_ref, *rest):
    if grads:
        c_ref, dc_ref, gup_ref, gbu_ref, du_ref, ct_ref = rest
    else:
        dc_ref, = rest
    step = pl.program_id(0)
    n, width = dz_ref.shape

    @pl.when(step == 0)
    def _():
        dc_ref[...] = jnp.zeros_like(dc_ref) if base_ref is None else base_ref[...]
        if grads:
            ct_ref[:width] = c_ref[...].T
            ct_ref[width:] = jnp.ones_like(ct_ref[width:])

    for r in range(n // rows):
        at = slice(r * rows, r * rows + rows)
        dg = dot(dz_ref[at], wdown_ref[...], ((1,), (1,)))
        du = (dg * gp_ref[at].astype(F32)).astype(BF16)
        if grads:
            du_ref[at] = du
        dc_ref[at] += dot(du, wup_ref[...], ((1,), (1,)))
    if grads:
        gup = dot(ct_ref[...], du_ref[...])
        gup_ref[...] = gup[:width].astype(BF16)
        gbu_ref[...] = gup[width:width + 8]


def mlp_bwd(dz, gp, wup, wdown, c=None, at=0, parts=1, carry=None, after=(), chunk=1280, rows=256):
    n, width = dz.shape
    ff = wup.shape[1] // parts
    first = at * ff // chunk
    grads = c is not None
    args = [dz, gp, wup, wdown]
    in_specs = [whole(dz.shape), pl.BlockSpec((n, chunk), lambda i: (0, i + first)), pl.BlockSpec((width, chunk), lambda i: (0, i + first)),
                pl.BlockSpec((chunk, width), lambda i: (i + first, 0))]
    outs = [jax.ShapeDtypeStruct((n, width), F32)]
    specs = [whole((n, width))]
    scratch = []
    if grads:
        args += [c]
        in_specs += [whole(c.shape)]
        outs += [jax.ShapeDtypeStruct((width, ff), BF16), jax.ShapeDtypeStruct((8, ff), F32)]
        specs += [pl.BlockSpec((width, chunk), lambda i: (0, i)), pl.BlockSpec((8, chunk), lambda i: (0, i))]
        scratch = [pltpu.VMEM((n, chunk), BF16), pltpu.VMEM((width + 16, n), BF16)]
    if carry is not None:
        args += [carry]
        in_specs += [whole(carry.shape)]
    used, waits = len(args), len(after)
    args += after
    in_specs += tied(waits)

    def body(*refs):
        base = refs[used - 1] if carry is not None else None
        mlp_bwd_body(grads, rows, base, *refs[:5 if grads else 4], *refs[used + waits:])

    return pl.pallas_call(
        body,
        grid=(ff // chunk,),
        in_specs=in_specs,
        out_specs=specs,
        out_shape=outs,
        scratch_shapes=scratch,
        compiler_params=pltpu.CompilerParams(vmem_limit_bytes=VMEM_LIMIT),
        cost_estimate=cost((34 if grads else 26) / parts),
        name="feed_forward_back",
    )(*args)


def down_grad_body(g_ref, dz_ref, out_ref):
    out_ref[...] = dot(g_ref[...], dz_ref[...], ((0,), (0,))).astype(BF16)


def down_grad(g, dz, chunk=1280):
    n, ff = g.shape
    width = dz.shape[1]
    return pl.pallas_call(
        down_grad_body,
        grid=(ff // chunk,),
        in_specs=[pl.BlockSpec((n, chunk), lambda i: (0, i)), whole(dz.shape)],
        out_specs=pl.BlockSpec((chunk, width), lambda i: (i, 0)),
        out_shape=jax.ShapeDtypeStruct((ff, width), BF16),
        compiler_params=pltpu.CompilerParams(vmem_limit_bytes=VMEM_LIMIT),
        cost_estimate=cost(10),
        name="down_gradient",
    )(g, dz)


def attn_bwd_body(grads, dc_ref, dz_ref, m_ref, h_ref, qkv_ref, e_ref, o_ref, inv_ref, proj_ref, vec_ref, dh_ref, *outs):
    if grads:
        dr_ref, dqkv_ref, small_ref = outs
    width = h_ref.shape[2]
    vec = vec_ref[...]

    if grads:
        @pl.when(pl.program_id(0) == 0)
        def _():
            small_ref[...] = jnp.zeros_like(small_ref)

    dz = dz_ref[0].astype(F32)
    back, g_gain1, g_shift1 = norm_back(m_ref[0], vec[1:2], dc_ref[0])
    dm = dz + back
    dr = dm.astype(BF16)
    if grads:
        dr_ref[0] = dr
    do_all = dot(dr, proj_ref[:, 3 * width:4 * width], ((1,), (1,))).astype(BF16)
    seq = h_ref.shape[1]
    head_of = lax.broadcasted_iota(jnp.int32, (1, 128), 1) // HEAD_DIM
    ones = jnp.ones((seq, 128), BF16)
    zero = jnp.zeros((seq, 128), BF16)
    dq_all, dk_all, dv_all = [], [], []
    for g in range(width // 128):
        at = slice(128 * g, 128 * g + 128)
        q = qkv_ref[0, :, 128 * g:128 * g + 128]
        k = qkv_ref[0, :, width + 128 * g:width + 128 * g + 128]
        v = jnp.concatenate([qkv_ref[0, :, 2 * width + 128 * g:2 * width + 128 * g + 128], ones], axis=1)
        scaled = do_all[:, at].astype(F32) * (inv_ref[0, :, at] * SCALE)
        do = scaled.astype(BF16)
        less = (-scaled * o_ref[0, :, at].astype(F32)).astype(BF16)
        do_t, q_t = do.T, q.T
        dq = None
        dk_t, dv_t = [], []
        for j in range(GROUP):
            mine = head_of == j
            e = e_ref[0, GROUP * g + j]
            rows = slice(HEAD_DIM * j, HEAD_DIM * j + HEAD_DIM)
            dv_t.append(dot(do_t[rows], e))
            dp = dot(jnp.concatenate([jnp.where(mine, do, zero), jnp.where(mine, less, zero)], axis=1), v, ((1,), (1,)))
            ds = (e.astype(F32) * dp).astype(BF16)
            part = dot(ds, jnp.where(mine, k, zero))
            dq = part if dq is None else dq + part
            dk_t.append(dot(q_t[rows], ds))
        dq_all.append(dq.astype(BF16))
        dk_all.append(jnp.concatenate(dk_t, axis=0).astype(BF16).T)
        dv_all.append((jnp.concatenate(dv_t, axis=0) * (1.0 / SCALE)).astype(BF16).T)
    dqkv = jnp.concatenate(dq_all + dk_all + dv_all, axis=1)
    if grads:
        dqkv_ref[0] = dqkv
    da = dot(dqkv, proj_ref[:, :3 * width], ((1,), (1,)))
    back, g_gain0, g_shift0 = norm_back(h_ref[0].astype(F32), vec[0:1], da)
    dh_ref[0] = (dm + back).astype(dh_ref.dtype)
    if not grads:
        return
    total = lambda x: jnp.sum(x.astype(F32), axis=0, keepdims=True)
    small_ref[...] += jnp.concatenate(
        [g_gain0, g_gain1, g_shift0, g_shift1, total(dqkv[:, :width]), total(dqkv[:, 2 * width:]), total(dr), total(dz)], axis=0)


def attn_bwd(dc, dz, m, h, qkv, e, o, inv, proj, vec, at, parts, grads, after=()):
    n, seq, width = h.shape
    n //= parts
    row = lambda *tail: pl.BlockSpec((1,) + tail, lambda i: (i + at * n,) + (0,) * len(tail))
    out = lambda *tail: pl.BlockSpec((1,) + tail, lambda i: (i,) + (0,) * len(tail))
    shapes = [((seq, width), F32), ((seq, width), BF16), ((seq, 3 * width), BF16)]
    specs = [out(*s) for s, _ in shapes] + [whole((8, width))]
    results = [jax.ShapeDtypeStruct((n,) + s, d) for s, d in shapes] + [jax.ShapeDtypeStruct((8, width), F32)]
    if not grads:
        specs, results = specs[:1], [jax.ShapeDtypeStruct((n, seq, width), BF16)]
    waits = len(after)
    return pl.pallas_call(
        lambda *refs: attn_bwd_body(grads, *refs[:10], *refs[10 + waits:]),
        grid=(n,),
        in_specs=[row(seq, width), row(seq, width), row(seq, width), row(seq, width), row(seq, 3 * width), row(HEADS, seq, seq), row(seq, width), row(seq, width),
                  whole(proj.shape), whole(vec.shape)] + tied(waits),
        out_specs=specs,
        out_shape=results,
        compiler_params=pltpu.CompilerParams(vmem_limit_bytes=VMEM_LIMIT),
        cost_estimate=cost(9 * n),
        name="attention_back",
    )(dc, dz, m, h, qkv, e, o, inv, proj, vec, *after)


def proj_grad_body(a_ref, dqkv_ref, o_ref, dr_ref, table_ref, out_ref, at_ref):
    step = pl.program_id(0)
    width = a_ref.shape[1]

    @pl.when(step == 0)
    def _():
        at_ref[...] = a_ref[...].T
        out_ref[:, 3 * width:4 * width] = dot(o_ref[...], dr_ref[...], ((0,), (0,))).astype(BF16)
        out_ref[:, 4 * width:] = table_ref[...].astype(BF16)

    out_ref[:, pl.ds(pl.multiple_of(step * width, 128), width)] = dot(at_ref[...], dqkv_ref[...]).astype(BF16)


def proj_grad(a, dqkv, o, dr, table, after=()):
    n, width = a.shape
    waits = len(after)
    shape = (width, 4 * width + table.shape[1])
    return pl.pallas_call(
        lambda *refs: proj_grad_body(*refs[:5], *refs[5 + waits:]),
        grid=(3,),
        in_specs=[whole(a.shape), pl.BlockSpec((n, width), lambda i: (0, i)), whole(o.shape), whole(dr.shape), whole(table.shape)] + tied(waits),
        out_specs=whole(shape),
        out_shape=jax.ShapeDtypeStruct(shape, BF16),
        scratch_shapes=[pltpu.VMEM((width, n), BF16)],
        compiler_params=pltpu.CompilerParams(vmem_limit_bytes=VMEM_LIMIT),
        cost_estimate=cost(9),
        name="projection_gradients",
    )(a, dqkv, o, dr, table, *after)


def place_body(count, to_ref, *refs):
    pieces, out_ref, sems = refs[:count], refs[count], refs[count + 1]
    copies = [pltpu.make_async_copy(piece, out_ref.at[to_ref[i]], sems.at[i]) for i, piece in enumerate(pieces)]
    for copy in copies:
        copy.start()
    for copy in copies:
        copy.wait()


def place(pieces, to, after=()):
    rows, columns = pieces[0].shape
    count, waits = len(pieces), len(after)
    out = pl.pallas_call(
        lambda *refs: place_body(count, *refs[:count + 1], *refs[count + 1 + waits:]),
        in_specs=[pl.BlockSpec(memory_space=pltpu.SMEM)] + [pl.BlockSpec(memory_space=pl.ANY)] * count + tied(waits),
        out_specs=pl.BlockSpec(memory_space=pltpu.VMEM),
        out_shape=jax.ShapeDtypeStruct((count, rows, columns), BF16),
        scratch_shapes=[pltpu.SemaphoreType.DMA((count,))],
        compiler_params=pltpu.CompilerParams(vmem_limit_bytes=VMEM_LIMIT),
        cost_estimate=cost(4),
        name="place_pieces",
    )(to, *pieces, *after)
    return out.reshape(count * rows, columns)


def places(count):
    return count // 4, 2, 2


def hop(value, kind, step=1):
    zs, ys, cores = places(lax.axis_size("dp"))
    pairs = []
    for z in range(zs):
        for y in range(ys):
            for c in range(cores):
                to = {"core": (z, y, c ^ 1), "y": (z, y ^ 1, c), "z": ((z + step) % zs, y, c)}[kind]
                pairs.append(((z * ys + y) * cores + c, (to[0] * ys + to[1]) * cores + to[2]))
    return lax.ppermute(value, "dp", pairs)


def pick(value, index, axis):
    return lax.dynamic_index_in_dim(value, index, axis, keepdims=False)


def behind_me():
    zs, ys, cores = places(lax.axis_size("dp"))
    me = lax.axis_index("dp")
    return me // (cores * ys), (me // cores) % ys, me % cores


def along_line(shard):
    return [shard] + [hop(shard, "z", step) for step in range(1, places(lax.axis_size("dp"))[0])]


def both(mine, got):
    return (mine.astype(F32) + got.astype(F32)).astype(BF16)


def core_step(grad, rows):
    zs, ys, cores = places(lax.axis_size("dp"))
    _, _, c = behind_me()
    parts = grad.reshape(zs, ys, cores, rows, grad.shape[1])
    return hop(pick(parts, 1 - c, 2), "core"), pick(parts, c, 2)


def y_step(parts):
    _, y, _ = behind_me()
    return hop(pick(parts, 1 - y, 1), "y"), pick(parts, y, 1)


def z_step(parts):
    zs, _, _ = places(lax.axis_size("dp"))
    z, _, _ = behind_me()
    return [hop(pick(parts, (z + step) % zs, 0), "z", step) for step in range(1, zs)], pick(parts, z, 0)


def z_total(got, mine):
    total = mine.astype(F32)
    for piece in got:
        total = total + piece.astype(F32)
    return total


def held(value, *after):
    return lax.optimization_barrier((value, *after))[0]


def assemble(line, other, siblings):
    zs, ys, cores = places(lax.axis_size("dp"))
    z, y, c = behind_me()
    to = []
    for core in (c, 1 - c):
        for row in (y, 1 - y):
            to += [(((z + zs - step) % zs) * ys + row) * cores + core for step in range(zs)]
    return place(line + other + siblings, jnp.stack(to).astype(jnp.int32))


def on_device(tokens, lengths, cotangent, w_qkv, w_out, w_up, w_down, norm_gain, norm_bias, bias_vec, up_bias):
    section = lax.axis_index("section")
    windows, seq, width = tokens.shape
    n = windows * seq
    shard = w_qkv.shape[1]
    per_row = up_bias.shape[1] // shard
    ff = w_up.shape[2]
    parts = 2
    part = windows // parts
    by_hand = lax.axis_size("dp") == 16
    table = jnp.concatenate([norm_gain[0], norm_bias[0], bias_vec[0]], axis=0).T
    table = jnp.concatenate([table, up_bias.reshape(shard, per_row)], axis=1)
    used = table.shape[1]
    table = jnp.pad(table, ((0, 0), (0, 128 - used)))
    packed = jnp.concatenate([w_qkv[0], w_out[0], table], axis=1)
    proj = lax.all_gather(packed, "dp", axis=0, tiled=True)
    if by_hand:
        up_line = along_line(w_up[0])
        up_other = [hop(piece, "y") for piece in up_line]
        wup = assemble(up_line, up_other, [hop(piece, "core") for piece in up_line + up_other])
        own = w_down[0]
        near = held(own, *up_line[1:])
        near = [hop(near, "z", step) for step in (1, 3)]
        far = hop(held(own, near[0]), "z", 2)
        down_line = [own, near[0], far, near[1]]
        down_other = [hop(piece, "y") for piece in down_line]
    else:
        up_line, up_other, down_line, down_other = (), (), (), ()
        wup = lax.all_gather(w_up[0], "dp", axis=0, tiled=True)
        wdown = lax.all_gather(w_down[0], "dp", axis=0, tiled=True)
    small = proj[:, 4 * width:4 * width + used]
    vec = small[:, :8].T.astype(F32)
    bup = small[:, 8:].reshape(1, ff).astype(F32)

    mid, c = attn_fwd(tokens, lengths, proj, vec, False, (*up_line, *down_other[:1]))
    act = mlp_up(c.reshape(n, width), wup, bup, (*down_line, *down_other[1::2]))
    if by_hand:
        wdown = assemble(down_line, down_other, [hop(piece, "core") for piece in down_line + down_other])
    mid = mid.reshape(n, width)
    arrived = []
    for at in range(parts):
        y = mlp_down(act, mid, wdown, vec, at, parts)
        arrived.append(lax.ppermute(y.reshape(part, seq, width), "section", [(0, 1)]))
    h = jnp.where(section == 0, tokens, jnp.concatenate(arrived))

    m, c, qkv, e, o, a, inv = attn_fwd(h, lengths, proj, vec, True)
    c = c.reshape(n, width)
    y, g, gp = mlp_fwd(c, m.reshape(n, width), wup, wdown, bup, vec, True)

    dc, = mlp_bwd(cotangent.reshape(n, width), gp, wup, wdown)
    dc = dc.reshape(tokens.shape)
    arrived = []
    for at in range(parts):
        back, = attn_bwd(dc, cotangent, m, h, qkv, e, o, inv, proj, vec, at, parts, False)
        arrived.append(lax.ppermute(back, "section", [(1, 0)]))
    dz = jnp.where(section == 1, cotangent, jnp.concatenate(arrived))

    g_down = down_grad(g, dz.reshape(n, width))
    sum_down = lax.psum_scatter(g_down, "dp", scatter_dimension=0, tiled=True).astype(F32)
    flat = dz.reshape(n, width)
    dc, g_up_a, g_bup_a = mlp_bwd(flat, gp, wup, wdown, c, 0, 2, None, (g_down,))
    got_a, mine_a = core_step(g_up_a, shard)
    dc, g_up_b, g_bup_b = mlp_bwd(flat, gp, wup, wdown, c, 1, 2, dc)
    dc = dc.reshape(tokens.shape)
    got_b, mine_b = core_step(g_up_b, shard)
    ya = y_step(both(mine_a, got_a))
    back_a = attn_bwd(dc, dz, m, h, qkv, e, o, inv, proj, vec, 0, 2, True, (got_a,))
    yb = y_step(both(mine_b, got_b))
    za = z_step(both(ya[1], ya[0]))
    back_b = attn_bwd(dc, dz, m, h, qkv, e, o, inv, proj, vec, 1, 2, True, (back_a[0], got_b, ya[0]))
    dh, dr, dqkv = [jnp.concatenate([back_a[i], back_b[i]]) for i in range(3)]
    smalls = back_a[3] + back_b[3]
    g_bup = jnp.concatenate([g_bup_a[0], g_bup_b[0]])
    g_table = jnp.concatenate([smalls.T, g_bup.reshape(width, per_row)], axis=1)
    g_table = jnp.pad(g_table, ((0, 0), (0, 128 - used)))
    zb = z_step(both(yb[1], yb[0]))
    g_proj = proj_grad(a.reshape(n, width), dqkv.reshape(n, 3 * width), o.reshape(n, width), dr.reshape(n, width), g_table, (yb[0],))
    got_p, mine_p = core_step(g_proj, shard)
    yp = y_step(both(mine_p, got_p))
    sum_up = jnp.concatenate([z_total(*za), z_total(*zb)], axis=1)
    sum_proj = z_total(*z_step(held(both(yp[1], yp[0]), *zb[0])))
    vectors = sum_proj[:, 4 * width:4 * width + 8].T
    return (
        y.reshape((1,) + tokens.shape),
        dh[None],
        sum_proj[None, :, :3 * width],
        sum_proj[None, :, 3 * width:4 * width],
        sum_up[None],
        sum_down[None],
        vectors[None, 0:2],
        vectors[None, 2:4],
        vectors[None, 4:8],
        sum_proj[:, 4 * width + 8:4 * width + used].reshape(1, -1),
    )


def solution(mesh):
    sharded = [P("section", "dp", None)] * 4 + [P("section", None, "dp")] * 3 + [P("section", "dp")]
    windows = P("dp", None, None)
    out = P("section", "dp", None, None)
    return jax.shard_map(
        on_device, mesh=mesh, in_specs=(windows, P("dp"), windows, *sharded), out_specs=(out, out, *sharded), check_vma=False
    )
```

```python
import jax
import jax.numpy as jnp
from jax import lax
from jax.experimental import pallas as pl
from jax.experimental.pallas import tpu as pltpu
from jax.sharding import PartitionSpec as P

HEADS = 20
HEAD_DIM = 32
GROUP = 128 // HEAD_DIM
SCALE = HEAD_DIM ** -0.5
LOG2E = 1.4426950408889634
VMEM_LIMIT = 56 * 1024 * 1024
F32 = jnp.float32
BF16 = jnp.bfloat16


def cost(us):
    return pl.CostEstimate(flops=int(us * 1.1e9), bytes_accessed=1024, transcendentals=0)


def tied(count):
    return [pl.BlockSpec(memory_space=pl.ANY)] * count


def dot(a, b, dims=((1,), (0,))):
    return lax.dot_general(a, b, (dims, ((), ())), preferred_element_type=F32)


def gelu_pair(u):
    below = 0.5 + 0.5 * lax.erf(u * 0.7071067811865476)
    return u * below, below + (0.3989422804014327 * u) * jnp.exp(-0.5 * (u * u))


def normed(v, gain, shift):
    centered = v - jnp.mean(v, axis=-1, keepdims=True)
    spread = jnp.mean(centered * centered, axis=-1, keepdims=True)
    hat = centered * lax.rsqrt(spread + 1e-05)
    return hat * gain + shift


def norm_back(v, gain, grad):
    centered = v - jnp.mean(v, axis=-1, keepdims=True)
    spread = jnp.mean(centered * centered, axis=-1, keepdims=True)
    inv = lax.rsqrt(spread + 1e-05)
    hat = centered * inv
    g = grad * gain
    back = inv * (g - jnp.mean(g, axis=-1, keepdims=True) - hat * jnp.mean(g * hat, axis=-1, keepdims=True))
    return back, jnp.sum(grad * hat, axis=0, keepdims=True), jnp.sum(grad, axis=0, keepdims=True)


def attn_fwd_body(save, first_window, len_ref, h_ref, wqkv_ref, vec_ref, *outs):
    if save:
        m_ref, c_ref, qkv_ref, e_ref, o_ref, a_ref, inv_ref = outs
    else:
        m_ref, c_ref = outs
    width = h_ref.shape[2]
    seq = h_ref.shape[1]
    length = len_ref[pl.program_id(0) + first_window]
    h = h_ref[0].astype(F32)
    vec = vec_ref[...]
    a = normed(h, vec[0:1], vec[2:3]).astype(BF16)
    q_all = (dot(a, wqkv_ref[:, :width]) + vec[4:5]).astype(BF16)
    k_all = dot(a, wqkv_ref[:, width:2 * width]).astype(BF16)
    v_all = (dot(a, wqkv_ref[:, 2 * width:3 * width]) + vec[5:6]).astype(BF16)
    if save:
        a_ref[0] = a
        qkv_ref[0, :, :width] = q_all
        qkv_ref[0, :, width:2 * width] = k_all
        qkv_ref[0, :, 2 * width:] = v_all
    head_of = lax.broadcasted_iota(jnp.int32, (1, 128), 1) // HEAD_DIM
    key_at = lax.broadcasted_iota(jnp.int32, (seq, 128), 0)
    lane = lax.broadcasted_iota(jnp.int32, (seq, 128), 1)
    past = jnp.where((lane == 0) & (key_at >= length), -1e30, 0.0).astype(BF16)
    first = jnp.where(lane == 0, 1.0, 0.0).astype(BF16)
    ones = jnp.ones((seq, 128), BF16)
    zero = jnp.zeros((seq, 128), BF16)
    mixed = []
    for g in range(width // 128):
        at = slice(128 * g, 128 * g + 128)
        q, v = q_all[:, at], v_all[:, at]
        k = jnp.concatenate([k_all[:, at], past], axis=1)
        acc, inv = None, None
        for j in range(GROUP):
            mine = head_of == j
            s = dot(jnp.concatenate([jnp.where(mine, q, zero), first], axis=1), k, ((1,), (1,)))
            e = jnp.exp2((s - jnp.max(s, axis=1, keepdims=True)) * (SCALE * LOG2E)).astype(BF16)
            if save:
                e_ref[0, GROUP * g + j] = e
            both_parts = dot(e, jnp.concatenate([jnp.where(mine, v, zero), ones], axis=1))
            one_over = 1.0 / both_parts[:, 128:]
            part = both_parts[:, :128] * one_over
            acc = part if acc is None else acc + part
            inv = one_over if inv is None else jnp.where(mine, one_over, inv)
        mixed.append(acc.astype(BF16))
        if save:
            inv_ref[0, :, at] = inv
    o = jnp.concatenate(mixed, axis=1)
    if save:
        o_ref[0] = o
    m = h + dot(o, wqkv_ref[:, 3 * width:4 * width]) + vec[6:7]
    m_ref[0] = m
    c_ref[0] = normed(m, vec[1:2], vec[3:4]).astype(BF16)


def whole(shape):
    return pl.BlockSpec(shape, lambda *_: (0,) * len(shape))


def attn_fwd(h, lengths, proj, vec, save, at=0, parts=1, earlier=(), after=()):
    count, seq, width = h.shape
    n = count * parts
    row = lambda *tail: pl.BlockSpec((1,) + tail, lambda i, *_: (i + at * count,) + (0,) * len(tail))
    shapes = [((seq, width), F32), ((seq, width), BF16)]
    if save:
        shapes += [((seq, 3 * width), BF16), ((HEADS, seq, seq), BF16), ((seq, width), BF16), ((seq, width), BF16), ((seq, width), F32)]
    waits = len(earlier) + len(after)
    return pl.pallas_call(
        lambda *refs: attn_fwd_body(save, at * count, *refs[:4], *refs[4 + waits:]),
        grid_spec=pltpu.PrefetchScalarGridSpec(
            num_scalar_prefetch=1,
            grid=(count,),
            in_specs=[pl.BlockSpec((1, seq, width), lambda i, *_: (i, 0, 0)), whole(proj.shape), whole(vec.shape)] + tied(waits),
            out_specs=[row(*s) for s, _ in shapes],
        ),
        out_shape=[jax.ShapeDtypeStruct((n,) + s, d) for s, d in shapes],
        input_output_aliases={4 + i: i for i in range(len(earlier))},
        compiler_params=pltpu.CompilerParams(vmem_limit_bytes=VMEM_LIMIT),
        cost_estimate=cost(4.5 * count),
        name="attention_forward",
    )(lengths, h, proj, vec, *earlier, *after)


def mlp_fwd_body(save, rows, c_ref, m_ref, wup_ref, wdown_ref, bup_ref, vec_ref, *outs):
    if save:
        y_ref, g_ref, gp_ref, acc_ref = outs
    else:
        y_ref, acc_ref = outs
    step = pl.program_id(0)

    @pl.when(step == 0)
    def _():
        acc_ref[...] = m_ref[...] + vec_ref[7:8]

    for r in range(c_ref.shape[0] // rows):
        at = slice(r * rows, r * rows + rows)
        u = dot(c_ref[at], wup_ref[...]) + bup_ref[...]
        act, slope = gelu_pair(u)
        act = act.astype(BF16)
        if save:
            g_ref[at] = act
            gp_ref[at] = slope.astype(BF16)
        acc_ref[at] += dot(act, wdown_ref[...])

    @pl.when(step == pl.num_programs(0) - 1)
    def _():
        y_ref[...] = acc_ref[...].astype(BF16)


def mlp_fwd(c, m, wup, wdown, bup, vec, save, chunk=1280, rows=256):
    n, width = c.shape
    ff = wup.shape[1]
    outs = [jax.ShapeDtypeStruct((n, width), BF16)]
    specs = [whole((n, width))]
    if save:
        outs += [jax.ShapeDtypeStruct((n, ff), BF16)] * 2
        specs += [pl.BlockSpec((n, chunk), lambda i: (0, i))] * 2
    return pl.pallas_call(
        lambda *refs: mlp_fwd_body(save, rows, *refs),
        grid=(ff // chunk,),
        in_specs=[whole(c.shape), whole(m.shape), pl.BlockSpec((width, chunk), lambda i: (0, i)),
                  pl.BlockSpec((chunk, width), lambda i: (i, 0)), pl.BlockSpec((1, chunk), lambda i: (0, i)), whole(vec.shape)],
        out_specs=specs,
        out_shape=outs,
        scratch_shapes=[pltpu.VMEM((n, width), F32)],
        compiler_params=pltpu.CompilerParams(vmem_limit_bytes=VMEM_LIMIT),
        cost_estimate=cost(26),
        name="feed_forward",
    )(c, m, wup, wdown, bup, vec)


def mlp_up_body(rows, c_ref, wup_ref, bup_ref, g_ref):
    for r in range(c_ref.shape[0] // rows):
        at = slice(r * rows, r * rows + rows)
        g_ref[at] = gelu_pair(dot(c_ref[at], wup_ref[...]) + bup_ref[...])[0].astype(BF16)


def mlp_up(c, wup, bup, after=(), chunk=1280, rows=256):
    n, width = c.shape
    ff = wup.shape[1]
    waits = len(after)
    return pl.pallas_call(
        lambda *refs: mlp_up_body(rows, *refs[:3], *refs[3 + waits:]),
        grid=(ff // chunk,),
        in_specs=[whole(c.shape), pl.BlockSpec((width, chunk), lambda i: (0, i)), pl.BlockSpec((1, chunk), lambda i: (0, i))] + tied(waits),
        out_specs=pl.BlockSpec((n, chunk), lambda i: (0, i)),
        out_shape=jax.ShapeDtypeStruct((n, ff), BF16),
        compiler_params=pltpu.CompilerParams(vmem_limit_bytes=VMEM_LIMIT),
        cost_estimate=cost(0.0125 * n),
        name="feed_forward_up",
    )(c, wup, bup, *after)


def mlp_down_body(g_ref, m_ref, wdown_ref, vec_ref, y_ref, acc_ref):
    step = pl.program_id(0)

    @pl.when(step == 0)
    def _():
        acc_ref[...] = m_ref[...] + vec_ref[7:8]

    acc_ref[...] += dot(g_ref[...], wdown_ref[...])

    @pl.when(step == pl.num_programs(0) - 1)
    def _():
        y_ref[...] = acc_ref[...].astype(BF16)


def mlp_down(g, m, wdown, vec, at, parts, after=(), chunk=1280):
    ff, width = wdown.shape
    rows = g.shape[0] // parts
    waits = len(after)
    return pl.pallas_call(
        lambda *refs: mlp_down_body(*refs[:4], *refs[4 + waits:]),
        grid=(ff // chunk,),
        in_specs=[pl.BlockSpec((rows, chunk), lambda i: (at, i)), pl.BlockSpec((rows, width), lambda i: (at, 0)),
                  pl.BlockSpec((chunk, width), lambda i: (i, 0)), whole(vec.shape)] + tied(waits),
        out_specs=whole((rows, width)),
        out_shape=jax.ShapeDtypeStruct((rows, width), BF16),
        scratch_shapes=[pltpu.VMEM((rows, width), F32)],
        compiler_params=pltpu.CompilerParams(vmem_limit_bytes=VMEM_LIMIT),
        cost_estimate=cost(0.017 * rows),
        name="feed_forward_down",
    )(g, m, wdown, vec, *after)


def mlp_bwd_body(save, rows, dz_ref, gp_ref, wup_ref, wdown_ref, dc_ref, *outs):
    @pl.when(pl.program_id(0) == 0)
    def _():
        dc_ref[...] = jnp.zeros_like(dc_ref)

    for r in range(dz_ref.shape[0] // rows):
        at = slice(r * rows, r * rows + rows)
        dg = dot(dz_ref[at], wdown_ref[...], ((1,), (1,)))
        du = (dg * gp_ref[at].astype(F32)).astype(BF16)
        if save:
            outs[0][at] = du
        dc_ref[at] += dot(du, wup_ref[...], ((1,), (1,)))


def mlp_bwd(dz, gp, wup, wdown, save, at=0, parts=1, earlier=(), after=(), chunk=1280, rows=256):
    n, width = dz.shape
    ff = wup.shape[1]
    args = [dz, gp, wup, wdown, *earlier, *after]
    outs = [jax.ShapeDtypeStruct((n * parts, width), F32)]
    specs = [pl.BlockSpec((n, width), lambda i: (at, 0))]
    if save:
        outs += [jax.ShapeDtypeStruct((n * parts, ff), BF16)]
        specs += [pl.BlockSpec((n, chunk), lambda i: (at, i))]
    return pl.pallas_call(
        lambda *refs: mlp_bwd_body(save, rows, *refs[:4], *refs[len(args):]),
        grid=(ff // chunk,),
        in_specs=[whole(dz.shape), pl.BlockSpec((n, chunk), lambda i: (at, i)), pl.BlockSpec((width, chunk), lambda i: (0, i)),
                  pl.BlockSpec((chunk, width), lambda i: (i, 0))] + tied(len(args) - 4),
        out_specs=specs,
        out_shape=outs,
        input_output_aliases={4 + i: i for i in range(len(earlier))},
        compiler_params=pltpu.CompilerParams(vmem_limit_bytes=VMEM_LIMIT),
        cost_estimate=cost(22 / parts),
        name="feed_forward_back",
    )(*args)


def up_grad_body(c_ref, order_ref, du_ref, keep_ref, send_ref, sum_ref, ct_ref):
    half = keep_ref.shape[0]

    @pl.when(pl.program_id(0) == 0)
    def _():
        ct_ref[:2 * half] = dot(order_ref[...], c_ref[...], ((1,), (1,))).astype(BF16)
        ct_ref[2 * half:] = jnp.ones_like(ct_ref[2 * half:])

    grad = dot(ct_ref[...], du_ref[...])
    keep_ref[...] = grad[:half].astype(BF16)
    send_ref[...] = grad[half:2 * half].astype(BF16)
    sum_ref[...] = grad[2 * half:2 * half + 8]


def up_grad(c, order, du, at, parts, after=(), chunk=1280):
    n, width = c.shape
    ff = du.shape[1] // parts
    first = at * ff // chunk
    waits = len(after)
    column = lambda rows: pl.BlockSpec((rows, chunk), lambda i: (0, i))
    return pl.pallas_call(
        lambda *refs: up_grad_body(*refs[:3], *refs[3 + waits:]),
        grid=(ff // chunk,),
        in_specs=[whole(c.shape), whole(order.shape), pl.BlockSpec((n, chunk), lambda i: (0, i + first))] + tied(waits),
        out_specs=[column(width // 2), column(width // 2), column(8)],
        out_shape=[jax.ShapeDtypeStruct((width // 2, ff), BF16)] * 2 + [jax.ShapeDtypeStruct((8, ff), F32)],
        scratch_shapes=[pltpu.VMEM((width + 16, n), BF16)],
        compiler_params=pltpu.CompilerParams(vmem_limit_bytes=VMEM_LIMIT),
        cost_estimate=cost(13 / parts),
        name="up_gradient",
    )(c, order, du, *after)


def down_grad_body(g_ref, dz_ref, out_ref):
    out_ref[...] = dot(g_ref[...], dz_ref[...], ((0,), (0,))).astype(BF16)


def down_grad(g, dz, after=(), chunk=1280):
    n, ff = g.shape
    width = dz.shape[1]
    waits = len(after)
    return pl.pallas_call(
        lambda *refs: down_grad_body(*refs[:2], *refs[2 + waits:]),
        grid=(ff // chunk,),
        in_specs=[pl.BlockSpec((n, chunk), lambda i: (0, i)), whole(dz.shape)] + tied(waits),
        out_specs=pl.BlockSpec((chunk, width), lambda i: (i, 0)),
        out_shape=jax.ShapeDtypeStruct((ff, width), BF16),
        compiler_params=pltpu.CompilerParams(vmem_limit_bytes=VMEM_LIMIT),
        cost_estimate=cost(12),
        name="down_gradient",
    )(g, dz, *after)


def attn_bwd_body(grads, base_ref, dc_ref, dz_ref, m_ref, h_ref, qkv_ref, e_ref, o_ref, inv_ref, proj_ref, vec_ref, dh_ref, *outs):
    if grads:
        dr_ref, dqkv_ref, small_ref = outs
    width = h_ref.shape[2]
    vec = vec_ref[...]

    if grads:
        @pl.when(pl.program_id(0) == 0)
        def _():
            small_ref[...] = jnp.zeros_like(small_ref) if base_ref is None else base_ref[...]

    dz = dz_ref[0].astype(F32)
    back, g_gain1, g_shift1 = norm_back(m_ref[0], vec[1:2], dc_ref[0])
    dm = dz + back
    dr = dm.astype(BF16)
    if grads:
        dr_ref[0] = dr
    do_all = dot(dr, proj_ref[:, 3 * width:4 * width], ((1,), (1,))).astype(BF16)
    seq = h_ref.shape[1]
    head_of = lax.broadcasted_iota(jnp.int32, (1, 128), 1) // HEAD_DIM
    ones = jnp.ones((seq, 128), BF16)
    zero = jnp.zeros((seq, 128), BF16)
    dq_all, dk_all, dv_all = [], [], []
    for g in range(width // 128):
        at = slice(128 * g, 128 * g + 128)
        q = qkv_ref[0, :, 128 * g:128 * g + 128]
        k = qkv_ref[0, :, width + 128 * g:width + 128 * g + 128]
        v = jnp.concatenate([qkv_ref[0, :, 2 * width + 128 * g:2 * width + 128 * g + 128], ones], axis=1)
        scaled = do_all[:, at].astype(F32) * (inv_ref[0, :, at] * SCALE)
        do = scaled.astype(BF16)
        less = (-scaled * o_ref[0, :, at].astype(F32)).astype(BF16)
        do_t, q_t = do.T, q.T
        dq = None
        dk_t, dv_t = [], []
        for j in range(GROUP):
            mine = head_of == j
            e = e_ref[0, GROUP * g + j]
            rows = slice(HEAD_DIM * j, HEAD_DIM * j + HEAD_DIM)
            dv_t.append(dot(do_t[rows], e))
            dp = dot(jnp.concatenate([jnp.where(mine, do, zero), jnp.where(mine, less, zero)], axis=1), v, ((1,), (1,)))
            ds = (e.astype(F32) * dp).astype(BF16)
            part = dot(ds, jnp.where(mine, k, zero))
            dq = part if dq is None else dq + part
            dk_t.append(dot(q_t[rows], ds))
        dq_all.append(dq.astype(BF16))
        dk_all.append(jnp.concatenate(dk_t, axis=0).astype(BF16).T)
        dv_all.append((jnp.concatenate(dv_t, axis=0) * (1.0 / SCALE)).astype(BF16).T)
    dqkv = jnp.concatenate(dq_all + dk_all + dv_all, axis=1)
    if grads:
        dqkv_ref[0] = dqkv
    da = dot(dqkv, proj_ref[:, :3 * width], ((1,), (1,)))
    back, g_gain0, g_shift0 = norm_back(h_ref[0].astype(F32), vec[0:1], da)
    dh_ref[0] = (dm + back).astype(dh_ref.dtype)
    if not grads:
        return
    total = lambda x: jnp.sum(x.astype(F32), axis=0, keepdims=True)
    small_ref[...] += jnp.concatenate(
        [g_gain0, g_gain1, g_shift0, g_shift1, total(dqkv[:, :width]), total(dqkv[:, 2 * width:]), total(dr), total(dz)], axis=0)


def attn_bwd(dc, dz, m, h, qkv, e, o, inv, proj, vec, at, parts, grads, earlier=(), after=()):
    n, seq, width = h.shape
    count = n // parts
    row = lambda *tail: pl.BlockSpec((1,) + tail, lambda i: (i + at * count,) + (0,) * len(tail))
    if grads:
        shapes = [((seq, width), F32), ((seq, width), BF16), ((seq, 3 * width), BF16)]
        specs = [row(*s) for s, _ in shapes] + [whole((8, width))]
        results = [jax.ShapeDtypeStruct((n,) + s, d) for s, d in shapes] + [jax.ShapeDtypeStruct((8, width), F32)]
    else:
        specs = [pl.BlockSpec((1, seq, width), lambda i: (i, 0, 0))]
        results = [jax.ShapeDtypeStruct((count, seq, width), BF16)]
    args = [dc, dz, m, h, qkv, e, o, inv, proj, vec]
    in_specs = [row(seq, width), row(seq, width), row(seq, width), row(seq, width), row(seq, 3 * width), row(HEADS, seq, seq),
                row(seq, width), row(seq, width), whole(proj.shape), whole(vec.shape)]
    base = len(args)
    if earlier:
        args += [earlier[3], *earlier[:3]]
        in_specs += [whole(earlier[3].shape)] + tied(3)
    aliases = {base + 1 + i: i for i in range(3)} if earlier else {}
    args += after
    in_specs += tied(len(after))
    used = len(args)

    def body(*refs):
        attn_bwd_body(grads, refs[base] if earlier else None, *refs[:base], *refs[used:])

    return pl.pallas_call(
        body,
        grid=(count,),
        in_specs=in_specs,
        out_specs=specs,
        out_shape=results,
        input_output_aliases=aliases,
        compiler_params=pltpu.CompilerParams(vmem_limit_bytes=VMEM_LIMIT),
        cost_estimate=cost(7 * count),
        name="attention_back",
    )(*args)


def proj_grad_body(a_ref, dqkv_ref, o_ref, dr_ref, table_ref, order_ref, keep_ref, send_ref, at_ref):
    step = pl.program_id(0)
    width = a_ref.shape[1]
    half = width // 2
    order = order_ref[...]

    def put(at, value):
        keep_ref[:, at] = value[:half].astype(BF16)
        send_ref[:, at] = value[half:].astype(BF16)

    @pl.when(step == 0)
    def _():
        at_ref[...] = dot(order, a_ref[...], ((1,), (1,))).astype(BF16)
        put(slice(3 * width, 4 * width), dot(dot(order, o_ref[...], ((1,), (1,))).astype(BF16), dr_ref[...]))
        put(slice(4 * width, None), dot(order, table_ref[...].astype(BF16)))

    put(pl.ds(pl.multiple_of(step * width, 128), width), dot(at_ref[...], dqkv_ref[...]))


def proj_grad(a, dqkv, o, dr, table, order, after=()):
    n, width = a.shape
    waits = len(after)
    shape = (width // 2, 4 * width + table.shape[1])
    return pl.pallas_call(
        lambda *refs: proj_grad_body(*refs[:6], *refs[6 + waits:]),
        grid=(3,),
        in_specs=[whole(a.shape), pl.BlockSpec((n, width), lambda i: (0, i)), whole(o.shape), whole(dr.shape), whole(table.shape),
                  whole(order.shape)] + tied(waits),
        out_specs=[whole(shape)] * 2,
        out_shape=[jax.ShapeDtypeStruct(shape, BF16)] * 2,
        scratch_shapes=[pltpu.VMEM((width, n), BF16)],
        compiler_params=pltpu.CompilerParams(vmem_limit_bytes=VMEM_LIMIT),
        cost_estimate=cost(9),
        name="projection_gradients",
    )(a, dqkv, o, dr, table, order, *after)


def place_body(count, to_ref, *refs):
    pieces, out_ref, sems = refs[:count], refs[count], refs[count + 1]
    copies = [pltpu.make_async_copy(piece, out_ref.at[to_ref[i]], sems.at[i]) for i, piece in enumerate(pieces)]
    for copy in copies:
        copy.start()
    for copy in copies:
        copy.wait()


def place(pieces, to, after=()):
    rows, columns = pieces[0].shape
    count, waits = len(pieces), len(after)
    out = pl.pallas_call(
        lambda *refs: place_body(count, *refs[:count + 1], *refs[count + 1 + waits:]),
        in_specs=[pl.BlockSpec(memory_space=pltpu.SMEM)] + [pl.BlockSpec(memory_space=pl.ANY)] * count + tied(waits),
        out_specs=pl.BlockSpec(memory_space=pltpu.VMEM),
        out_shape=jax.ShapeDtypeStruct((count, rows, columns), BF16),
        scratch_shapes=[pltpu.SemaphoreType.DMA((count,))],
        compiler_params=pltpu.CompilerParams(vmem_limit_bytes=VMEM_LIMIT),
        cost_estimate=cost(4),
        name="place_pieces",
    )(to, *pieces, *after)
    return out.reshape(count * rows, columns)


def places(count):
    return count // 4, 2, 2


def hop(value, kind, step=1):
    zs, ys, cores = places(lax.axis_size("dp"))
    pairs = []
    for z in range(zs):
        for y in range(ys):
            for c in range(cores):
                to = {"core": (z, y, c ^ 1), "y": (z, y ^ 1, c), "z": ((z + step) % zs, y, c)}[kind]
                pairs.append(((z * ys + y) * cores + c, (to[0] * ys + to[1]) * cores + to[2]))
    return lax.ppermute(value, "dp", pairs)


def behind_me():
    zs, ys, cores = places(lax.axis_size("dp"))
    me = lax.axis_index("dp")
    return me // (cores * ys), (me // cores) % ys, me % cores


def along_line(shard):
    return [shard] + [hop(shard, "z", step) for step in range(1, places(lax.axis_size("dp"))[0])]


def both(mine, got):
    return (mine.astype(F32) + got.astype(F32)).astype(BF16)


def scatter_order(shard):
    zs, ys, cores = places(lax.axis_size("dp"))
    z, y, c = behind_me()
    row = jnp.arange(zs * ys * cores * shard)
    block = row // shard
    to = (((z + block % zs) % zs) * ys + (y ^ (block // zs % ys))) * cores + (c ^ (block // (zs * ys)))
    return (jnp.arange(zs * ys * cores * shard)[None, :] == (to * shard + row % shard)[:, None]).astype(BF16)


def y_step(mine, got):
    half = mine.shape[0] // 2
    return both(mine[:half], got[:half]), hop(both(mine[half:], got[half:]), "y")


def z_step(mine, got):
    zs, _, _ = places(lax.axis_size("dp"))
    rows = mine.shape[0] // zs
    at = lambda v, k: v[k * rows:k * rows + rows]
    return [at(mine, 0), at(got, 0)] + [hop(both(at(mine, k), at(got, k)), "z", k) for k in range(1, zs)]


def total(terms):
    out = terms[0].astype(F32)
    for term in terms[1:]:
        out = out + term.astype(F32)
    return out


def held(value, *after):
    return lax.optimization_barrier((value, *after))[0]


def assemble(line, other, siblings, after=()):
    zs, ys, cores = places(lax.axis_size("dp"))
    z, y, c = behind_me()
    to = []
    for core in (c, 1 - c):
        for row in (y, 1 - y):
            to += [(((z + zs - step) % zs) * ys + row) * cores + core for step in range(zs)]
    return place(line + other + siblings, jnp.stack(to).astype(jnp.int32), after)


def on_device(tokens, lengths, cotangent, w_qkv, w_out, w_up, w_down, norm_gain, norm_bias, bias_vec, up_bias):
    section = lax.axis_index("section")
    windows, seq, width = tokens.shape
    n = windows * seq
    shard = w_qkv.shape[1]
    per_row = up_bias.shape[1] // shard
    ff = w_up.shape[2]
    parts = 2
    part = windows // parts
    by_hand = lax.axis_size("dp") == 16
    table = jnp.concatenate([norm_gain[0], norm_bias[0], bias_vec[0]], axis=0).T
    table = jnp.concatenate([table, up_bias.reshape(shard, per_row)], axis=1)
    used = table.shape[1]
    table = jnp.pad(table, ((0, 0), (0, 128 - used)))
    packed = jnp.concatenate([w_qkv[0], w_out[0], table], axis=1)
    if by_hand:
        up, down = w_up[0], w_down[0]
        order = scatter_order(shard)
        proj_1, proj_3, proj_2 = hop(packed, "z", 1), hop(packed, "z", 3), hop(packed, "z", 2)
        proj_y0, up_y0 = hop(packed, "y"), hop(up, "y")
        now = (proj_1, proj_2, proj_3, proj_y0)
        up_1, up_3 = hop(held(up, *now), "z", 1), hop(held(up, *now), "z", 3)
        proj_y = [hop(held(piece, *now), "y") for piece in (proj_1, proj_2, proj_3)]
        now = (up_1, up_3, up_y0, *proj_y)
        up_2 = hop(held(up, *now), "z", 2)
        up_y1, up_y3 = hop(held(up_1, *now), "y"), hop(held(up_3, *now), "y")
        line, other = [packed, proj_1, proj_2, proj_3], [proj_y0, *proj_y]
        proj = assemble(line, other, [hop(held(piece, *now), "core") for piece in line + other])
        now = (up_2, up_y1, up_y3)
        down_1, down_3 = hop(held(down, *now), "z", 1), hop(held(down, *now), "z", 3)
        up_y2, down_y0 = hop(held(up_2, *now), "y"), hop(held(down, *now), "y")
    else:
        order = (jnp.arange(width)[None, :] == jnp.arange(width)[:, None]).astype(BF16)
        proj = lax.all_gather(packed, "dp", axis=0, tiled=True)
        wup = lax.all_gather(w_up[0], "dp", axis=0, tiled=True)
        wdown = lax.all_gather(w_down[0], "dp", axis=0, tiled=True)
    small = proj[:, 4 * width:4 * width + used]
    vec = small[:, :8].T.astype(F32)
    bup = small[:, 8:].reshape(1, ff).astype(F32)

    mid, c = attn_fwd(tokens, lengths, proj, vec, False)
    c = c.reshape(n, width)
    if by_hand:
        now = (down_1, down_3, up_y2, down_y0, c)
        down_2 = hop(held(down, *now), "z", 2)
        down_y1, down_y3 = hop(held(down_1, *now), "y"), hop(held(down_3, *now), "y")
        line, other = [up, up_1, up_2, up_3], [up_y0, up_y1, up_y2, up_y3]
        wup = assemble(line, other, [hop(held(piece, *now), "core") for piece in line + other])
    act = mlp_up(c, wup, bup)
    if by_hand:
        now = (down_2, down_y1, down_y3, act)
        down_y2 = hop(held(down_2, *now), "y")
    if by_hand:
        line, other = [down, down_1, down_2, down_3], [down_y0, down_y1, down_y2, down_y3]
        wdown = assemble(line, other, [hop(piece, "core") for piece in line + other])
    mid = mid.reshape(n, width)
    kept = ()
    arrived = []
    for at in range(parts):
        y = mlp_down(act, mid, wdown, vec, at, parts)
        arrived.append(lax.ppermute(y.reshape(part, seq, width), "section", [(0, 1)]))
    h = []
    for at in range(parts):
        h.append(jnp.where(section == 0, tokens[at * part:at * part + part], held(arrived[at], *kept[:1])))
        kept = attn_fwd(h[at], lengths, proj, vec, True, at, parts, kept)
    h = jnp.concatenate(h)
    m, c, qkv, e, o, a, inv = kept
    c = c.reshape(n, width)
    y, g, gp = mlp_fwd(c, m.reshape(n, width), wup, wdown, bup, vec, True)

    dc, = mlp_bwd(cotangent.reshape(n, width), gp, wup, wdown, False)
    dc = dc.reshape(tokens.shape)
    arrived = []
    for at in range(parts):
        back, = attn_bwd(dc, cotangent, m, h, qkv, e, o, inv, proj, vec, at, parts, False)
        arrived.append(lax.ppermute(back, "section", [(1, 0)]))
    dz, more = [], ()
    for at in range(parts):
        dz.append(jnp.where(section == 1, cotangent[at * part:at * part + part], held(arrived[at], *more[:1])))
        more = mlp_bwd(dz[at].reshape(part * seq, width), gp, wup, wdown, True, at, parts, more)
    dz = jnp.concatenate(dz)
    dc, du = more
    dc = dc.reshape(tokens.shape)
    g_down = down_grad(g, dz.reshape(n, width))
    sum_down = lax.psum_scatter(g_down, "dp", scatter_dimension=0, tiled=True).astype(F32)
    keep_u, send_u, bup_u = up_grad(c, order, du, 0, 1, (g_down,))
    if by_hand:
        got_u = hop(send_u, "core")
        half = ff // 2
        mine_a, got_a = y_step(keep_u[:, :half], got_u[:, :half])
        mine_b, got_b = y_step(keep_u[:, half:], held(got_u[:, half:], got_a))
        back = attn_bwd(dc, dz, m, h, qkv, e, o, inv, proj, vec, 0, 2, True, (), (got_u,))
        terms_a = z_step(mine_a, got_a)
        back = attn_bwd(dc, dz, m, h, qkv, e, o, inv, proj, vec, 1, 2, True, back, (got_a,))
        terms_b = z_step(mine_b, got_b)
        wait = (got_b, *terms_a[2:])
    else:
        back = attn_bwd(dc, dz, m, h, qkv, e, o, inv, proj, vec, 0, 1, True)
        wait = ()
    dh, dr, dqkv, smalls = back
    g_bup = bup_u[0].reshape(width, per_row)
    g_table = jnp.concatenate([smalls.T, g_bup], axis=1)
    g_table = jnp.pad(g_table, ((0, 0), (0, 128 - used)))
    keep_p, send_p = proj_grad(
        a.reshape(n, width), dqkv.reshape(n, 3 * width), o.reshape(n, width), dr.reshape(n, width), g_table, order, wait)
    if by_hand:
        sum_up = jnp.concatenate([total(terms_a), total(terms_b)], axis=1)
        mine_p, got_p = y_step(keep_p, hop(send_p, "core"))
        sum_proj = total(z_step(mine_p, held(got_p, *terms_b)))
    else:
        scatter = lambda *halves: lax.psum_scatter(jnp.concatenate(halves), "dp", scatter_dimension=0, tiled=True).astype(F32)
        sum_up = scatter(keep_u, send_u)
        sum_proj = scatter(keep_p, send_p)
    vectors = sum_proj[:, 4 * width:4 * width + 8].T
    return (
        y.reshape((1,) + tokens.shape),
        dh[None],
        sum_proj[None, :, :3 * width],
        sum_proj[None, :, 3 * width:4 * width],
        sum_up[None],
        sum_down[None],
        vectors[None, 0:2],
        vectors[None, 2:4],
        vectors[None, 4:8],
        sum_proj[:, 4 * width + 8:4 * width + used].reshape(1, -1),
    )


def solution(mesh):
    sharded = [P("section", "dp", None)] * 4 + [P("section", None, "dp")] * 3 + [P("section", "dp")]
    windows = P("dp", None, None)
    out = P("section", "dp", None, None)
    return jax.shard_map(
        on_device, mesh=mesh, in_specs=(windows, P("dp"), windows, *sharded), out_specs=(out, out, *sharded), check_vma=False
    )
```

```python
import jax
import jax.numpy as jnp
from jax import lax
from jax.experimental import pallas as pl
from jax.experimental.pallas import tpu as pltpu
from jax.sharding import PartitionSpec as P

HEADS = 20
HEAD_DIM = 32
GROUP = 128 // HEAD_DIM
SCALE = HEAD_DIM ** -0.5
LOG2E = 1.4426950408889634
VMEM_LIMIT = 56 * 1024 * 1024
F32 = jnp.float32
BF16 = jnp.bfloat16


def cost(us):
    return pl.CostEstimate(flops=int(us * 1.1e9), bytes_accessed=1024, transcendentals=0)


def tied(count):
    return [pl.BlockSpec(memory_space=pl.ANY)] * count


def dot(a, b, dims=((1,), (0,))):
    return lax.dot_general(a, b, (dims, ((), ())), preferred_element_type=F32)


def gelu_pair(u):
    below = 0.5 + 0.5 * lax.erf(u * 0.7071067811865476)
    return u * below, below + (0.3989422804014327 * u) * jnp.exp(-0.5 * (u * u))


def normed(v, gain, shift):
    centered = v - jnp.mean(v, axis=-1, keepdims=True)
    spread = jnp.mean(centered * centered, axis=-1, keepdims=True)
    hat = centered * lax.rsqrt(spread + 1e-05)
    return hat * gain + shift


def norm_back(v, gain, grad):
    centered = v - jnp.mean(v, axis=-1, keepdims=True)
    spread = jnp.mean(centered * centered, axis=-1, keepdims=True)
    inv = lax.rsqrt(spread + 1e-05)
    hat = centered * inv
    g = grad * gain
    back = inv * (g - jnp.mean(g, axis=-1, keepdims=True) - hat * jnp.mean(g * hat, axis=-1, keepdims=True))
    return back, jnp.sum(grad * hat, axis=0, keepdims=True), jnp.sum(grad, axis=0, keepdims=True)


def attn_fwd_body(save, first_window, len_ref, h_ref, wqkv_ref, vec_ref, *outs):
    if save:
        m_ref, c_ref, qkv_ref, e_ref, o_ref, a_ref, inv_ref = outs
    else:
        m_ref, c_ref = outs
    width = h_ref.shape[2]
    seq = h_ref.shape[1]
    length = len_ref[pl.program_id(0) + first_window]
    h = h_ref[0].astype(F32)
    vec = vec_ref[...]
    a = normed(h, vec[0:1], vec[2:3]).astype(BF16)
    q_all = (dot(a, wqkv_ref[:, :width]) + vec[4:5]).astype(BF16)
    k_all = dot(a, wqkv_ref[:, width:2 * width]).astype(BF16)
    v_all = (dot(a, wqkv_ref[:, 2 * width:3 * width]) + vec[5:6]).astype(BF16)
    if save:
        a_ref[0] = a
        qkv_ref[0, :, :width] = q_all
        qkv_ref[0, :, width:2 * width] = k_all
        qkv_ref[0, :, 2 * width:] = v_all
    head_of = lax.broadcasted_iota(jnp.int32, (1, 128), 1) // HEAD_DIM
    key_at = lax.broadcasted_iota(jnp.int32, (seq, 128), 0)
    lane = lax.broadcasted_iota(jnp.int32, (seq, 128), 1)
    past = jnp.where((lane == 0) & (key_at >= length), -1e30, 0.0).astype(BF16)
    first = jnp.where(lane == 0, 1.0, 0.0).astype(BF16)
    ones = jnp.ones((seq, 128), BF16)
    zero = jnp.zeros((seq, 128), BF16)
    mixed = []
    for g in range(width // 128):
        at = slice(128 * g, 128 * g + 128)
        q, v = q_all[:, at], v_all[:, at]
        k = jnp.concatenate([k_all[:, at], past], axis=1)
        acc, inv = None, None
        for j in range(GROUP):
            mine = head_of == j
            s = dot(jnp.concatenate([jnp.where(mine, q, zero), first], axis=1), k, ((1,), (1,)))
            e = jnp.exp2((s - jnp.max(s, axis=1, keepdims=True)) * (SCALE * LOG2E)).astype(BF16)
            if save:
                e_ref[0, GROUP * g + j] = e
            both_parts = dot(e, jnp.concatenate([jnp.where(mine, v, zero), ones], axis=1))
            one_over = 1.0 / both_parts[:, 128:]
            part = both_parts[:, :128] * one_over
            acc = part if acc is None else acc + part
            inv = one_over if inv is None else jnp.where(mine, one_over, inv)
        mixed.append(acc.astype(BF16))
        if save:
            inv_ref[0, :, at] = inv
    o = jnp.concatenate(mixed, axis=1)
    if save:
        o_ref[0] = o
    m = h + dot(o, wqkv_ref[:, 3 * width:4 * width]) + vec[6:7]
    m_ref[0] = m
    c_ref[0] = normed(m, vec[1:2], vec[3:4]).astype(BF16)


def whole(shape):
    return pl.BlockSpec(shape, lambda *_: (0,) * len(shape))


def attn_fwd(h, lengths, proj, vec, save, at=0, parts=1, earlier=(), after=()):
    count, seq, width = h.shape
    n = count * parts
    row = lambda *tail: pl.BlockSpec((1,) + tail, lambda i, *_: (i + at * count,) + (0,) * len(tail))
    shapes = [((seq, width), F32), ((seq, width), BF16)]
    if save:
        shapes += [((seq, 3 * width), BF16), ((HEADS, seq, seq), BF16), ((seq, width), BF16), ((seq, width), BF16), ((seq, width), F32)]
    waits = len(earlier) + len(after)
    return pl.pallas_call(
        lambda *refs: attn_fwd_body(save, at * count, *refs[:4], *refs[4 + waits:]),
        grid_spec=pltpu.PrefetchScalarGridSpec(
            num_scalar_prefetch=1,
            grid=(count,),
            in_specs=[pl.BlockSpec((1, seq, width), lambda i, *_: (i, 0, 0)), whole(proj.shape), whole(vec.shape)] + tied(waits),
            out_specs=[row(*s) for s, _ in shapes],
        ),
        out_shape=[jax.ShapeDtypeStruct((n,) + s, d) for s, d in shapes],
        input_output_aliases={4 + i: i for i in range(len(earlier))},
        compiler_params=pltpu.CompilerParams(vmem_limit_bytes=VMEM_LIMIT),
        cost_estimate=cost(4.5 * count),
        name="attention_forward",
    )(lengths, h, proj, vec, *earlier, *after)


def mlp_fwd_body(save, rows, c_ref, m_ref, wup_ref, wdown_ref, bup_ref, vec_ref, *outs):
    if save:
        y_ref, g_ref, gp_ref, acc_ref = outs
    else:
        y_ref, acc_ref = outs
    step = pl.program_id(0)

    @pl.when(step == 0)
    def _():
        acc_ref[...] = m_ref[...] + vec_ref[7:8]

    for r in range(c_ref.shape[0] // rows):
        at = slice(r * rows, r * rows + rows)
        u = dot(c_ref[at], wup_ref[...]) + bup_ref[...]
        act, slope = gelu_pair(u)
        act = act.astype(BF16)
        if save:
            g_ref[at] = act
            gp_ref[at] = slope.astype(BF16)
        acc_ref[at] += dot(act, wdown_ref[...])

    @pl.when(step == pl.num_programs(0) - 1)
    def _():
        y_ref[...] = acc_ref[...].astype(BF16)


def mlp_fwd(c, m, wup, wdown, bup, vec, save, chunk=1280, rows=256):
    n, width = c.shape
    ff = wup.shape[1]
    outs = [jax.ShapeDtypeStruct((n, width), BF16)]
    specs = [whole((n, width))]
    if save:
        outs += [jax.ShapeDtypeStruct((n, ff), BF16)] * 2
        specs += [pl.BlockSpec((n, chunk), lambda i: (0, i))] * 2
    return pl.pallas_call(
        lambda *refs: mlp_fwd_body(save, rows, *refs),
        grid=(ff // chunk,),
        in_specs=[whole(c.shape), whole(m.shape), pl.BlockSpec((width, chunk), lambda i: (0, i)),
                  pl.BlockSpec((chunk, width), lambda i: (i, 0)), pl.BlockSpec((1, chunk), lambda i: (0, i)), whole(vec.shape)],
        out_specs=specs,
        out_shape=outs,
        scratch_shapes=[pltpu.VMEM((n, width), F32)],
        compiler_params=pltpu.CompilerParams(vmem_limit_bytes=VMEM_LIMIT),
        cost_estimate=cost(26),
        name="feed_forward",
    )(c, m, wup, wdown, bup, vec)


def mlp_both_body(rows, c_ref, m_ref, dz_ref, wup_ref, wdown_ref, bup_ref, vec_ref, y_ref, g_ref, gp_ref, dc_ref, acc_ref):
    step = pl.program_id(0)

    @pl.when(step == 0)
    def _():
        acc_ref[...] = m_ref[...] + vec_ref[7:8]
        dc_ref[...] = jnp.zeros_like(dc_ref)

    for r in range(c_ref.shape[0] // rows):
        at = slice(r * rows, r * rows + rows)
        u = dot(c_ref[at], wup_ref[...]) + bup_ref[...]
        dg = dot(dz_ref[at], wdown_ref[...], ((1,), (1,)))
        act, slope = gelu_pair(u)
        act, slope = act.astype(BF16), slope.astype(BF16)
        g_ref[at] = act
        gp_ref[at] = slope
        acc_ref[at] += dot(act, wdown_ref[...])
        dc_ref[at] += dot((dg * slope.astype(F32)).astype(BF16), wup_ref[...], ((1,), (1,)))

    @pl.when(step == pl.num_programs(0) - 1)
    def _():
        y_ref[...] = acc_ref[...].astype(BF16)


def mlp_both(c, m, dz, wup, wdown, bup, vec, chunk=1280, rows=256):
    n, width = c.shape
    ff = wup.shape[1]
    column = pl.BlockSpec((n, chunk), lambda i: (0, i))
    return pl.pallas_call(
        lambda *refs: mlp_both_body(rows, *refs),
        grid=(ff // chunk,),
        in_specs=[whole(c.shape), whole(m.shape), whole(dz.shape), pl.BlockSpec((width, chunk), lambda i: (0, i)),
                  pl.BlockSpec((chunk, width), lambda i: (i, 0)), pl.BlockSpec((1, chunk), lambda i: (0, i)), whole(vec.shape)],
        out_specs=[whole((n, width)), column, column, whole((n, width))],
        out_shape=[jax.ShapeDtypeStruct((n, width), BF16), jax.ShapeDtypeStruct((n, ff), BF16), jax.ShapeDtypeStruct((n, ff), BF16),
                   jax.ShapeDtypeStruct((n, width), F32)],
        scratch_shapes=[pltpu.VMEM((n, width), F32)],
        compiler_params=pltpu.CompilerParams(vmem_limit_bytes=VMEM_LIMIT),
        cost_estimate=cost(42),
        name="feed_forward_both",
    )(c, m, dz, wup, wdown, bup, vec)


def mlp_up_body(rows, c_ref, wup_ref, bup_ref, g_ref):
    for r in range(c_ref.shape[0] // rows):
        at = slice(r * rows, r * rows + rows)
        g_ref[at] = gelu_pair(dot(c_ref[at], wup_ref[...]) + bup_ref[...])[0].astype(BF16)


def mlp_up(c, wup, bup, after=(), chunk=1280, rows=256):
    n, width = c.shape
    ff = wup.shape[1]
    waits = len(after)
    return pl.pallas_call(
        lambda *refs: mlp_up_body(rows, *refs[:3], *refs[3 + waits:]),
        grid=(ff // chunk,),
        in_specs=[whole(c.shape), pl.BlockSpec((width, chunk), lambda i: (0, i)), pl.BlockSpec((1, chunk), lambda i: (0, i))] + tied(waits),
        out_specs=pl.BlockSpec((n, chunk), lambda i: (0, i)),
        out_shape=jax.ShapeDtypeStruct((n, ff), BF16),
        compiler_params=pltpu.CompilerParams(vmem_limit_bytes=VMEM_LIMIT),
        cost_estimate=cost(0.0125 * n),
        name="feed_forward_up",
    )(c, wup, bup, *after)


def mlp_down_body(g_ref, m_ref, wdown_ref, vec_ref, y_ref, acc_ref):
    step = pl.program_id(0)

    @pl.when(step == 0)
    def _():
        acc_ref[...] = m_ref[...] + vec_ref[7:8]

    acc_ref[...] += dot(g_ref[...], wdown_ref[...])

    @pl.when(step == pl.num_programs(0) - 1)
    def _():
        y_ref[...] = acc_ref[...].astype(BF16)


def mlp_down(g, m, wdown, vec, at, parts, after=(), chunk=1280):
    ff, width = wdown.shape
    rows = g.shape[0] // parts
    waits = len(after)
    return pl.pallas_call(
        lambda *refs: mlp_down_body(*refs[:4], *refs[4 + waits:]),
        grid=(ff // chunk,),
        in_specs=[pl.BlockSpec((rows, chunk), lambda i: (at, i)), pl.BlockSpec((rows, width), lambda i: (at, 0)),
                  pl.BlockSpec((chunk, width), lambda i: (i, 0)), whole(vec.shape)] + tied(waits),
        out_specs=whole((rows, width)),
        out_shape=jax.ShapeDtypeStruct((rows, width), BF16),
        scratch_shapes=[pltpu.VMEM((rows, width), F32)],
        compiler_params=pltpu.CompilerParams(vmem_limit_bytes=VMEM_LIMIT),
        cost_estimate=cost(0.017 * rows),
        name="feed_forward_down",
    )(g, m, wdown, vec, *after)


def mlp_bwd_body(save, rows, dz_ref, gp_ref, wup_ref, wdown_ref, dc_ref, *outs):
    @pl.when(pl.program_id(0) == 0)
    def _():
        dc_ref[...] = jnp.zeros_like(dc_ref)

    for r in range(dz_ref.shape[0] // rows):
        at = slice(r * rows, r * rows + rows)
        dg = dot(dz_ref[at], wdown_ref[...], ((1,), (1,)))
        du = (dg * gp_ref[at].astype(F32)).astype(BF16)
        if save:
            outs[0][at] = du
        dc_ref[at] += dot(du, wup_ref[...], ((1,), (1,)))


def mlp_bwd(dz, gp, wup, wdown, save, at=0, parts=1, earlier=(), after=(), chunk=1280, rows=256):
    n, width = dz.shape
    ff = wup.shape[1]
    args = [dz, gp, wup, wdown, *earlier, *after]
    outs = [jax.ShapeDtypeStruct((n * parts, width), F32)]
    specs = [pl.BlockSpec((n, width), lambda i: (at, 0))]
    if save:
        outs += [jax.ShapeDtypeStruct((n, ff), BF16)]
        specs += [pl.BlockSpec((n, chunk), lambda i: (0, i))]
    return pl.pallas_call(
        lambda *refs: mlp_bwd_body(save, rows, *refs[:4], *refs[len(args):]),
        grid=(ff // chunk,),
        in_specs=[whole(dz.shape), pl.BlockSpec((n, chunk), lambda i: (at, i)), pl.BlockSpec((width, chunk), lambda i: (0, i)),
                  pl.BlockSpec((chunk, width), lambda i: (i, 0))] + tied(len(args) - 4),
        out_specs=specs,
        out_shape=outs,
        input_output_aliases={4 + i: i for i in range(len(earlier))},
        compiler_params=pltpu.CompilerParams(vmem_limit_bytes=VMEM_LIMIT),
        cost_estimate=cost(22 / parts),
        name="feed_forward_back",
    )(*args)


def up_grad_body(c_ref, order_ref, du_ref, keep_ref, send_ref, sum_ref, ct_ref):
    half = keep_ref.shape[0]

    @pl.when(pl.program_id(0) == 0)
    def _():
        ct_ref[:2 * half] = dot(order_ref[...], c_ref[...], ((1,), (1,))).astype(BF16)
        ct_ref[2 * half:] = jnp.ones_like(ct_ref[2 * half:])

    grad = dot(ct_ref[...], du_ref[...])
    keep_ref[...] = grad[:half].astype(BF16)
    send_ref[...] = grad[half:2 * half].astype(BF16)
    sum_ref[...] = grad[2 * half:2 * half + 8]


def up_grad(c, order, du, at, parts, after=(), chunk=1280):
    n, width = c.shape
    ff = du.shape[1] // parts
    first = at * ff // chunk
    waits = len(after)
    column = lambda rows: pl.BlockSpec((rows, chunk), lambda i: (0, i))
    return pl.pallas_call(
        lambda *refs: up_grad_body(*refs[:3], *refs[3 + waits:]),
        grid=(ff // chunk,),
        in_specs=[whole(c.shape), whole(order.shape), pl.BlockSpec((n, chunk), lambda i: (0, i + first))] + tied(waits),
        out_specs=[column(width // 2), column(width // 2), column(8)],
        out_shape=[jax.ShapeDtypeStruct((width // 2, ff), BF16)] * 2 + [jax.ShapeDtypeStruct((8, ff), F32)],
        scratch_shapes=[pltpu.VMEM((width + 16, n), BF16)],
        compiler_params=pltpu.CompilerParams(vmem_limit_bytes=VMEM_LIMIT),
        cost_estimate=cost(13 / parts),
        name="up_gradient",
    )(c, order, du, *after)


def mlp_grad_body(rows, dz_ref, gp_ref, wup_ref, wdown_ref, early_ref, c_ref, order_ref, dc_ref, keep_ref, send_ref, sum_ref, du_ref, ct_ref):
    half = keep_ref.shape[0]
    count = early_ref.shape[0]

    @pl.when(pl.program_id(0) == 0)
    def _():
        dc_ref[...] = jnp.zeros_like(dc_ref)
        ct_ref[:2 * half] = dot(order_ref[...], c_ref[...], ((1,), (1,))).astype(BF16)
        ct_ref[2 * half:] = jnp.ones_like(ct_ref[2 * half:])

    for r in range(dz_ref.shape[0] // rows):
        at = slice(r * rows, r * rows + rows)
        dg = dot(dz_ref[at], wdown_ref[...], ((1,), (1,)))
        du = (dg * gp_ref[at].astype(F32)).astype(BF16)
        du_ref[at] = du
        dc_ref[at] += dot(du, wup_ref[...], ((1,), (1,)))
    grad = dot(ct_ref[:, :count], early_ref[...]) + dot(ct_ref[:, count:], du_ref[...])
    keep_ref[...] = grad[:half].astype(BF16)
    send_ref[...] = grad[half:2 * half].astype(BF16)
    sum_ref[...] = grad[2 * half:2 * half + 8]


def mlp_grad(dz, gp, wup, wdown, early, c, order, dc, after=(), chunk=1280, rows=256):
    count, width = dz.shape
    n, ff = gp.shape
    at = n // count - 1
    waits = 1 + len(after)
    column = lambda rows: pl.BlockSpec((rows, chunk), lambda i: (0, i))
    return pl.pallas_call(
        lambda *refs: mlp_grad_body(rows, *refs[:7], *refs[7 + waits:]),
        grid=(ff // chunk,),
        in_specs=[whole(dz.shape), pl.BlockSpec((count, chunk), lambda i: (at, i)), column(width), pl.BlockSpec((chunk, width), lambda i: (i, 0)),
                  column(n - count), whole(c.shape), whole(order.shape)] + tied(waits),
        out_specs=[pl.BlockSpec((count, width), lambda i: (at, 0)), column(width // 2), column(width // 2), column(8)],
        out_shape=[jax.ShapeDtypeStruct((n, width), F32)] + [jax.ShapeDtypeStruct((width // 2, ff), BF16)] * 2 + [jax.ShapeDtypeStruct((8, ff), F32)],
        scratch_shapes=[pltpu.VMEM((count, chunk), BF16), pltpu.VMEM((width + 16, n), BF16)],
        input_output_aliases={7: 0},
        compiler_params=pltpu.CompilerParams(vmem_limit_bytes=VMEM_LIMIT),
        cost_estimate=cost(21),
        name="feed_forward_gradients",
    )(dz, gp, wup, wdown, early, c, order, dc, *after)


def down_grad_body(g_ref, dz_ref, out_ref):
    out_ref[...] = dot(g_ref[...], dz_ref[...], ((0,), (0,))).astype(BF16)


def down_grad(g, dz, after=(), chunk=1280):
    n, ff = g.shape
    width = dz.shape[1]
    waits = len(after)
    return pl.pallas_call(
        lambda *refs: down_grad_body(*refs[:2], *refs[2 + waits:]),
        grid=(ff // chunk,),
        in_specs=[pl.BlockSpec((n, chunk), lambda i: (0, i)), whole(dz.shape)] + tied(waits),
        out_specs=pl.BlockSpec((chunk, width), lambda i: (i, 0)),
        out_shape=jax.ShapeDtypeStruct((ff, width), BF16),
        compiler_params=pltpu.CompilerParams(vmem_limit_bytes=VMEM_LIMIT),
        cost_estimate=cost(12),
        name="down_gradient",
    )(g, dz, *after)


def attn_bwd_body(grads, base_ref, dc_ref, dz_ref, m_ref, h_ref, qkv_ref, e_ref, o_ref, inv_ref, proj_ref, vec_ref, dh_ref, *outs):
    if grads:
        dr_ref, dqkv_ref, small_ref = outs
    width = h_ref.shape[2]
    vec = vec_ref[...]

    if grads:
        @pl.when(pl.program_id(0) == 0)
        def _():
            small_ref[...] = jnp.zeros_like(small_ref) if base_ref is None else base_ref[...]

    dz = dz_ref[0].astype(F32)
    back, g_gain1, g_shift1 = norm_back(m_ref[0], vec[1:2], dc_ref[0])
    dm = dz + back
    dr = dm.astype(BF16)
    if grads:
        dr_ref[0] = dr
    do_all = dot(dr, proj_ref[:, 3 * width:4 * width], ((1,), (1,))).astype(BF16)
    seq = h_ref.shape[1]
    head_of = lax.broadcasted_iota(jnp.int32, (1, 128), 1) // HEAD_DIM
    ones = jnp.ones((seq, 128), BF16)
    zero = jnp.zeros((seq, 128), BF16)
    dq_all, dk_all, dv_all = [], [], []
    for g in range(width // 128):
        at = slice(128 * g, 128 * g + 128)
        q = qkv_ref[0, :, 128 * g:128 * g + 128]
        k = qkv_ref[0, :, width + 128 * g:width + 128 * g + 128]
        v = jnp.concatenate([qkv_ref[0, :, 2 * width + 128 * g:2 * width + 128 * g + 128], ones], axis=1)
        scaled = do_all[:, at].astype(F32) * (inv_ref[0, :, at] * SCALE)
        do = scaled.astype(BF16)
        less = (-scaled * o_ref[0, :, at].astype(F32)).astype(BF16)
        do_t, q_t = do.T, q.T
        dq = None
        dk_t, dv_t = [], []
        for j in range(GROUP):
            mine = head_of == j
            e = e_ref[0, GROUP * g + j]
            rows = slice(HEAD_DIM * j, HEAD_DIM * j + HEAD_DIM)
            dv_t.append(dot(do_t[rows], e))
            dp = dot(jnp.concatenate([jnp.where(mine, do, zero), jnp.where(mine, less, zero)], axis=1), v, ((1,), (1,)))
            ds = (e.astype(F32) * dp).astype(BF16)
            part = dot(ds, jnp.where(mine, k, zero))
            dq = part if dq is None else dq + part
            dk_t.append(dot(q_t[rows], ds))
        dq_all.append(dq.astype(BF16))
        dk_all.append(jnp.concatenate(dk_t, axis=0).astype(BF16).T)
        dv_all.append((jnp.concatenate(dv_t, axis=0) * (1.0 / SCALE)).astype(BF16).T)
    dqkv = jnp.concatenate(dq_all + dk_all + dv_all, axis=1)
    if grads:
        dqkv_ref[0] = dqkv
    da = dot(dqkv, proj_ref[:, :3 * width], ((1,), (1,)))
    back, g_gain0, g_shift0 = norm_back(h_ref[0].astype(F32), vec[0:1], da)
    dh_ref[0] = (dm + back).astype(dh_ref.dtype)
    if not grads:
        return
    total = lambda x: jnp.sum(x.astype(F32), axis=0, keepdims=True)
    small_ref[...] += jnp.concatenate(
        [g_gain0, g_gain1, g_shift0, g_shift1, total(dqkv[:, :width]), total(dqkv[:, 2 * width:]), total(dr), total(dz)], axis=0)


def attn_bwd(dc, dz, m, h, qkv, e, o, inv, proj, vec, at, parts, grads, earlier=(), after=()):
    n, seq, width = h.shape
    count = n // parts
    row = lambda *tail: pl.BlockSpec((1,) + tail, lambda i: (i + at * count,) + (0,) * len(tail))
    if grads:
        shapes = [((seq, width), F32), ((seq, width), BF16), ((seq, 3 * width), BF16)]
        specs = [row(*s) for s, _ in shapes] + [whole((8, width))]
        results = [jax.ShapeDtypeStruct((n,) + s, d) for s, d in shapes] + [jax.ShapeDtypeStruct((8, width), F32)]
    else:
        specs = [pl.BlockSpec((1, seq, width), lambda i: (i, 0, 0))]
        results = [jax.ShapeDtypeStruct((count, seq, width), BF16)]
    args = [dc, dz, m, h, qkv, e, o, inv, proj, vec]
    in_specs = [row(seq, width), row(seq, width), row(seq, width), row(seq, width), row(seq, 3 * width), row(HEADS, seq, seq),
                row(seq, width), row(seq, width), whole(proj.shape), whole(vec.shape)]
    base = len(args)
    if earlier:
        args += [earlier[3], *earlier[:3]]
        in_specs += [whole(earlier[3].shape)] + tied(3)
    aliases = {base + 1 + i: i for i in range(3)} if earlier else {}
    args += after
    in_specs += tied(len(after))
    used = len(args)

    def body(*refs):
        attn_bwd_body(grads, refs[base] if earlier else None, *refs[:base], *refs[used:])

    return pl.pallas_call(
        body,
        grid=(count,),
        in_specs=in_specs,
        out_specs=specs,
        out_shape=results,
        input_output_aliases=aliases,
        compiler_params=pltpu.CompilerParams(vmem_limit_bytes=VMEM_LIMIT),
        cost_estimate=cost(7 * count),
        name="attention_back",
    )(*args)


def proj_grad_body(a_ref, dqkv_ref, o_ref, dr_ref, table_ref, order_ref, keep_ref, send_ref, at_ref):
    step = pl.program_id(0)
    width = a_ref.shape[1]
    half = width // 2
    order = order_ref[...]

    def put(at, value):
        keep_ref[:, at] = value[:half].astype(BF16)
        send_ref[:, at] = value[half:].astype(BF16)

    @pl.when(step == 0)
    def _():
        at_ref[...] = dot(order, a_ref[...], ((1,), (1,))).astype(BF16)
        put(slice(3 * width, 4 * width), dot(dot(order, o_ref[...], ((1,), (1,))).astype(BF16), dr_ref[...]))
        put(slice(4 * width, None), dot(order, table_ref[...].astype(BF16)))

    put(pl.ds(pl.multiple_of(step * width, 128), width), dot(at_ref[...], dqkv_ref[...]))


def proj_grad(a, dqkv, o, dr, table, order, after=()):
    n, width = a.shape
    waits = len(after)
    shape = (width // 2, 4 * width + table.shape[1])
    return pl.pallas_call(
        lambda *refs: proj_grad_body(*refs[:6], *refs[6 + waits:]),
        grid=(3,),
        in_specs=[whole(a.shape), pl.BlockSpec((n, width), lambda i: (0, i)), whole(o.shape), whole(dr.shape), whole(table.shape),
                  whole(order.shape)] + tied(waits),
        out_specs=[whole(shape)] * 2,
        out_shape=[jax.ShapeDtypeStruct(shape, BF16)] * 2,
        scratch_shapes=[pltpu.VMEM((width, n), BF16)],
        compiler_params=pltpu.CompilerParams(vmem_limit_bytes=VMEM_LIMIT),
        cost_estimate=cost(9),
        name="projection_gradients",
    )(a, dqkv, o, dr, table, order, *after)


def place_body(count, to_ref, *refs):
    pieces, out_ref, sems = refs[:count], refs[count], refs[count + 1]
    copies = [pltpu.make_async_copy(piece, out_ref.at[to_ref[i]], sems.at[i]) for i, piece in enumerate(pieces)]
    for copy in copies:
        copy.start()
    for copy in copies:
        copy.wait()


def place(pieces, to, after=()):
    rows, columns = pieces[0].shape
    count, waits = len(pieces), len(after)
    out = pl.pallas_call(
        lambda *refs: place_body(count, *refs[:count + 1], *refs[count + 1 + waits:]),
        in_specs=[pl.BlockSpec(memory_space=pltpu.SMEM)] + [pl.BlockSpec(memory_space=pl.ANY)] * count + tied(waits),
        out_specs=pl.BlockSpec(memory_space=pltpu.VMEM),
        out_shape=jax.ShapeDtypeStruct((count, rows, columns), BF16),
        scratch_shapes=[pltpu.SemaphoreType.DMA((count,))],
        compiler_params=pltpu.CompilerParams(vmem_limit_bytes=VMEM_LIMIT),
        cost_estimate=cost(4),
        name="place_pieces",
    )(to, *pieces, *after)
    return out.reshape(count * rows, columns)


def place_down_body(count, to_ref, g_ref, m_ref, vec_ref, *refs):
    pieces, (w_ref, y_ref), sems = refs[:count], refs[count:count + 2], refs[count + 2]
    rows = pieces[0].shape[0]
    copies = [pltpu.make_async_copy(piece, w_ref.at[pl.ds(pl.multiple_of(to_ref[i] * rows, rows), rows)], sems.at[i])
              for i, piece in enumerate(pieces)]
    for copy in copies:
        copy.start()
    for copy in copies:
        copy.wait()
    y_ref[...] = (m_ref[...] + vec_ref[7:8] + dot(g_ref[...], w_ref[...])).astype(BF16)


def place_down(pieces, to, g, m, vec, parts):
    rows, width = pieces[0].shape
    count = len(pieces)
    ff = count * rows
    n = g.shape[0] // parts
    return pl.pallas_call(
        lambda *refs: place_down_body(count, *refs),
        grid=(1,),
        in_specs=[pl.BlockSpec(memory_space=pltpu.SMEM), whole((n, ff)), whole((n, width)), whole(vec.shape)] + tied(count),
        out_specs=[whole((ff, width)), whole((n, width))],
        out_shape=[jax.ShapeDtypeStruct((ff, width), BF16), jax.ShapeDtypeStruct((n, width), BF16)],
        scratch_shapes=[pltpu.SemaphoreType.DMA((count,))],
        compiler_params=pltpu.CompilerParams(vmem_limit_bytes=VMEM_LIMIT),
        cost_estimate=cost(10),
        name="place_and_feed_forward_down",
    )(to, g, m, vec, *pieces)


def places(count):
    return count // 4, 2, 2


def hop(value, kind, step=1):
    zs, ys, cores = places(lax.axis_size("dp"))
    pairs = []
    for z in range(zs):
        for y in range(ys):
            for c in range(cores):
                to = {"core": (z, y, c ^ 1), "y": (z, y ^ 1, c), "z": ((z + step) % zs, y, c)}[kind]
                pairs.append(((z * ys + y) * cores + c, (to[0] * ys + to[1]) * cores + to[2]))
    return lax.ppermute(value, "dp", pairs)


def behind_me():
    zs, ys, cores = places(lax.axis_size("dp"))
    me = lax.axis_index("dp")
    return me // (cores * ys), (me // cores) % ys, me % cores


def along_line(shard):
    return [shard] + [hop(shard, "z", step) for step in range(1, places(lax.axis_size("dp"))[0])]


def both(mine, got):
    return (mine.astype(F32) + got.astype(F32)).astype(BF16)


def scatter_order(shard):
    zs, ys, cores = places(lax.axis_size("dp"))
    z, y, c = behind_me()
    row = jnp.arange(zs * ys * cores * shard)
    block = row // shard
    to = (((z + block % zs) % zs) * ys + (y ^ (block // zs % ys))) * cores + (c ^ (block // (zs * ys)))
    return (jnp.arange(zs * ys * cores * shard)[None, :] == (to * shard + row % shard)[:, None]).astype(BF16)


def y_step(mine, got):
    half = mine.shape[0] // 2
    return (mine[:half], got[:half]), hop(both(mine[half:], got[half:]), "y")


def z_step(mine, got):
    zs, _, _ = places(lax.axis_size("dp"))
    rows = got.shape[0] // zs
    terms = [[term[k * rows:k * rows + rows] for term in (*mine, got)] for k in range(zs)]
    return terms[0] + [hop(total(terms[k]).astype(BF16), "z", k) for k in range(1, zs)]


def total(terms):
    out = terms[0].astype(F32)
    for term in terms[1:]:
        out = out + term.astype(F32)
    return out


def held(value, *after):
    return lax.optimization_barrier((value, *after))[0]


def siblings(pieces, *after):
    return [hop(held(piece, *after), "core") for piece in pieces]


def places_of_pieces():
    zs, ys, cores = places(lax.axis_size("dp"))
    z, y, c = behind_me()
    to = []
    for core in (c, 1 - c):
        for row in (y, 1 - y):
            to += [(((z + zs - step) % zs) * ys + row) * cores + core for step in range(zs)]
    return jnp.stack(to).astype(jnp.int32)


def on_device(tokens, lengths, cotangent, w_qkv, w_out, w_up, w_down, norm_gain, norm_bias, bias_vec, up_bias):
    section = lax.axis_index("section")
    windows, seq, width = tokens.shape
    n = windows * seq
    shard = w_qkv.shape[1]
    per_row = up_bias.shape[1] // shard
    ff = w_up.shape[2]
    parts = 2
    part = windows // parts
    by_hand = lax.axis_size("dp") == 16
    table = jnp.concatenate([norm_gain[0], norm_bias[0], bias_vec[0]], axis=0).T
    table = jnp.concatenate([table, up_bias.reshape(shard, per_row)], axis=1)
    used = table.shape[1]
    table = jnp.pad(table, ((0, 0), (0, 128 - used)))
    packed = jnp.concatenate([w_qkv[0], w_out[0], table], axis=1)
    if by_hand:
        down = w_down[0]
        order, to = scatter_order(shard), places_of_pieces()
        wup = lax.all_gather(w_up[0], "dp", axis=0, tiled=True)
        proj_z = [hop(packed, "z", step) for step in (1, 2, 3)]
        proj_y0, down_y0 = hop(packed, "y"), hop(down, "y")
        now = (*proj_z, proj_y0, down_y0)
        down_1, down_3 = hop(held(down, *now), "z", 1), hop(held(down, *now), "z", 3)
        proj_y = [hop(held(piece, *now), "y") for piece in proj_z]
        now = (down_1, down_3, *proj_y)
        pieces = [packed, *proj_z, proj_y0, *proj_y]
        proj = place(pieces + siblings(pieces, *now), to)
        down_2 = hop(held(down, *now), "z", 2)
        down_y1, down_y3 = hop(held(down_1, *now), "y"), hop(held(down_3, *now), "y")
    else:
        order = (jnp.arange(width)[None, :] == jnp.arange(width)[:, None]).astype(BF16)
        proj = lax.all_gather(packed, "dp", axis=0, tiled=True)
        wup = lax.all_gather(w_up[0], "dp", axis=0, tiled=True)
        wdown = lax.all_gather(w_down[0], "dp", axis=0, tiled=True)
    small = proj[:, 4 * width:4 * width + used]
    vec = small[:, :8].T.astype(F32)
    bup = small[:, 8:].reshape(1, ff).astype(F32)

    mid, c = attn_fwd(tokens, lengths, proj, vec, False)
    c = c.reshape(n, width)
    mid = mid.reshape(n, width)
    if by_hand:
        now = (down_2, down_y1, down_y3, c)
        down_y2 = hop(held(down_2, *now), "y")
    act = mlp_up(c, wup, bup)
    if by_hand:
        pieces = [down, down_1, down_2, down_3, down_y0, down_y1, down_y2, down_y3]
        wdown, y_a = place_down(pieces + siblings(pieces, act), to, act, mid, vec, parts)
    else:
        y_a = mlp_down(act, mid, wdown, vec, 0, parts)
    y_b = mlp_down(act, mid, wdown, vec, 1, parts)
    kept = ()
    arrived = [lax.ppermute(y.reshape(part, seq, width), "section", [(0, 1)]) for y in (y_a, y_b)]
    h = []
    for at in range(parts):
        h.append(jnp.where(section == 0, tokens[at * part:at * part + part], held(arrived[at], *kept[:1])))
        kept = attn_fwd(h[at], lengths, proj, vec, True, at, parts, kept)
    h = jnp.concatenate(h)
    m, c, qkv, e, o, a, inv = kept
    c = c.reshape(n, width)
    y, g, gp, dc = mlp_both(c, m.reshape(n, width), cotangent.reshape(n, width), wup, wdown, bup, vec)
    dc = dc.reshape(tokens.shape)
    arrived = []
    for at in range(parts):
        back, = attn_bwd(dc, cotangent, m, h, qkv, e, o, inv, proj, vec, at, parts, False)
        arrived.append(lax.ppermute(back, "section", [(1, 0)]))
    dz = [jnp.where(section == 1, cotangent[:part], arrived[0])]
    dc, du = mlp_bwd(dz[0].reshape(part * seq, width), gp, wup, wdown, True, 0, parts)
    dz.append(jnp.where(section == 1, cotangent[part:], held(arrived[1], dc)))
    last = dz[1].reshape(part * seq, width)
    dz = jnp.concatenate(dz)
    g_down = down_grad(g, dz.reshape(n, width))
    sum_down = lax.psum_scatter(g_down, "dp", scatter_dimension=0, tiled=True).astype(F32)
    dc, keep_u, send_u, bup_u = mlp_grad(last, gp, wup, wdown, du, c, order, dc, (g_down,))
    dc = dc.reshape(tokens.shape)
    if by_hand:
        got_u = hop(send_u, "core")
        half = ff // 2
        mine_a, got_a = y_step(keep_u[:, :half], got_u[:, :half])
        mine_b, got_b = y_step(keep_u[:, half:], got_u[:, half:])
        back = attn_bwd(dc, dz, m, h, qkv, e, o, inv, proj, vec, 0, 1, True, (), (got_u,))
        terms_a = z_step(mine_a, held(got_a, back[3]))
        wait = (got_a,)
    else:
        back = attn_bwd(dc, dz, m, h, qkv, e, o, inv, proj, vec, 0, 1, True)
        wait = ()
    dh, dr, dqkv, smalls = back
    g_bup = bup_u[0].reshape(width, per_row)
    g_table = jnp.concatenate([smalls.T, g_bup], axis=1)
    g_table = jnp.pad(g_table, ((0, 0), (0, 128 - used)))
    keep_p, send_p = proj_grad(
        a.reshape(n, width), dqkv.reshape(n, 3 * width), o.reshape(n, width), dr.reshape(n, width), g_table, order, wait)
    if by_hand:
        terms_b = z_step(mine_b, got_b)
        sum_up = jnp.concatenate([total(terms_a), total(terms_b)], axis=1)
        mine_p, got_p = y_step(keep_p, hop(held(send_p, got_b, *terms_a[3:]), "core"))
        sum_proj = total(z_step(mine_p, held(got_p, *terms_b)))
    else:
        scatter = lambda *halves: lax.psum_scatter(jnp.concatenate(halves), "dp", scatter_dimension=0, tiled=True).astype(F32)
        sum_up = scatter(keep_u, send_u)
        sum_proj = scatter(keep_p, send_p)
    vectors = sum_proj[:, 4 * width:4 * width + 8].T
    return (
        y.reshape((1,) + tokens.shape),
        dh[None],
        sum_proj[None, :, :3 * width],
        sum_proj[None, :, 3 * width:4 * width],
        sum_up[None],
        sum_down[None],
        vectors[None, 0:2],
        vectors[None, 2:4],
        vectors[None, 4:8],
        sum_proj[:, 4 * width + 8:4 * width + used].reshape(1, -1),
    )


def solution(mesh):
    sharded = [P("section", "dp", None)] * 4 + [P("section", None, "dp")] * 3 + [P("section", "dp")]
    windows = P("dp", None, None)
    out = P("section", "dp", None, None)
    return jax.shard_map(
        on_device, mesh=mesh, in_specs=(windows, P("dp"), windows, *sharded), out_specs=(out, out, *sharded), check_vma=False
    )
```

```python
import jax
import jax.numpy as jnp
from jax import lax
from jax.experimental import pallas as pl
from jax.experimental.pallas import tpu as pltpu
from jax.sharding import PartitionSpec as P

HEADS = 20
HEAD_DIM = 32
GROUP = 128 // HEAD_DIM
SCALE = HEAD_DIM ** -0.5
LOG2E = 1.4426950408889634
VMEM_LIMIT = 56 * 1024 * 1024
F32 = jnp.float32
BF16 = jnp.bfloat16


def cost(us):
    return pl.CostEstimate(flops=int(us * 1.1e9), bytes_accessed=1024, transcendentals=0)


def tied(count):
    return [pl.BlockSpec(memory_space=pl.ANY)] * count


def dot(a, b, dims=((1,), (0,))):
    return lax.dot_general(a, b, (dims, ((), ())), preferred_element_type=F32)


def gelu_pair(u):
    below = 0.5 + 0.5 * lax.erf(u * 0.7071067811865476)
    return u * below, below + (0.3989422804014327 * u) * jnp.exp(-0.5 * (u * u))


def normed(v, gain, shift):
    centered = v - jnp.mean(v, axis=-1, keepdims=True)
    spread = jnp.mean(centered * centered, axis=-1, keepdims=True)
    hat = centered * lax.rsqrt(spread + 1e-05)
    return hat * gain + shift


def norm_back(v, gain, grad):
    centered = v - jnp.mean(v, axis=-1, keepdims=True)
    spread = jnp.mean(centered * centered, axis=-1, keepdims=True)
    inv = lax.rsqrt(spread + 1e-05)
    hat = centered * inv
    g = grad * gain
    back = inv * (g - jnp.mean(g, axis=-1, keepdims=True) - hat * jnp.mean(g * hat, axis=-1, keepdims=True))
    return back, jnp.sum(grad * hat, axis=0, keepdims=True), jnp.sum(grad, axis=0, keepdims=True)


def attn_fwd_body(save, first_window, len_ref, h_ref, *rest):
    if save:
        arrived_ref, wqkv_ref, vec_ref, m_ref, c_ref, qkv_ref, e_ref, o_ref, a_ref, inv_ref, taken_ref = rest
    else:
        wqkv_ref, m_ref, c_ref = rest
    width = h_ref.shape[2]
    seq = h_ref.shape[1]
    length = len_ref[pl.program_id(0) + first_window]
    if save:
        taken = jnp.where(len_ref[len_ref.shape[0] - 1] == 0, h_ref[0], arrived_ref[0])
        taken_ref[0] = taken
        h = taken.astype(F32)
        vec = vec_ref[...]
    else:
        h = h_ref[0].astype(F32)
        vec = wqkv_ref[:, 4 * width:].astype(F32).T
    a = normed(h, vec[0:1], vec[2:3]).astype(BF16)
    q_all = (dot(a, wqkv_ref[:, :width]) + vec[4:5]).astype(BF16)
    k_all = dot(a, wqkv_ref[:, width:2 * width]).astype(BF16)
    v_all = (dot(a, wqkv_ref[:, 2 * width:3 * width]) + vec[5:6]).astype(BF16)
    if save:
        a_ref[0] = a
        qkv_ref[0, :, :width] = q_all
        qkv_ref[0, :, width:2 * width] = k_all
        qkv_ref[0, :, 2 * width:] = v_all
    head_of = lax.broadcasted_iota(jnp.int32, (1, 128), 1) // HEAD_DIM
    key_at = lax.broadcasted_iota(jnp.int32, (seq, 128), 0)
    lane = lax.broadcasted_iota(jnp.int32, (seq, 128), 1)
    past = jnp.where((lane == 0) & (key_at >= length), -1e30, 0.0).astype(BF16)
    first = jnp.where(lane == 0, 1.0, 0.0).astype(BF16)
    ones = jnp.ones((seq, 128), BF16)
    zero = jnp.zeros((seq, 128), BF16)
    mixed = []
    for g in range(width // 128):
        at = slice(128 * g, 128 * g + 128)
        q, v = q_all[:, at], v_all[:, at]
        k = jnp.concatenate([k_all[:, at], past], axis=1)
        acc, inv = None, None
        stacked = dot(jnp.concatenate([jnp.concatenate([jnp.where(head_of == j, q, zero), first], axis=1) for j in range(GROUP)], axis=0), k, ((1,), (1,)))
        for j in range(GROUP):
            mine = head_of == j
            s = stacked[seq * j:seq * j + seq]
            e = jnp.exp2((s - jnp.max(s, axis=1, keepdims=True)) * (SCALE * LOG2E)).astype(BF16)
            if save:
                e_ref[0, GROUP * g + j] = e
            both_parts = dot(e, jnp.concatenate([jnp.where(mine, v, zero), ones], axis=1))
            one_over = 1.0 / both_parts[:, 128:]
            part = both_parts[:, :128] * one_over
            acc = part if acc is None else acc + part
            inv = one_over if inv is None else jnp.where(mine, one_over, inv)
        mixed.append(acc.astype(BF16))
        if save:
            inv_ref[0, :, at] = inv
    o = jnp.concatenate(mixed, axis=1)
    if save:
        o_ref[0] = o
    m = h + dot(o, wqkv_ref[:, 3 * width:4 * width]) + vec[6:7]
    m_ref[0] = m
    c_ref[0] = normed(m, vec[1:2], vec[3:4]).astype(BF16)


def whole(shape):
    return pl.BlockSpec(shape, lambda *_: (0,) * len(shape))


def attn_fwd(h, lengths, proj, save, at=0, parts=1, arrived=None, vec=None, earlier=(), after=()):
    n, seq, width = h.shape
    count = n // parts
    row = lambda *tail: pl.BlockSpec((1,) + tail, lambda i, *_: (i + at * count,) + (0,) * len(tail))
    shapes = [((seq, width), F32), ((seq, width), BF16)]
    args, in_specs = [h], [row(seq, width)]
    if save:
        shapes += [((seq, 3 * width), BF16), ((HEADS, seq, seq), BF16), ((seq, width), BF16), ((seq, width), BF16), ((seq, width), F32), ((seq, width), BF16)]
        args += [arrived, proj, vec]
        in_specs += [pl.BlockSpec((1, seq, width), lambda i, *_: (i, 0, 0)), whole(proj.shape), whole(vec.shape)]
    else:
        args += [proj]
        in_specs += [whole(proj.shape)]
    used, waits = 1 + len(args), len(earlier) + len(after)
    return pl.pallas_call(
        lambda *refs: attn_fwd_body(save, at * count, *refs[:used], *refs[used + waits:]),
        grid_spec=pltpu.PrefetchScalarGridSpec(
            num_scalar_prefetch=1,
            grid=(count,),
            in_specs=in_specs + tied(waits),
            out_specs=[row(*s) for s, _ in shapes],
        ),
        out_shape=[jax.ShapeDtypeStruct((n,) + s, d) for s, d in shapes],
        input_output_aliases={used + i: i for i in range(len(earlier))},
        compiler_params=pltpu.CompilerParams(vmem_limit_bytes=VMEM_LIMIT),
        cost_estimate=cost(4.5 * count),
        name="attention_forward",
    )(lengths, *args, *earlier, *after)


def mlp_fwd_body(save, rows, c_ref, m_ref, wup_ref, wdown_ref, bup_ref, vec_ref, *outs):
    if save:
        y_ref, g_ref, gp_ref, acc_ref = outs
    else:
        y_ref, acc_ref = outs
    step = pl.program_id(0)

    @pl.when(step == 0)
    def _():
        acc_ref[...] = m_ref[...] + vec_ref[7:8]

    for r in range(c_ref.shape[0] // rows):
        at = slice(r * rows, r * rows + rows)
        u = dot(c_ref[at], wup_ref[...]) + bup_ref[...]
        act, slope = gelu_pair(u)
        act = act.astype(BF16)
        if save:
            g_ref[at] = act
            gp_ref[at] = slope.astype(BF16)
        acc_ref[at] += dot(act, wdown_ref[...])

    @pl.when(step == pl.num_programs(0) - 1)
    def _():
        y_ref[...] = acc_ref[...].astype(BF16)


def mlp_fwd(c, m, wup, wdown, bup, vec, save, chunk=1280, rows=256):
    n, width = c.shape
    ff = wup.shape[1]
    outs = [jax.ShapeDtypeStruct((n, width), BF16)]
    specs = [whole((n, width))]
    if save:
        outs += [jax.ShapeDtypeStruct((n, ff), BF16)] * 2
        specs += [pl.BlockSpec((n, chunk), lambda i: (0, i))] * 2
    return pl.pallas_call(
        lambda *refs: mlp_fwd_body(save, rows, *refs),
        grid=(ff // chunk,),
        in_specs=[whole(c.shape), whole(m.shape), pl.BlockSpec((width, chunk), lambda i: (0, i)),
                  pl.BlockSpec((chunk, width), lambda i: (i, 0)), pl.BlockSpec((1, chunk), lambda i: (0, i)), whole(vec.shape)],
        out_specs=specs,
        out_shape=outs,
        scratch_shapes=[pltpu.VMEM((n, width), F32)],
        compiler_params=pltpu.CompilerParams(vmem_limit_bytes=VMEM_LIMIT),
        cost_estimate=cost(26),
        name="feed_forward",
    )(c, m, wup, wdown, bup, vec)


def mlp_both_body(rows, c_ref, m_ref, dz_ref, wup_ref, wdown_ref, bup_ref, vec_ref, y_ref, g_ref, gp_ref, dc_ref, acc_ref):
    step = pl.program_id(0)

    @pl.when(step == 0)
    def _():
        acc_ref[...] = m_ref[...] + vec_ref[7:8]
        dc_ref[...] = jnp.zeros_like(dc_ref)

    for r in range(c_ref.shape[0] // rows):
        at = slice(r * rows, r * rows + rows)
        u = dot(c_ref[at], wup_ref[...]) + bup_ref[...]
        dg = dot(dz_ref[at], wdown_ref[...], ((1,), (1,)))
        act, slope = gelu_pair(u)
        act, slope = act.astype(BF16), slope.astype(BF16)
        g_ref[at] = act
        gp_ref[at] = slope
        acc_ref[at] += dot(act, wdown_ref[...])
        dc_ref[at] += dot((dg * slope.astype(F32)).astype(BF16), wup_ref[...], ((1,), (1,)))

    @pl.when(step == pl.num_programs(0) - 1)
    def _():
        y_ref[...] = acc_ref[...].astype(BF16)


def mlp_both(c, m, dz, wup, wdown, bup, vec, chunk=1280, rows=256):
    n, width = c.shape
    ff = wup.shape[1]
    column = pl.BlockSpec((n, chunk), lambda i: (0, i))
    return pl.pallas_call(
        lambda *refs: mlp_both_body(rows, *refs),
        grid=(ff // chunk,),
        in_specs=[whole(c.shape), whole(m.shape), whole(dz.shape), pl.BlockSpec((width, chunk), lambda i: (0, i)),
                  pl.BlockSpec((chunk, width), lambda i: (i, 0)), pl.BlockSpec((1, chunk), lambda i: (0, i)), whole(vec.shape)],
        out_specs=[whole((n, width)), column, column, whole((n, width))],
        out_shape=[jax.ShapeDtypeStruct((n, width), BF16), jax.ShapeDtypeStruct((n, ff), BF16), jax.ShapeDtypeStruct((n, ff), BF16),
                   jax.ShapeDtypeStruct((n, width), F32)],
        scratch_shapes=[pltpu.VMEM((n, width), F32)],
        compiler_params=pltpu.CompilerParams(vmem_limit_bytes=VMEM_LIMIT),
        cost_estimate=cost(42),
        name="feed_forward_both",
    )(c, m, dz, wup, wdown, bup, vec)


def mlp_up_body(rows, c_ref, wup_ref, bup_ref, g_ref):
    for r in range(c_ref.shape[0] // rows):
        at = slice(r * rows, r * rows + rows)
        g_ref[at] = gelu_pair(dot(c_ref[at], wup_ref[...]) + bup_ref[...])[0].astype(BF16)


def mlp_up(c, wup, bup, after=(), chunk=1280, rows=256):
    n, width = c.shape
    ff = wup.shape[1]
    waits = len(after)
    return pl.pallas_call(
        lambda *refs: mlp_up_body(rows, *refs[:3], *refs[3 + waits:]),
        grid=(ff // chunk,),
        in_specs=[whole(c.shape), pl.BlockSpec((width, chunk), lambda i: (0, i)), pl.BlockSpec((1, chunk), lambda i: (0, i))] + tied(waits),
        out_specs=pl.BlockSpec((n, chunk), lambda i: (0, i)),
        out_shape=jax.ShapeDtypeStruct((n, ff), BF16),
        compiler_params=pltpu.CompilerParams(vmem_limit_bytes=VMEM_LIMIT),
        cost_estimate=cost(0.0125 * n),
        name="feed_forward_up",
    )(c, wup, bup, *after)


def mlp_down_body(g_ref, m_ref, wdown_ref, vec_ref, y_ref, acc_ref):
    step = pl.program_id(0)

    @pl.when(step == 0)
    def _():
        acc_ref[...] = m_ref[...] + vec_ref[7:8]

    acc_ref[...] += dot(g_ref[...], wdown_ref[...])

    @pl.when(step == pl.num_programs(0) - 1)
    def _():
        y_ref[...] = acc_ref[...].astype(BF16)


def mlp_down(g, m, wdown, vec, at, parts, after=(), chunk=1280):
    ff, width = wdown.shape
    rows = g.shape[0] // parts
    waits = len(after)
    return pl.pallas_call(
        lambda *refs: mlp_down_body(*refs[:4], *refs[4 + waits:]),
        grid=(ff // chunk,),
        in_specs=[pl.BlockSpec((rows, chunk), lambda i: (at, i)), pl.BlockSpec((rows, width), lambda i: (at, 0)),
                  pl.BlockSpec((chunk, width), lambda i: (i, 0)), whole(vec.shape)] + tied(waits),
        out_specs=whole((rows, width)),
        out_shape=jax.ShapeDtypeStruct((rows, width), BF16),
        scratch_shapes=[pltpu.VMEM((rows, width), F32)],
        compiler_params=pltpu.CompilerParams(vmem_limit_bytes=VMEM_LIMIT),
        cost_estimate=cost(0.017 * rows),
        name="feed_forward_down",
    )(g, m, wdown, vec, *after)


def mlp_bwd_body(save, rows, dz_ref, gp_ref, wup_ref, wdown_ref, dc_ref, *outs):
    @pl.when(pl.program_id(0) == 0)
    def _():
        dc_ref[...] = jnp.zeros_like(dc_ref)

    for r in range(dz_ref.shape[0] // rows):
        at = slice(r * rows, r * rows + rows)
        dg = dot(dz_ref[at], wdown_ref[...], ((1,), (1,)))
        du = (dg * gp_ref[at].astype(F32)).astype(BF16)
        if save:
            outs[0][at] = du
        dc_ref[at] += dot(du, wup_ref[...], ((1,), (1,)))


def mlp_bwd(dz, gp, wup, wdown, save, at=0, parts=1, earlier=(), after=(), chunk=1280, rows=256):
    n, width = dz.shape
    ff = wup.shape[1]
    args = [dz, gp, wup, wdown, *earlier, *after]
    outs = [jax.ShapeDtypeStruct((n * parts, width), F32)]
    specs = [pl.BlockSpec((n, width), lambda i: (at, 0))]
    if save:
        outs += [jax.ShapeDtypeStruct((n, ff), BF16)]
        specs += [pl.BlockSpec((n, chunk), lambda i: (0, i))]
    return pl.pallas_call(
        lambda *refs: mlp_bwd_body(save, rows, *refs[:4], *refs[len(args):]),
        grid=(ff // chunk,),
        in_specs=[whole(dz.shape), pl.BlockSpec((n, chunk), lambda i: (at, i)), pl.BlockSpec((width, chunk), lambda i: (0, i)),
                  pl.BlockSpec((chunk, width), lambda i: (i, 0))] + tied(len(args) - 4),
        out_specs=specs,
        out_shape=outs,
        input_output_aliases={4 + i: i for i in range(len(earlier))},
        compiler_params=pltpu.CompilerParams(vmem_limit_bytes=VMEM_LIMIT),
        cost_estimate=cost(22 / parts),
        name="feed_forward_back",
    )(*args)


def up_grad_body(c_ref, order_ref, du_ref, keep_ref, send_ref, sum_ref, ct_ref):
    half = keep_ref.shape[0]

    @pl.when(pl.program_id(0) == 0)
    def _():
        ct_ref[:2 * half] = dot(order_ref[...], c_ref[...], ((1,), (1,))).astype(BF16)
        ct_ref[2 * half:] = jnp.ones_like(ct_ref[2 * half:])

    grad = dot(ct_ref[...], du_ref[...])
    keep_ref[...] = grad[:half].astype(BF16)
    send_ref[...] = grad[half:2 * half].astype(BF16)
    sum_ref[...] = grad[2 * half:2 * half + 8]


def up_grad(c, order, du, at, parts, after=(), chunk=1280):
    n, width = c.shape
    ff = du.shape[1] // parts
    first = at * ff // chunk
    waits = len(after)
    column = lambda rows: pl.BlockSpec((rows, chunk), lambda i: (0, i))
    return pl.pallas_call(
        lambda *refs: up_grad_body(*refs[:3], *refs[3 + waits:]),
        grid=(ff // chunk,),
        in_specs=[whole(c.shape), whole(order.shape), pl.BlockSpec((n, chunk), lambda i: (0, i + first))] + tied(waits),
        out_specs=[column(width // 2), column(width // 2), column(8)],
        out_shape=[jax.ShapeDtypeStruct((width // 2, ff), BF16)] * 2 + [jax.ShapeDtypeStruct((8, ff), F32)],
        scratch_shapes=[pltpu.VMEM((width + 16, n), BF16)],
        compiler_params=pltpu.CompilerParams(vmem_limit_bytes=VMEM_LIMIT),
        cost_estimate=cost(13 / parts),
        name="up_gradient",
    )(c, order, du, *after)


def mlp_grad_body(rows, dz_ref, gp_ref, wup_ref, wdown_ref, early_ref, c_ref, order_ref, dc_ref, keep_ref, send_ref, sum_ref, du_ref, ct_ref):
    half = keep_ref.shape[0]
    count = early_ref.shape[0]

    @pl.when(pl.program_id(0) == 0)
    def _():
        dc_ref[...] = jnp.zeros_like(dc_ref)
        ct_ref[:2 * half] = dot(order_ref[...], c_ref[...], ((1,), (1,))).astype(BF16)
        ct_ref[2 * half:] = jnp.ones_like(ct_ref[2 * half:])

    for r in range(dz_ref.shape[0] // rows):
        at = slice(r * rows, r * rows + rows)
        dg = dot(dz_ref[at], wdown_ref[...], ((1,), (1,)))
        du = (dg * gp_ref[at].astype(F32)).astype(BF16)
        du_ref[at] = du
        dc_ref[at] += dot(du, wup_ref[...], ((1,), (1,)))
    grad = dot(ct_ref[:, :count], early_ref[...]) + dot(ct_ref[:, count:], du_ref[...])
    keep_ref[...] = grad[:half].astype(BF16)
    send_ref[...] = grad[half:2 * half].astype(BF16)
    sum_ref[...] = grad[2 * half:2 * half + 8]


def mlp_grad(dz, gp, wup, wdown, early, c, order, dc, after=(), chunk=1280, rows=256):
    count, width = dz.shape
    n, ff = gp.shape
    at = n // count - 1
    waits = 1 + len(after)
    column = lambda rows: pl.BlockSpec((rows, chunk), lambda i: (0, i))
    return pl.pallas_call(
        lambda *refs: mlp_grad_body(rows, *refs[:7], *refs[7 + waits:]),
        grid=(ff // chunk,),
        in_specs=[whole(dz.shape), pl.BlockSpec((count, chunk), lambda i: (at, i)), column(width), pl.BlockSpec((chunk, width), lambda i: (i, 0)),
                  column(n - count), whole(c.shape), whole(order.shape)] + tied(waits),
        out_specs=[pl.BlockSpec((count, width), lambda i: (at, 0)), column(width // 2), column(width // 2), column(8)],
        out_shape=[jax.ShapeDtypeStruct((n, width), F32)] + [jax.ShapeDtypeStruct((width // 2, ff), BF16)] * 2 + [jax.ShapeDtypeStruct((8, ff), F32)],
        scratch_shapes=[pltpu.VMEM((count, chunk), BF16), pltpu.VMEM((width + 16, n), BF16)],
        input_output_aliases={7: 0},
        compiler_params=pltpu.CompilerParams(vmem_limit_bytes=VMEM_LIMIT),
        cost_estimate=cost(21),
        name="feed_forward_gradients",
    )(dz, gp, wup, wdown, early, c, order, dc, *after)


def down_grad_body(g_ref, dz_ref, out_ref):
    out_ref[...] = dot(g_ref[...], dz_ref[...], ((0,), (0,))).astype(BF16)


def down_grad(g, dz, after=(), chunk=1280):
    n, ff = g.shape
    width = dz.shape[1]
    waits = len(after)
    return pl.pallas_call(
        lambda *refs: down_grad_body(*refs[:2], *refs[2 + waits:]),
        grid=(ff // chunk,),
        in_specs=[pl.BlockSpec((n, chunk), lambda i: (0, i)), whole(dz.shape)] + tied(waits),
        out_specs=pl.BlockSpec((chunk, width), lambda i: (i, 0)),
        out_shape=jax.ShapeDtypeStruct((ff, width), BF16),
        compiler_params=pltpu.CompilerParams(vmem_limit_bytes=VMEM_LIMIT),
        cost_estimate=cost(12),
        name="down_gradient",
    )(g, dz, *after)


def attn_bwd_body(grads, base_ref, dc_ref, dz_ref, m_ref, h_ref, qkv_ref, e_ref, o_ref, inv_ref, proj_ref, vec_ref, dh_ref, *outs):
    if grads:
        dr_ref, dqkv_ref, small_ref = outs
    width = h_ref.shape[2]
    vec = vec_ref[...]

    if grads:
        @pl.when(pl.program_id(0) == 0)
        def _():
            small_ref[...] = jnp.zeros_like(small_ref) if base_ref is None else base_ref[...]

    dz = dz_ref[0].astype(F32)
    back, g_gain1, g_shift1 = norm_back(m_ref[0], vec[1:2], dc_ref[0])
    dm = dz + back
    dr = dm.astype(BF16)
    if grads:
        dr_ref[0] = dr
    do_all = dot(dr, proj_ref[:, 3 * width:4 * width], ((1,), (1,))).astype(BF16)
    seq = h_ref.shape[1]
    head_of = lax.broadcasted_iota(jnp.int32, (1, 128), 1) // HEAD_DIM
    ones = jnp.ones((seq, 128), BF16)
    zero = jnp.zeros((seq, 128), BF16)
    dq_all, dk_all, dv_all = [], [], []
    for g in range(width // 128):
        at = slice(128 * g, 128 * g + 128)
        q = qkv_ref[0, :, 128 * g:128 * g + 128]
        k = qkv_ref[0, :, width + 128 * g:width + 128 * g + 128]
        v = jnp.concatenate([qkv_ref[0, :, 2 * width + 128 * g:2 * width + 128 * g + 128], ones], axis=1)
        scaled = do_all[:, at].astype(F32) * (inv_ref[0, :, at] * SCALE)
        do = scaled.astype(BF16)
        less = (-scaled * o_ref[0, :, at].astype(F32)).astype(BF16)
        do_t, q_t = do.T, q.T
        dq = None
        dk_t, dv_t = [], []
        stacked = dot(jnp.concatenate([jnp.concatenate([jnp.where(head_of == j, do, zero), jnp.where(head_of == j, less, zero)], axis=1)
                                       for j in range(GROUP)], axis=0), v, ((1,), (1,)))
        for j in range(GROUP):
            mine = head_of == j
            e = e_ref[0, GROUP * g + j]
            rows = slice(HEAD_DIM * j, HEAD_DIM * j + HEAD_DIM)
            dv_t.append(dot(do_t[rows], e))
            dp = stacked[seq * j:seq * j + seq]
            ds = (e.astype(F32) * dp).astype(BF16)
            part = dot(ds, jnp.where(mine, k, zero))
            dq = part if dq is None else dq + part
            dk_t.append(dot(q_t[rows], ds))
        dq_all.append(dq.astype(BF16))
        dk_all.append(jnp.concatenate(dk_t, axis=0).astype(BF16).T)
        dv_all.append((jnp.concatenate(dv_t, axis=0) * (1.0 / SCALE)).astype(BF16).T)
    dqkv = jnp.concatenate(dq_all + dk_all + dv_all, axis=1)
    if grads:
        dqkv_ref[0] = dqkv
    da = dot(dqkv, proj_ref[:, :3 * width], ((1,), (1,)))
    back, g_gain0, g_shift0 = norm_back(h_ref[0].astype(F32), vec[0:1], da)
    dh_ref[0] = (dm + back).astype(dh_ref.dtype)
    if not grads:
        return
    total = lambda x: jnp.sum(x.astype(F32), axis=0, keepdims=True)
    small_ref[...] += jnp.concatenate(
        [g_gain0, g_gain1, g_shift0, g_shift1, total(dqkv[:, :width]), total(dqkv[:, 2 * width:]), total(dr), total(dz)], axis=0)


def attn_bwd(dc, dz, m, h, qkv, e, o, inv, proj, vec, at, parts, grads, earlier=(), after=()):
    n, seq, width = h.shape
    count = n // parts
    row = lambda *tail: pl.BlockSpec((1,) + tail, lambda i: (i + at * count,) + (0,) * len(tail))
    if grads:
        shapes = [((seq, width), F32), ((seq, width), BF16), ((seq, 3 * width), BF16)]
        specs = [row(*s) for s, _ in shapes] + [whole((8, width))]
        results = [jax.ShapeDtypeStruct((n,) + s, d) for s, d in shapes] + [jax.ShapeDtypeStruct((8, width), F32)]
    else:
        specs = [pl.BlockSpec((1, seq, width), lambda i: (i, 0, 0))]
        results = [jax.ShapeDtypeStruct((count, seq, width), BF16)]
    args = [dc, dz, m, h, qkv, e, o, inv, proj, vec]
    in_specs = [row(seq, width), row(seq, width), row(seq, width), row(seq, width), row(seq, 3 * width), row(HEADS, seq, seq),
                row(seq, width), row(seq, width), whole(proj.shape), whole(vec.shape)]
    base = len(args)
    if earlier:
        args += [earlier[3], *earlier[:3]]
        in_specs += [whole(earlier[3].shape)] + tied(3)
    aliases = {base + 1 + i: i for i in range(3)} if earlier else {}
    args += after
    in_specs += tied(len(after))
    used = len(args)

    def body(*refs):
        attn_bwd_body(grads, refs[base] if earlier else None, *refs[:base], *refs[used:])

    return pl.pallas_call(
        body,
        grid=(count,),
        in_specs=in_specs,
        out_specs=specs,
        out_shape=results,
        input_output_aliases=aliases,
        compiler_params=pltpu.CompilerParams(vmem_limit_bytes=VMEM_LIMIT),
        cost_estimate=cost(7 * count),
        name="attention_back",
    )(*args)


def proj_grad_body(a_ref, dqkv_ref, o_ref, dr_ref, small_ref, bias_ref, order_ref, keep_ref, send_ref, at_ref):
    step = pl.program_id(0)
    width = a_ref.shape[1]
    half = width // 2
    order = order_ref[...]

    def put(at, value):
        keep_ref[:, at] = value[:half].astype(BF16)
        send_ref[:, at] = value[half:].astype(BF16)

    @pl.when(step == 0)
    def _():
        at_ref[...] = dot(order, a_ref[...], ((1,), (1,))).astype(BF16)
        put(slice(3 * width, 4 * width), dot(dot(order, o_ref[...], ((1,), (1,))).astype(BF16), dr_ref[...]))
        table = jnp.concatenate([small_ref[...], bias_ref[...], jnp.zeros((112, width), F32)], axis=0).astype(BF16)
        put(slice(4 * width, None), dot(order, table, ((1,), (1,))))

    put(pl.ds(pl.multiple_of(step * width, 128), width), dot(at_ref[...], dqkv_ref[...]))


def proj_grad(a, dqkv, o, dr, small, bias, order, after=()):
    n, width = a.shape
    waits = len(after)
    shape = (width // 2, 4 * width + 128)
    return pl.pallas_call(
        lambda *refs: proj_grad_body(*refs[:7], *refs[7 + waits:]),
        grid=(3,),
        in_specs=[whole(a.shape), pl.BlockSpec((n, width), lambda i: (0, i)), whole(o.shape), whole(dr.shape), whole(small.shape), whole(bias.shape),
                  whole(order.shape)] + tied(waits),
        out_specs=[whole(shape)] * 2,
        out_shape=[jax.ShapeDtypeStruct(shape, BF16)] * 2,
        scratch_shapes=[pltpu.VMEM((width, n), BF16)],
        compiler_params=pltpu.CompilerParams(vmem_limit_bytes=VMEM_LIMIT),
        cost_estimate=cost(9),
        name="projection_gradients",
    )(a, dqkv, o, dr, small, bias, order, *after)


def place_body(count, to_ref, *refs):
    pieces, out_ref, sems = refs[:count], refs[count], refs[count + 1]
    copies = [pltpu.make_async_copy(piece, out_ref.at[to_ref[i]], sems.at[i]) for i, piece in enumerate(pieces)]
    for copy in copies:
        copy.start()
    for copy in copies:
        copy.wait()


def place(pieces, to, after=()):
    rows, columns = pieces[0].shape
    count, waits = len(pieces), len(after)
    out = pl.pallas_call(
        lambda *refs: place_body(count, *refs[:count + 1], *refs[count + 1 + waits:]),
        in_specs=[pl.BlockSpec(memory_space=pltpu.SMEM)] + [pl.BlockSpec(memory_space=pl.ANY)] * count + tied(waits),
        out_specs=pl.BlockSpec(memory_space=pltpu.VMEM),
        out_shape=jax.ShapeDtypeStruct((count, rows, columns), BF16),
        scratch_shapes=[pltpu.SemaphoreType.DMA((count,))],
        compiler_params=pltpu.CompilerParams(vmem_limit_bytes=VMEM_LIMIT),
        cost_estimate=cost(4),
        name="place_pieces",
    )(to, *pieces, *after)
    return out.reshape(count * rows, columns)


def place_down_body(count, to_ref, g_ref, m_ref, vec_ref, *refs):
    pieces, (w_ref, y_ref), sems = refs[:count], refs[count:count + 2], refs[count + 2]
    rows = pieces[0].shape[0]
    copies = [pltpu.make_async_copy(piece, w_ref.at[pl.ds(pl.multiple_of(to_ref[i] * rows, rows), rows)], sems.at[i])
              for i, piece in enumerate(pieces)]
    for copy in copies:
        copy.start()
    for copy in copies:
        copy.wait()
    y_ref[...] = (m_ref[...] + vec_ref[7:8] + dot(g_ref[...], w_ref[...])).astype(BF16)


def place_down(pieces, to, g, m, vec, parts):
    rows, width = pieces[0].shape
    count = len(pieces)
    ff = count * rows
    n = g.shape[0] // parts
    return pl.pallas_call(
        lambda *refs: place_down_body(count, *refs),
        grid=(1,),
        in_specs=[pl.BlockSpec(memory_space=pltpu.SMEM), whole((n, ff)), whole((n, width)), whole(vec.shape)] + tied(count),
        out_specs=[whole((ff, width)), whole((n, width))],
        out_shape=[jax.ShapeDtypeStruct((ff, width), BF16), jax.ShapeDtypeStruct((n, width), BF16)],
        scratch_shapes=[pltpu.SemaphoreType.DMA((count,))],
        compiler_params=pltpu.CompilerParams(vmem_limit_bytes=VMEM_LIMIT),
        cost_estimate=cost(10),
        name="place_and_feed_forward_down",
    )(to, g, m, vec, *pieces)


def finish_body(rows, per_row, width, *refs):
    *terms, qkv_ref, out_ref, gain_ref, shift_ref, bias_ref, up_ref = refs
    total = terms[0][:rows].astype(F32)
    for term in terms[1:]:
        total = total + term[:rows].astype(F32)
    qkv_ref[0] = total[:, :3 * width]
    out_ref[0] = total[:, 3 * width:4 * width]
    small = total[:, 4 * width:]
    vectors = small.T
    gain_ref[0] = vectors[0:2]
    shift_ref[0] = vectors[2:4]
    bias_ref[0] = vectors[4:8]
    flat = rows * per_row
    spread = lax.broadcasted_iota(jnp.int32, (128, flat), 1) % per_row + 8 == lax.broadcasted_iota(jnp.int32, (128, flat), 0)
    wide = lax.dot_general(small, spread.astype(F32), (((1,), (0,)), ((), ())), precision=lax.Precision.HIGHEST, preferred_element_type=F32)
    here = lax.broadcasted_iota(jnp.int32, (rows, flat), 1) // per_row == lax.broadcasted_iota(jnp.int32, (rows, flat), 0)
    up_ref[...] = jnp.sum(jnp.where(here, wide, 0.0), axis=0, keepdims=True)


def finish(large, pieces, rows, per_row):
    columns = large[0].shape[1]
    width = (columns - 128) // 4
    shapes = [(1, rows, 3 * width), (1, rows, width), (1, 2, rows), (1, 2, rows), (1, 4, rows), (1, rows * per_row)]
    return pl.pallas_call(
        lambda *refs: finish_body(rows, per_row, width, *refs),
        grid=(1,),
        in_specs=[pl.BlockSpec((2 * rows, columns), lambda i: (0, 0))] * len(large) + [whole(piece.shape) for piece in pieces],
        out_specs=[whole(s) for s in shapes],
        out_shape=[jax.ShapeDtypeStruct(s, F32) for s in shapes],
        compiler_params=pltpu.CompilerParams(vmem_limit_bytes=VMEM_LIMIT),
        cost_estimate=cost(2),
        name="gather_projection_gradients",
    )(*large, *pieces)


def places(count):
    return count // 4, 2, 2


def hop(value, kind, step=1):
    zs, ys, cores = places(lax.axis_size("dp"))
    pairs = []
    for z in range(zs):
        for y in range(ys):
            for c in range(cores):
                to = {"core": (z, y, c ^ 1), "y": (z, y ^ 1, c), "z": ((z + step) % zs, y, c)}[kind]
                pairs.append(((z * ys + y) * cores + c, (to[0] * ys + to[1]) * cores + to[2]))
    return lax.ppermute(value, "dp", pairs)


def behind_me():
    zs, ys, cores = places(lax.axis_size("dp"))
    me = lax.axis_index("dp")
    return me // (cores * ys), (me // cores) % ys, me % cores


def along_line(shard):
    return [shard] + [hop(shard, "z", step) for step in range(1, places(lax.axis_size("dp"))[0])]


def both(mine, got):
    return (mine.astype(F32) + got.astype(F32)).astype(BF16)


def scatter_order(shard):
    zs, ys, cores = places(lax.axis_size("dp"))
    z, y, c = behind_me()
    row = jnp.arange(zs * ys * cores * shard)
    block = row // shard
    to = (((z + block % zs) % zs) * ys + (y ^ (block // zs % ys))) * cores + (c ^ (block // (zs * ys)))
    return (jnp.arange(zs * ys * cores * shard)[None, :] == (to * shard + row % shard)[:, None]).astype(BF16)


def y_step(mine, got):
    half = mine.shape[0] // 2
    return (mine[:half], got[:half]), hop(both(mine[half:], got[half:]), "y")


def z_step(mine, got):
    zs, _, _ = places(lax.axis_size("dp"))
    rows = got.shape[0] // zs
    terms = [[term[k * rows:k * rows + rows] for term in (*mine, got)] for k in range(zs)]
    return terms[0] + [hop(total(terms[k]).astype(BF16), "z", k) for k in range(1, zs)]


def total(terms):
    out = terms[0].astype(F32)
    for term in terms[1:]:
        out = out + term.astype(F32)
    return out


def held(value, *after):
    return lax.optimization_barrier((value, *after))[0]


def siblings(pieces, *after):
    return [hop(held(piece, *after), "core") for piece in pieces]


def places_of_pieces():
    zs, ys, cores = places(lax.axis_size("dp"))
    z, y, c = behind_me()
    to = []
    for core in (c, 1 - c):
        for row in (y, 1 - y):
            to += [(((z + zs - step) % zs) * ys + row) * cores + core for step in range(zs)]
    return jnp.stack(to).astype(jnp.int32)


def on_device(tokens, lengths, cotangent, w_qkv, w_out, w_up, w_down, norm_gain, norm_bias, bias_vec, up_bias):
    section = lax.axis_index("section")
    windows, seq, width = tokens.shape
    n = windows * seq
    shard = w_qkv.shape[1]
    per_row = up_bias.shape[1] // shard
    ff = w_up.shape[2]
    parts = 2
    part = windows // parts
    by_hand = lax.axis_size("dp") == 16
    table = jnp.concatenate([norm_gain[0], norm_bias[0], bias_vec[0]], axis=0).T
    table = jnp.concatenate([table, up_bias.reshape(shard, per_row)], axis=1)
    used = table.shape[1]
    table = jnp.pad(table, ((0, 0), (0, 128 - used)))
    packed = jnp.concatenate([w_qkv[0], w_out[0], table], axis=1)
    if by_hand:
        down = w_down[0]
        order, to = scatter_order(shard), places_of_pieces()
        wup = lax.all_gather(w_up[0], "dp", axis=0, tiled=True)
        proj_1, proj_3 = hop(packed, "z", 1), hop(packed, "z", 3)
        proj_y0, down_y0 = hop(packed, "y"), hop(down, "y")
        now = (proj_1, proj_3, proj_y0, order)
        proj_2 = hop(held(packed, *now), "z", 2)
        proj_y1, proj_y3 = hop(held(proj_1, *now), "y"), hop(held(proj_3, *now), "y")
        now = (proj_2, proj_y1, proj_y3, down_y0)
        down_1 = hop(held(down, *now), "z", 1)
        proj_y2 = hop(held(proj_2, *now), "y")
        now = (down_1, proj_y2)
        pieces = [packed, proj_1, proj_2, proj_3, proj_y0, proj_y1, proj_y2, proj_y3]
        proj = place(pieces + siblings(pieces, proj_y2), to)
        down_2, down_3 = hop(held(down, *now), "z", 2), hop(held(down, *now), "z", 3)
        down_y1 = hop(held(down_1, *now), "y")
    else:
        order = (jnp.arange(width)[None, :] == jnp.arange(width)[:, None]).astype(BF16)
        proj = lax.all_gather(packed, "dp", axis=0, tiled=True)
        wup = lax.all_gather(w_up[0], "dp", axis=0, tiled=True)
        wdown = lax.all_gather(w_down[0], "dp", axis=0, tiled=True)
    small = proj[:, 4 * width:4 * width + used]
    vec = small[:, :8].T.astype(F32)
    bup = small[:, 8:].reshape(1, ff).astype(F32)

    mid, c = attn_fwd(tokens, lengths, proj, False)
    c = c.reshape(n, width)
    mid = mid.reshape(n, width)
    if by_hand:
        now = (down_2, down_3, down_y1, c)
        down_y2, down_y3 = hop(held(down_2, *now), "y"), hop(held(down_3, *now), "y")
    act = mlp_up(c, wup, bup)
    if by_hand:
        pieces = [down, down_1, down_2, down_3, down_y0, down_y1, down_y2, down_y3]
        wdown, y_a = place_down(pieces + siblings(pieces, act), to, act, mid, vec, parts)
    else:
        y_a = mlp_down(act, mid, wdown, vec, 0, parts)
    y_b = mlp_down(act, mid, wdown, vec, 1, parts)
    kept = ()
    arrived = [lax.ppermute(y.reshape(part, seq, width), "section", [(0, 1)]) for y in (y_a, y_b)]
    lengths = jnp.append(lengths, section)
    for at in range(parts):
        kept = attn_fwd(tokens, lengths, proj, True, at, parts, held(arrived[at], *kept[:1]), vec, kept)
    m, c, qkv, e, o, a, inv, h = kept
    c = c.reshape(n, width)
    y, g, gp, dc = mlp_both(c, m.reshape(n, width), cotangent.reshape(n, width), wup, wdown, bup, vec)
    dc = dc.reshape(tokens.shape)
    arrived = []
    for at in range(parts):
        back, = attn_bwd(dc, cotangent, m, h, qkv, e, o, inv, proj, vec, at, parts, False)
        arrived.append(lax.ppermute(back, "section", [(1, 0)]))
    dz = [jnp.where(section == 1, cotangent[:part], arrived[0])]
    dc, du = mlp_bwd(dz[0].reshape(part * seq, width), gp, wup, wdown, True, 0, parts)
    dz.append(jnp.where(section == 1, cotangent[part:], held(arrived[1], dc)))
    last = dz[1].reshape(part * seq, width)
    dz = jnp.concatenate(dz)
    g_down = down_grad(g, dz.reshape(n, width))
    sum_down = lax.psum_scatter(g_down, "dp", scatter_dimension=0, tiled=True).astype(F32)
    dc, keep_u, send_u, bup_u = mlp_grad(last, gp, wup, wdown, du, c, order, dc, (g_down,))
    dc = dc.reshape(tokens.shape)
    if by_hand:
        got_u = hop(send_u, "core")
        half = ff // 2
        rest = keep_u.shape[0] // 2
        mine_a, mine_b = [(keep_u[:rest, at], got_u[:rest, at]) for at in (slice(0, half), slice(half, ff))]
        send_a = both(keep_u[rest:, :half], got_u[rest:, :half])
        got_a = hop(send_a, "y")
        send_b = both(held(keep_u, send_a)[rest:, half:], held(got_u, send_a)[rest:, half:])
        got_b = hop(send_b, "y")
        back = attn_bwd(dc, dz, m, h, qkv, e, o, inv, proj, vec, 0, 1, True, (), (got_u,))
        terms_a = z_step(mine_a, held(got_a, back[3]))
        wait = (got_a,)
    else:
        back = attn_bwd(dc, dz, m, h, qkv, e, o, inv, proj, vec, 0, 1, True)
        wait = ()
    dh, dr, dqkv, smalls = back
    g_bup = bup_u[0].reshape(width, per_row).T
    keep_p, send_p = proj_grad(
        a.reshape(n, width), dqkv.reshape(n, 3 * width), o.reshape(n, width), dr.reshape(n, width), smalls, g_bup, order, wait)
    if by_hand:
        terms_b = z_step(mine_b, got_b)
        sum_up = jnp.concatenate([total(terms_a), total(terms_b)], axis=1)
        core_p = hop(held(send_p, got_b, *terms_a[3:]), "core")
        mine_p, got_p = y_step(keep_p, core_p)
        pieces = z_step(mine_p, held(got_p, *terms_b))[3:]
        rest = finish((keep_p, core_p, got_p), pieces, shard, per_row)
    else:
        scatter = lambda *halves: lax.psum_scatter(jnp.concatenate(halves), "dp", scatter_dimension=0, tiled=True).astype(F32)
        sum_up = scatter(keep_u, send_u)
        sum_proj = scatter(keep_p, send_p)
        vectors = sum_proj[:, 4 * width:4 * width + 8].T
        rest = (
            sum_proj[None, :, :3 * width],
            sum_proj[None, :, 3 * width:4 * width],
            vectors[None, 0:2],
            vectors[None, 2:4],
            vectors[None, 4:8],
            sum_proj[:, 4 * width + 8:4 * width + used].reshape(1, -1),
        )
    return (y.reshape((1,) + tokens.shape), dh[None], rest[0], rest[1], sum_up[None], sum_down[None], *rest[2:])


def solution(mesh):
    sharded = [P("section", "dp", None)] * 4 + [P("section", None, "dp")] * 3 + [P("section", "dp")]
    windows = P("dp", None, None)
    out = P("section", "dp", None, None)
    return jax.shard_map(
        on_device, mesh=mesh, in_specs=(windows, P("dp"), windows, *sharded), out_specs=(out, out, *sharded), check_vma=False
    )
```

```python
import jax
import jax.numpy as jnp
from jax import lax
from jax.experimental import pallas as pl
from jax.experimental.pallas import tpu as pltpu
from jax.sharding import PartitionSpec as P

HEADS = 20
HEAD_DIM = 32
GROUP = 128 // HEAD_DIM
SCALE = HEAD_DIM ** -0.5
LOG2E = 1.4426950408889634
VMEM_LIMIT = 56 * 1024 * 1024
F32 = jnp.float32
BF16 = jnp.bfloat16


def cost(us):
    return pl.CostEstimate(flops=int(us * 1.1e9), bytes_accessed=1024, transcendentals=0)


def tied(count):
    return [pl.BlockSpec(memory_space=pl.ANY)] * count


def dot(a, b, dims=((1,), (0,))):
    return lax.dot_general(a, b, (dims, ((), ())), preferred_element_type=F32)


def gelu_pair(u):
    below = 0.5 + 0.5 * lax.erf(u * 0.7071067811865476)
    return u * below, below + (0.3989422804014327 * u) * jnp.exp(-0.5 * (u * u))


def normed(v, gain, shift):
    centered = v - jnp.mean(v, axis=-1, keepdims=True)
    spread = jnp.mean(centered * centered, axis=-1, keepdims=True)
    hat = centered * lax.rsqrt(spread + 1e-05)
    return hat * gain + shift


def norm_back(v, gain, grad):
    centered = v - jnp.mean(v, axis=-1, keepdims=True)
    spread = jnp.mean(centered * centered, axis=-1, keepdims=True)
    inv = lax.rsqrt(spread + 1e-05)
    hat = centered * inv
    g = grad * gain
    back = inv * (g - jnp.mean(g, axis=-1, keepdims=True) - hat * jnp.mean(g * hat, axis=-1, keepdims=True))
    return back, jnp.sum(grad * hat, axis=0, keepdims=True), jnp.sum(grad, axis=0, keepdims=True)


def attn_fwd_body(save, first_window, len_ref, h_ref, *rest):
    if save:
        arrived_ref, wqkv_ref, vec_ref, m_ref, c_ref, qkv_ref, e_ref, o_ref, a_ref, inv_ref, taken_ref = rest
    else:
        wqkv_ref, m_ref, c_ref = rest
    width = h_ref.shape[2]
    seq = h_ref.shape[1]
    length = len_ref[pl.program_id(0) + first_window]
    if save:
        taken = jnp.where(len_ref[len_ref.shape[0] - 1] == 0, h_ref[0], arrived_ref[0])
        taken_ref[0] = taken
        h = taken.astype(F32)
        vec = vec_ref[...]
    else:
        h = h_ref[0].astype(F32)
        vec = wqkv_ref[:, 4 * width:].astype(F32).T
    a = normed(h, vec[0:1], vec[2:3]).astype(BF16)
    q_all = (dot(a, wqkv_ref[:, :width]) + vec[4:5]).astype(BF16)
    k_all = dot(a, wqkv_ref[:, width:2 * width]).astype(BF16)
    v_all = (dot(a, wqkv_ref[:, 2 * width:3 * width]) + vec[5:6]).astype(BF16)
    if save:
        a_ref[0] = a
        qkv_ref[0, :, :width] = q_all
        qkv_ref[0, :, width:2 * width] = k_all
        qkv_ref[0, :, 2 * width:] = v_all
    head_of = lax.broadcasted_iota(jnp.int32, (1, 128), 1) // HEAD_DIM
    key_at = lax.broadcasted_iota(jnp.int32, (seq, 128), 0)
    lane = lax.broadcasted_iota(jnp.int32, (seq, 128), 1)
    past = jnp.where((lane == 0) & (key_at >= length), -1e30, 0.0).astype(BF16)
    first = jnp.where(lane == 0, 1.0, 0.0).astype(BF16)
    ones = jnp.ones((seq, 128), BF16)
    zero = jnp.zeros((seq, 128), BF16)
    mixed = []
    for g in range(width // 128):
        at = slice(128 * g, 128 * g + 128)
        q, v = q_all[:, at], v_all[:, at]
        k = jnp.concatenate([k_all[:, at], past], axis=1)
        acc, inv = None, None
        stacked = dot(jnp.concatenate([jnp.concatenate([jnp.where(head_of == j, q, zero), first], axis=1) for j in range(GROUP)], axis=0), k, ((1,), (1,)))
        for j in range(GROUP):
            mine = head_of == j
            s = stacked[seq * j:seq * j + seq]
            e = jnp.exp2((s - jnp.max(s, axis=1, keepdims=True)) * (SCALE * LOG2E)).astype(BF16)
            if save:
                e_ref[0, GROUP * g + j] = e
            both_parts = dot(e, jnp.concatenate([jnp.where(mine, v, zero), ones], axis=1))
            one_over = 1.0 / both_parts[:, 128:]
            part = both_parts[:, :128] * one_over
            acc = part if acc is None else acc + part
            inv = one_over if inv is None else jnp.where(mine, one_over, inv)
        mixed.append(acc.astype(BF16))
        if save:
            inv_ref[0, :, at] = inv
    o = jnp.concatenate(mixed, axis=1)
    if save:
        o_ref[0] = o
    m = h + dot(o, wqkv_ref[:, 3 * width:4 * width]) + vec[6:7]
    m_ref[0] = m
    c_ref[0] = normed(m, vec[1:2], vec[3:4]).astype(BF16)


def whole(shape):
    return pl.BlockSpec(shape, lambda *_: (0,) * len(shape))


def attn_fwd(h, lengths, proj, save, at=0, parts=1, arrived=None, vec=None, earlier=(), after=()):
    n, seq, width = h.shape
    count = n // parts
    row = lambda *tail: pl.BlockSpec((1,) + tail, lambda i, *_: (i + at * count,) + (0,) * len(tail))
    shapes = [((seq, width), F32), ((seq, width), BF16)]
    args, in_specs = [h], [row(seq, width)]
    if save:
        shapes += [((seq, 3 * width), BF16), ((HEADS, seq, seq), BF16), ((seq, width), BF16), ((seq, width), BF16), ((seq, width), F32), ((seq, width), BF16)]
        args += [arrived, proj, vec]
        in_specs += [pl.BlockSpec((1, seq, width), lambda i, *_: (i, 0, 0)), whole(proj.shape), whole(vec.shape)]
    else:
        args += [proj]
        in_specs += [whole(proj.shape)]
    used, waits = 1 + len(args), len(earlier) + len(after)
    return pl.pallas_call(
        lambda *refs: attn_fwd_body(save, at * count, *refs[:used], *refs[used + waits:]),
        grid_spec=pltpu.PrefetchScalarGridSpec(
            num_scalar_prefetch=1,
            grid=(count,),
            in_specs=in_specs + tied(waits),
            out_specs=[row(*s) for s, _ in shapes],
        ),
        out_shape=[jax.ShapeDtypeStruct((n,) + s, d) for s, d in shapes],
        input_output_aliases={used + i: i for i in range(len(earlier))},
        compiler_params=pltpu.CompilerParams(vmem_limit_bytes=VMEM_LIMIT),
        cost_estimate=cost(4.5 * count),
        name="attention_forward",
    )(lengths, *args, *earlier, *after)


def mlp_fwd_body(save, rows, c_ref, m_ref, wup_ref, wdown_ref, bup_ref, vec_ref, *outs):
    if save:
        y_ref, g_ref, gp_ref, acc_ref = outs
    else:
        y_ref, acc_ref = outs
    step = pl.program_id(0)

    @pl.when(step == 0)
    def _():
        acc_ref[...] = m_ref[...] + vec_ref[7:8]

    for r in range(c_ref.shape[0] // rows):
        at = slice(r * rows, r * rows + rows)
        u = dot(c_ref[at], wup_ref[...]) + bup_ref[...]
        act, slope = gelu_pair(u)
        act = act.astype(BF16)
        if save:
            g_ref[at] = act
            gp_ref[at] = slope.astype(BF16)
        acc_ref[at] += dot(act, wdown_ref[...])

    @pl.when(step == pl.num_programs(0) - 1)
    def _():
        y_ref[...] = acc_ref[...].astype(BF16)


def mlp_fwd(c, m, wup, wdown, bup, vec, save, chunk=1280, rows=256):
    n, width = c.shape
    ff = wup.shape[1]
    outs = [jax.ShapeDtypeStruct((n, width), BF16)]
    specs = [whole((n, width))]
    if save:
        outs += [jax.ShapeDtypeStruct((n, ff), BF16)] * 2
        specs += [pl.BlockSpec((n, chunk), lambda i: (0, i))] * 2
    return pl.pallas_call(
        lambda *refs: mlp_fwd_body(save, rows, *refs),
        grid=(ff // chunk,),
        in_specs=[whole(c.shape), whole(m.shape), pl.BlockSpec((width, chunk), lambda i: (0, i)),
                  pl.BlockSpec((chunk, width), lambda i: (i, 0)), pl.BlockSpec((1, chunk), lambda i: (0, i)), whole(vec.shape)],
        out_specs=specs,
        out_shape=outs,
        scratch_shapes=[pltpu.VMEM((n, width), F32)],
        compiler_params=pltpu.CompilerParams(vmem_limit_bytes=VMEM_LIMIT),
        cost_estimate=cost(26),
        name="feed_forward",
    )(c, m, wup, wdown, bup, vec)


def mlp_both_body(rows, c_ref, m_ref, dz_ref, wup_ref, wdown_ref, bup_ref, vec_ref, y_ref, g_ref, gp_ref, dc_ref, acc_ref):
    step = pl.program_id(0)

    @pl.when(step == 0)
    def _():
        acc_ref[...] = m_ref[...] + vec_ref[7:8]
        dc_ref[...] = jnp.zeros_like(dc_ref)

    for r in range(c_ref.shape[0] // rows):
        at = slice(r * rows, r * rows + rows)
        u = dot(c_ref[at], wup_ref[...]) + bup_ref[...]
        dg = dot(dz_ref[at], wdown_ref[...], ((1,), (1,)))
        act, slope = gelu_pair(u)
        act, slope = act.astype(BF16), slope.astype(BF16)
        g_ref[at] = act
        gp_ref[at] = slope
        acc_ref[at] += dot(act, wdown_ref[...])
        dc_ref[at] += dot((dg * slope.astype(F32)).astype(BF16), wup_ref[...], ((1,), (1,)))

    @pl.when(step == pl.num_programs(0) - 1)
    def _():
        y_ref[...] = acc_ref[...].astype(BF16)


def mlp_both(c, m, dz, wup, wdown, bup, vec, chunk=1280, rows=256):
    n, width = c.shape
    ff = wup.shape[1]
    column = pl.BlockSpec((n, chunk), lambda i: (0, i))
    return pl.pallas_call(
        lambda *refs: mlp_both_body(rows, *refs),
        grid=(ff // chunk,),
        in_specs=[whole(c.shape), whole(m.shape), whole(dz.shape), pl.BlockSpec((width, chunk), lambda i: (0, i)),
                  pl.BlockSpec((chunk, width), lambda i: (i, 0)), pl.BlockSpec((1, chunk), lambda i: (0, i)), whole(vec.shape)],
        out_specs=[whole((n, width)), column, column, whole((n, width))],
        out_shape=[jax.ShapeDtypeStruct((n, width), BF16), jax.ShapeDtypeStruct((n, ff), BF16), jax.ShapeDtypeStruct((n, ff), BF16),
                   jax.ShapeDtypeStruct((n, width), F32)],
        scratch_shapes=[pltpu.VMEM((n, width), F32)],
        compiler_params=pltpu.CompilerParams(vmem_limit_bytes=VMEM_LIMIT),
        cost_estimate=cost(42),
        name="feed_forward_both",
    )(c, m, dz, wup, wdown, bup, vec)


def mlp_up_body(rows, c_ref, wup_ref, bup_ref, g_ref):
    for r in range(c_ref.shape[0] // rows):
        at = slice(r * rows, r * rows + rows)
        g_ref[at] = gelu_pair(dot(c_ref[at], wup_ref[...]) + bup_ref[...])[0].astype(BF16)


def mlp_up(c, wup, bup, after=(), chunk=1280, rows=256):
    n, width = c.shape
    ff = wup.shape[1]
    waits = len(after)
    return pl.pallas_call(
        lambda *refs: mlp_up_body(rows, *refs[:3], *refs[3 + waits:]),
        grid=(ff // chunk,),
        in_specs=[whole(c.shape), pl.BlockSpec((width, chunk), lambda i: (0, i)), pl.BlockSpec((1, chunk), lambda i: (0, i))] + tied(waits),
        out_specs=pl.BlockSpec((n, chunk), lambda i: (0, i)),
        out_shape=jax.ShapeDtypeStruct((n, ff), BF16),
        compiler_params=pltpu.CompilerParams(vmem_limit_bytes=VMEM_LIMIT),
        cost_estimate=cost(0.0125 * n),
        name="feed_forward_up",
    )(c, wup, bup, *after)


def mlp_down_body(g_ref, m_ref, wdown_ref, vec_ref, y_ref, acc_ref):
    step = pl.program_id(0)

    @pl.when(step == 0)
    def _():
        acc_ref[...] = m_ref[...] + vec_ref[7:8]

    acc_ref[...] += dot(g_ref[...], wdown_ref[...])

    @pl.when(step == pl.num_programs(0) - 1)
    def _():
        y_ref[...] = acc_ref[...].astype(BF16)


def mlp_down(g, m, wdown, vec, at, parts, after=(), chunk=1280):
    ff, width = wdown.shape
    rows = g.shape[0] // parts
    waits = len(after)
    return pl.pallas_call(
        lambda *refs: mlp_down_body(*refs[:4], *refs[4 + waits:]),
        grid=(ff // chunk,),
        in_specs=[pl.BlockSpec((rows, chunk), lambda i: (at, i)), pl.BlockSpec((rows, width), lambda i: (at, 0)),
                  pl.BlockSpec((chunk, width), lambda i: (i, 0)), whole(vec.shape)] + tied(waits),
        out_specs=whole((rows, width)),
        out_shape=jax.ShapeDtypeStruct((rows, width), BF16),
        scratch_shapes=[pltpu.VMEM((rows, width), F32)],
        compiler_params=pltpu.CompilerParams(vmem_limit_bytes=VMEM_LIMIT),
        cost_estimate=cost(0.017 * rows),
        name="feed_forward_down",
    )(g, m, wdown, vec, *after)


def mlp_bwd_body(save, rows, dz_ref, gp_ref, wup_ref, wdown_ref, dc_ref, *outs):
    @pl.when(pl.program_id(0) == 0)
    def _():
        dc_ref[...] = jnp.zeros_like(dc_ref)

    for r in range(dz_ref.shape[0] // rows):
        at = slice(r * rows, r * rows + rows)
        dg = dot(dz_ref[at], wdown_ref[...], ((1,), (1,)))
        du = (dg * gp_ref[at].astype(F32)).astype(BF16)
        if save:
            outs[0][at] = du
        dc_ref[at] += dot(du, wup_ref[...], ((1,), (1,)))


def mlp_bwd(dz, gp, wup, wdown, save, at=0, parts=1, earlier=(), after=(), chunk=1280, rows=256):
    n, width = dz.shape
    ff = wup.shape[1]
    args = [dz, gp, wup, wdown, *earlier, *after]
    outs = [jax.ShapeDtypeStruct((n * parts, width), F32)]
    specs = [pl.BlockSpec((n, width), lambda i: (at, 0))]
    if save:
        outs += [jax.ShapeDtypeStruct((n, ff), BF16)]
        specs += [pl.BlockSpec((n, chunk), lambda i: (0, i))]
    return pl.pallas_call(
        lambda *refs: mlp_bwd_body(save, rows, *refs[:4], *refs[len(args):]),
        grid=(ff // chunk,),
        in_specs=[whole(dz.shape), pl.BlockSpec((n, chunk), lambda i: (at, i)), pl.BlockSpec((width, chunk), lambda i: (0, i)),
                  pl.BlockSpec((chunk, width), lambda i: (i, 0))] + tied(len(args) - 4),
        out_specs=specs,
        out_shape=outs,
        input_output_aliases={4 + i: i for i in range(len(earlier))},
        compiler_params=pltpu.CompilerParams(vmem_limit_bytes=VMEM_LIMIT),
        cost_estimate=cost(22 / parts),
        name="feed_forward_back",
    )(*args)


def up_grad_body(c_ref, order_ref, du_ref, keep_ref, send_ref, sum_ref, ct_ref):
    half = keep_ref.shape[0]

    @pl.when(pl.program_id(0) == 0)
    def _():
        ct_ref[:2 * half] = dot(order_ref[...], c_ref[...], ((1,), (1,))).astype(BF16)
        ct_ref[2 * half:] = jnp.ones_like(ct_ref[2 * half:])

    grad = dot(ct_ref[...], du_ref[...])
    keep_ref[...] = grad[:half].astype(BF16)
    send_ref[...] = grad[half:2 * half].astype(BF16)
    sum_ref[...] = grad[2 * half:2 * half + 8]


def up_grad(c, order, du, at, parts, after=(), chunk=1280):
    n, width = c.shape
    ff = du.shape[1] // parts
    first = at * ff // chunk
    waits = len(after)
    column = lambda rows: pl.BlockSpec((rows, chunk), lambda i: (0, i))
    return pl.pallas_call(
        lambda *refs: up_grad_body(*refs[:3], *refs[3 + waits:]),
        grid=(ff // chunk,),
        in_specs=[whole(c.shape), whole(order.shape), pl.BlockSpec((n, chunk), lambda i: (0, i + first))] + tied(waits),
        out_specs=[column(width // 2), column(width // 2), column(8)],
        out_shape=[jax.ShapeDtypeStruct((width // 2, ff), BF16)] * 2 + [jax.ShapeDtypeStruct((8, ff), F32)],
        scratch_shapes=[pltpu.VMEM((width + 16, n), BF16)],
        compiler_params=pltpu.CompilerParams(vmem_limit_bytes=VMEM_LIMIT),
        cost_estimate=cost(13 / parts),
        name="up_gradient",
    )(c, order, du, *after)


def mlp_grad_body(rows, dz_ref, gp_ref, wup_ref, wdown_ref, early_ref, c_ref, order_ref, dc_ref, keep_ref, send_ref, sum_ref, du_ref, ct_ref):
    half = keep_ref.shape[0]
    count = early_ref.shape[0]

    @pl.when(pl.program_id(0) == 0)
    def _():
        dc_ref[...] = jnp.zeros_like(dc_ref)
        ct_ref[:2 * half] = dot(order_ref[...], c_ref[...], ((1,), (1,))).astype(BF16)
        ct_ref[2 * half:] = jnp.ones_like(ct_ref[2 * half:])

    for r in range(dz_ref.shape[0] // rows):
        at = slice(r * rows, r * rows + rows)
        dg = dot(dz_ref[at], wdown_ref[...], ((1,), (1,)))
        du = (dg * gp_ref[at].astype(F32)).astype(BF16)
        du_ref[at] = du
        dc_ref[at] += dot(du, wup_ref[...], ((1,), (1,)))
    grad = dot(ct_ref[:, :count], early_ref[...]) + dot(ct_ref[:, count:], du_ref[...])
    keep_ref[...] = grad[:half].astype(BF16)
    send_ref[...] = grad[half:2 * half].astype(BF16)
    sum_ref[...] = grad[2 * half:2 * half + 8]


def mlp_grad(dz, gp, wup, wdown, early, c, order, dc, after=(), chunk=1280, rows=256):
    count, width = dz.shape
    n, ff = gp.shape
    at = n // count - 1
    waits = 1 + len(after)
    column = lambda rows: pl.BlockSpec((rows, chunk), lambda i: (0, i))
    return pl.pallas_call(
        lambda *refs: mlp_grad_body(rows, *refs[:7], *refs[7 + waits:]),
        grid=(ff // chunk,),
        in_specs=[whole(dz.shape), pl.BlockSpec((count, chunk), lambda i: (at, i)), column(width), pl.BlockSpec((chunk, width), lambda i: (i, 0)),
                  column(n - count), whole(c.shape), whole(order.shape)] + tied(waits),
        out_specs=[pl.BlockSpec((count, width), lambda i: (at, 0)), column(width // 2), column(width // 2), column(8)],
        out_shape=[jax.ShapeDtypeStruct((n, width), F32)] + [jax.ShapeDtypeStruct((width // 2, ff), BF16)] * 2 + [jax.ShapeDtypeStruct((8, ff), F32)],
        scratch_shapes=[pltpu.VMEM((count, chunk), BF16), pltpu.VMEM((width + 16, n), BF16)],
        input_output_aliases={7: 0},
        compiler_params=pltpu.CompilerParams(vmem_limit_bytes=VMEM_LIMIT),
        cost_estimate=cost(21),
        name="feed_forward_gradients",
    )(dz, gp, wup, wdown, early, c, order, dc, *after)


def down_grad_body(g_ref, dz_ref, out_ref):
    out_ref[...] = dot(g_ref[...], dz_ref[...], ((0,), (0,))).astype(BF16)


def down_grad(g, dz, after=(), chunk=1280):
    n, ff = g.shape
    width = dz.shape[1]
    waits = len(after)
    return pl.pallas_call(
        lambda *refs: down_grad_body(*refs[:2], *refs[2 + waits:]),
        grid=(ff // chunk,),
        in_specs=[pl.BlockSpec((n, chunk), lambda i: (0, i)), whole(dz.shape)] + tied(waits),
        out_specs=pl.BlockSpec((chunk, width), lambda i: (i, 0)),
        out_shape=jax.ShapeDtypeStruct((ff, width), BF16),
        compiler_params=pltpu.CompilerParams(vmem_limit_bytes=VMEM_LIMIT),
        cost_estimate=cost(12),
        name="down_gradient",
    )(g, dz, *after)


def attn_bwd_body(grads, base_ref, dc_ref, dz_ref, m_ref, h_ref, qkv_ref, e_ref, o_ref, inv_ref, proj_ref, vec_ref, dh_ref, *outs):
    if grads:
        dr_ref, dqkv_ref, small_ref = outs
    width = h_ref.shape[2]
    vec = vec_ref[...]

    if grads:
        @pl.when(pl.program_id(0) == 0)
        def _():
            small_ref[...] = jnp.zeros_like(small_ref) if base_ref is None else base_ref[...]

    dz = dz_ref[0].astype(F32)
    back, g_gain1, g_shift1 = norm_back(m_ref[0], vec[1:2], dc_ref[0])
    dm = dz + back
    dr = dm.astype(BF16)
    if grads:
        dr_ref[0] = dr
    do_all = dot(dr, proj_ref[:, 3 * width:4 * width], ((1,), (1,))).astype(BF16)
    seq = h_ref.shape[1]
    head_of = lax.broadcasted_iota(jnp.int32, (1, 128), 1) // HEAD_DIM
    ones = jnp.ones((seq, 128), BF16)
    zero = jnp.zeros((seq, 128), BF16)
    dq_all, dk_all, dv_all = [], [], []
    for g in range(width // 128):
        at = slice(128 * g, 128 * g + 128)
        q = qkv_ref[0, :, 128 * g:128 * g + 128]
        k = qkv_ref[0, :, width + 128 * g:width + 128 * g + 128]
        v = jnp.concatenate([qkv_ref[0, :, 2 * width + 128 * g:2 * width + 128 * g + 128], ones], axis=1)
        scaled = do_all[:, at].astype(F32) * (inv_ref[0, :, at] * SCALE)
        do = scaled.astype(BF16)
        less = (-scaled * o_ref[0, :, at].astype(F32)).astype(BF16)
        do_t, q_t = do.T, q.T
        dq = None
        dk_t, dv_t = [], []
        stacked = dot(jnp.concatenate([jnp.concatenate([jnp.where(head_of == j, do, zero), jnp.where(head_of == j, less, zero)], axis=1)
                                       for j in range(GROUP)], axis=0), v, ((1,), (1,)))
        for j in range(GROUP):
            mine = head_of == j
            e = e_ref[0, GROUP * g + j]
            rows = slice(HEAD_DIM * j, HEAD_DIM * j + HEAD_DIM)
            dv_t.append(dot(do_t[rows], e))
            dp = stacked[seq * j:seq * j + seq]
            ds = (e.astype(F32) * dp).astype(BF16)
            part = dot(ds, jnp.where(mine, k, zero))
            dq = part if dq is None else dq + part
            dk_t.append(dot(q_t[rows], ds))
        dq_all.append(dq.astype(BF16))
        dk_all.append(jnp.concatenate(dk_t, axis=0).astype(BF16).T)
        dv_all.append((jnp.concatenate(dv_t, axis=0) * (1.0 / SCALE)).astype(BF16).T)
    dqkv = jnp.concatenate(dq_all + dk_all + dv_all, axis=1)
    if grads:
        dqkv_ref[0] = dqkv
    da = dot(dqkv, proj_ref[:, :3 * width], ((1,), (1,)))
    back, g_gain0, g_shift0 = norm_back(h_ref[0].astype(F32), vec[0:1], da)
    dh_ref[0] = (dm + back).astype(dh_ref.dtype)
    if not grads:
        return
    total = lambda x: jnp.sum(x.astype(F32), axis=0, keepdims=True)
    small_ref[...] += jnp.concatenate(
        [g_gain0, g_gain1, g_shift0, g_shift1, total(dqkv[:, :width]), total(dqkv[:, 2 * width:]), total(dr), total(dz)], axis=0)


def attn_bwd(dc, dz, m, h, qkv, e, o, inv, proj, vec, at, parts, grads, earlier=(), after=()):
    n, seq, width = h.shape
    count = n // parts
    row = lambda *tail: pl.BlockSpec((1,) + tail, lambda i: (i + at * count,) + (0,) * len(tail))
    if grads:
        shapes = [((seq, width), F32), ((seq, width), BF16), ((seq, 3 * width), BF16)]
        specs = [row(*s) for s, _ in shapes] + [whole((8, width))]
        results = [jax.ShapeDtypeStruct((n,) + s, d) for s, d in shapes] + [jax.ShapeDtypeStruct((8, width), F32)]
    else:
        specs = [pl.BlockSpec((1, seq, width), lambda i: (i, 0, 0))]
        results = [jax.ShapeDtypeStruct((count, seq, width), BF16)]
    args = [dc, dz, m, h, qkv, e, o, inv, proj, vec]
    in_specs = [row(seq, width), row(seq, width), row(seq, width), row(seq, width), row(seq, 3 * width), row(HEADS, seq, seq),
                row(seq, width), row(seq, width), whole(proj.shape), whole(vec.shape)]
    base = len(args)
    if earlier:
        args += [earlier[3], *earlier[:3]]
        in_specs += [whole(earlier[3].shape)] + tied(3)
    aliases = {base + 1 + i: i for i in range(3)} if earlier else {}
    args += after
    in_specs += tied(len(after))
    used = len(args)

    def body(*refs):
        attn_bwd_body(grads, refs[base] if earlier else None, *refs[:base], *refs[used:])

    return pl.pallas_call(
        body,
        grid=(count,),
        in_specs=in_specs,
        out_specs=specs,
        out_shape=results,
        input_output_aliases=aliases,
        compiler_params=pltpu.CompilerParams(vmem_limit_bytes=VMEM_LIMIT),
        cost_estimate=cost(7 * count),
        name="attention_back",
    )(*args)


def proj_grad_body(a_ref, dqkv_ref, o_ref, dr_ref, small_ref, bias_ref, order_ref, keep_ref, send_ref, at_ref):
    step = pl.program_id(0)
    width = a_ref.shape[1]
    half = width // 2
    order = order_ref[...]

    def put(at, value):
        keep_ref[:, at] = value[:half].astype(BF16)
        send_ref[:, at] = value[half:].astype(BF16)

    @pl.when(step == 0)
    def _():
        at_ref[...] = dot(order, a_ref[...], ((1,), (1,))).astype(BF16)
        put(slice(3 * width, 4 * width), dot(dot(order, o_ref[...], ((1,), (1,))).astype(BF16), dr_ref[...]))
        table = jnp.concatenate([small_ref[...], bias_ref[...], jnp.zeros((112, width), F32)], axis=0).astype(BF16)
        put(slice(4 * width, None), dot(order, table, ((1,), (1,))))

    put(pl.ds(pl.multiple_of(step * width, 128), width), dot(at_ref[...], dqkv_ref[...]))


def proj_grad(a, dqkv, o, dr, small, bias, order, after=()):
    n, width = a.shape
    waits = len(after)
    shape = (width // 2, 4 * width + 128)
    return pl.pallas_call(
        lambda *refs: proj_grad_body(*refs[:7], *refs[7 + waits:]),
        grid=(3,),
        in_specs=[whole(a.shape), pl.BlockSpec((n, width), lambda i: (0, i)), whole(o.shape), whole(dr.shape), whole(small.shape), whole(bias.shape),
                  whole(order.shape)] + tied(waits),
        out_specs=[whole(shape)] * 2,
        out_shape=[jax.ShapeDtypeStruct(shape, BF16)] * 2,
        scratch_shapes=[pltpu.VMEM((width, n), BF16)],
        compiler_params=pltpu.CompilerParams(vmem_limit_bytes=VMEM_LIMIT),
        cost_estimate=cost(9),
        name="projection_gradients",
    )(a, dqkv, o, dr, small, bias, order, *after)


def place_body(count, to_ref, *refs):
    pieces, out_ref, sems = refs[:count], refs[count], refs[count + 1]
    copies = [pltpu.make_async_copy(piece, out_ref.at[to_ref[i]], sems.at[i]) for i, piece in enumerate(pieces)]
    for copy in copies:
        copy.start()
    for copy in copies:
        copy.wait()


def place(pieces, to, after=()):
    rows, columns = pieces[0].shape
    count, waits = len(pieces), len(after)
    out = pl.pallas_call(
        lambda *refs: place_body(count, *refs[:count + 1], *refs[count + 1 + waits:]),
        in_specs=[pl.BlockSpec(memory_space=pltpu.SMEM)] + [pl.BlockSpec(memory_space=pl.ANY)] * count + tied(waits),
        out_specs=pl.BlockSpec(memory_space=pltpu.VMEM),
        out_shape=jax.ShapeDtypeStruct((count, rows, columns), BF16),
        scratch_shapes=[pltpu.SemaphoreType.DMA((count,))],
        compiler_params=pltpu.CompilerParams(vmem_limit_bytes=VMEM_LIMIT),
        cost_estimate=cost(4),
        name="place_pieces",
    )(to, *pieces, *after)
    return out.reshape(count * rows, columns)


def place_down_body(count, to_ref, g_ref, m_ref, vec_ref, *refs):
    pieces, (w_ref, y_ref), (held_ref, act_ref, sems, act_sem, out_sem) = refs[:count], refs[count:count + 2], refs[count + 2:]
    rows = pieces[0].shape[0]
    copies = [pltpu.make_async_copy(piece, held_ref.at[pl.ds(pl.multiple_of(to_ref[i] * rows, rows), rows)], sems.at[i])
              for i, piece in enumerate(pieces)]
    copies.append(pltpu.make_async_copy(g_ref.at[pl.ds(0, act_ref.shape[0])], act_ref, act_sem))
    for copy in copies:
        copy.start()
    for copy in copies:
        copy.wait()
    out = pltpu.make_async_copy(held_ref, w_ref, out_sem)
    out.start()
    y_ref[...] = (m_ref[...] + vec_ref[7:8] + dot(act_ref[...], held_ref[...])).astype(BF16)
    out.wait()


def place_down(pieces, to, g, m, vec, parts):
    rows, width = pieces[0].shape
    count = len(pieces)
    ff = count * rows
    n = g.shape[0] // parts
    return pl.pallas_call(
        lambda *refs: place_down_body(count, *refs),
        grid=(1,),
        in_specs=[pl.BlockSpec(memory_space=pltpu.SMEM)] + tied(1) + [whole((n, width)), whole(vec.shape)] + tied(count),
        out_specs=[pl.BlockSpec(memory_space=pl.ANY), whole((n, width))],
        out_shape=[jax.ShapeDtypeStruct((ff, width), BF16), jax.ShapeDtypeStruct((n, width), BF16)],
        scratch_shapes=[pltpu.VMEM((ff, width), BF16), pltpu.VMEM((n, ff), BF16), pltpu.SemaphoreType.DMA((count,)),
                        pltpu.SemaphoreType.DMA(()), pltpu.SemaphoreType.DMA(())],
        compiler_params=pltpu.CompilerParams(vmem_limit_bytes=VMEM_LIMIT),
        cost_estimate=cost(10),
        name="place_and_feed_forward_down",
    )(to, g, m, vec, *pieces)


def finish_body(rows, per_row, width, *refs):
    *terms, down_ref, qkv_ref, out_ref, gain_ref, shift_ref, bias_ref, up_ref, wide_ref = refs
    wide_ref[0] = down_ref[...].astype(F32)
    total = terms[0][:rows].astype(F32)
    for term in terms[1:]:
        total = total + term[:rows].astype(F32)
    qkv_ref[0] = total[:, :3 * width]
    out_ref[0] = total[:, 3 * width:4 * width]
    small = total[:, 4 * width:]
    vectors = small.T
    gain_ref[0] = vectors[0:2]
    shift_ref[0] = vectors[2:4]
    bias_ref[0] = vectors[4:8]
    flat = rows * per_row
    spread = lax.broadcasted_iota(jnp.int32, (128, flat), 1) % per_row + 8 == lax.broadcasted_iota(jnp.int32, (128, flat), 0)
    wide = lax.dot_general(small, spread.astype(F32), (((1,), (0,)), ((), ())), precision=lax.Precision.HIGHEST, preferred_element_type=F32)
    here = lax.broadcasted_iota(jnp.int32, (rows, flat), 1) // per_row == lax.broadcasted_iota(jnp.int32, (rows, flat), 0)
    up_ref[...] = jnp.sum(jnp.where(here, wide, 0.0), axis=0, keepdims=True)


def finish(large, pieces, down, rows, per_row):
    columns = large[0].shape[1]
    width = (columns - 128) // 4
    shapes = [(1, rows, 3 * width), (1, rows, width), (1, 2, rows), (1, 2, rows), (1, 4, rows), (1, rows * per_row), (1, *down.shape)]
    return pl.pallas_call(
        lambda *refs: finish_body(rows, per_row, width, *refs),
        grid=(1,),
        in_specs=[pl.BlockSpec((2 * rows, columns), lambda i: (0, 0))] * len(large) + [whole(piece.shape) for piece in (*pieces, down)],
        out_specs=[whole(s) for s in shapes],
        out_shape=[jax.ShapeDtypeStruct(s, F32) for s in shapes],
        compiler_params=pltpu.CompilerParams(vmem_limit_bytes=VMEM_LIMIT),
        cost_estimate=cost(2),
        name="gather_projection_gradients",
    )(*large, *pieces, down)


def places(count):
    return count // 4, 2, 2


def hop(value, kind, step=1):
    zs, ys, cores = places(lax.axis_size("dp"))
    pairs = []
    for z in range(zs):
        for y in range(ys):
            for c in range(cores):
                to = {"core": (z, y, c ^ 1), "y": (z, y ^ 1, c), "z": ((z + step) % zs, y, c)}[kind]
                pairs.append(((z * ys + y) * cores + c, (to[0] * ys + to[1]) * cores + to[2]))
    return lax.ppermute(value, "dp", pairs)


def behind_me():
    zs, ys, cores = places(lax.axis_size("dp"))
    me = lax.axis_index("dp")
    return me // (cores * ys), (me // cores) % ys, me % cores


def along_line(shard):
    return [shard] + [hop(shard, "z", step) for step in range(1, places(lax.axis_size("dp"))[0])]


def both(mine, got):
    return (mine.astype(F32) + got.astype(F32)).astype(BF16)


def scatter_order(shard):
    zs, ys, cores = places(lax.axis_size("dp"))
    z, y, c = behind_me()
    row = jnp.arange(zs * ys * cores * shard)
    block = row // shard
    to = (((z + block % zs) % zs) * ys + (y ^ (block // zs % ys))) * cores + (c ^ (block // (zs * ys)))
    return (jnp.arange(zs * ys * cores * shard)[None, :] == (to * shard + row % shard)[:, None]).astype(BF16)


def y_step(mine, got):
    half = mine.shape[0] // 2
    return (mine[:half], got[:half]), hop(both(mine[half:], got[half:]), "y")


def z_step(mine, got):
    zs, _, _ = places(lax.axis_size("dp"))
    rows = got.shape[0] // zs
    terms = [[term[k * rows:k * rows + rows] for term in (*mine, got)] for k in range(zs)]
    return terms[0] + [hop(total(terms[k]).astype(BF16), "z", k) for k in range(1, zs)]


def total(terms):
    out = terms[0].astype(F32)
    for term in terms[1:]:
        out = out + term.astype(F32)
    return out


def held(value, *after):
    return lax.optimization_barrier((value, *after))[0]


def siblings(pieces, *after):
    return [hop(held(piece, *after), "core") for piece in pieces]


def places_of_pieces():
    zs, ys, cores = places(lax.axis_size("dp"))
    z, y, c = behind_me()
    to = []
    for core in (c, 1 - c):
        for row in (y, 1 - y):
            to += [(((z + zs - step) % zs) * ys + row) * cores + core for step in range(zs)]
    return jnp.stack(to).astype(jnp.int32)


def on_device(tokens, lengths, cotangent, w_qkv, w_out, w_up, w_down, norm_gain, norm_bias, bias_vec, up_bias):
    section = lax.axis_index("section")
    windows, seq, width = tokens.shape
    n = windows * seq
    shard = w_qkv.shape[1]
    per_row = up_bias.shape[1] // shard
    ff = w_up.shape[2]
    parts = 2
    part = windows // parts
    by_hand = lax.axis_size("dp") == 16
    table = jnp.concatenate([norm_gain[0], norm_bias[0], bias_vec[0]], axis=0).T
    table = jnp.concatenate([table, up_bias.reshape(shard, per_row)], axis=1)
    used = table.shape[1]
    table = jnp.pad(table, ((0, 0), (0, 128 - used)))
    packed = jnp.concatenate([w_qkv[0], w_out[0], table], axis=1)
    if by_hand:
        down = w_down[0]
        order, to = scatter_order(shard), places_of_pieces()
        wup = lax.all_gather(w_up[0], "dp", axis=0, tiled=True)
        proj_1, proj_3 = hop(packed, "z", 1), hop(packed, "z", 3)
        proj_y0, down_y0 = hop(packed, "y"), hop(down, "y")
        now = (proj_1, proj_3, proj_y0, order)
        proj_2, down_1 = hop(held(packed, *now), "z", 2), hop(held(down, *now), "z", 1)
        proj_y1, proj_y3 = hop(held(proj_1, *now), "y"), hop(held(proj_3, *now), "y")
        now = (proj_2, proj_y1, proj_y3, down_y0, down_1)
        down_3 = hop(held(down, *now), "z", 3)
        proj_y2, down_y1 = hop(held(proj_2, *now), "y"), hop(held(down_1, *now), "y")
        now = (down_3, proj_y2, down_y1)
        pieces = [packed, proj_1, proj_2, proj_3, proj_y0, proj_y1, proj_y2, proj_y3]
        proj = place(pieces + siblings(pieces, proj_y2), to)
        down_2 = hop(held(down, *now), "z", 2)
        down_y3 = hop(held(down_3, *now), "y")
    else:
        order = (jnp.arange(width)[None, :] == jnp.arange(width)[:, None]).astype(BF16)
        proj = lax.all_gather(packed, "dp", axis=0, tiled=True)
        wup = lax.all_gather(w_up[0], "dp", axis=0, tiled=True)
        wdown = lax.all_gather(w_down[0], "dp", axis=0, tiled=True)
    small = proj[:, 4 * width:4 * width + used]
    vec = small[:, :8].T.astype(F32)
    bup = small[:, 8:].reshape(1, ff).astype(F32)

    lengths = jnp.append(lengths, section)
    mid, c = attn_fwd(tokens, lengths, proj, False, after=(vec, bup))
    c = c.reshape(n, width)
    mid = mid.reshape(n, width)
    if by_hand:
        now = (down_2, down_y3, c)
        down_y2 = hop(held(down_2, *now), "y")
    act = mlp_up(c, wup, bup)
    if by_hand:
        pieces = [down, down_1, down_2, down_3, down_y0, down_y1, down_y2, down_y3]
        wdown, y_a = place_down(pieces + siblings(pieces, act), to, act, mid, vec, parts)
    else:
        y_a = mlp_down(act, mid, wdown, vec, 0, parts)
    y_b = mlp_down(act, mid, wdown, vec, 1, parts)
    kept = ()
    arrived = [lax.ppermute(y.reshape(part, seq, width), "section", [(0, 1)]) for y in (y_a, y_b)]
    for at in range(parts):
        kept = attn_fwd(tokens, lengths, proj, True, at, parts, held(arrived[at], *kept[:1]), vec, kept)
    m, c, qkv, e, o, a, inv, h = kept
    c = c.reshape(n, width)
    y, g, gp, dc = mlp_both(c, m.reshape(n, width), cotangent.reshape(n, width), wup, wdown, bup, vec)
    dc = dc.reshape(tokens.shape)
    arrived = []
    for at in range(parts):
        back, = attn_bwd(dc, cotangent, m, h, qkv, e, o, inv, proj, vec, at, parts, False)
        arrived.append(lax.ppermute(back, "section", [(1, 0)]))
    dz = [jnp.where(section == 1, cotangent[:part], arrived[0])]
    dc, du = mlp_bwd(dz[0].reshape(part * seq, width), gp, wup, wdown, True, 0, parts)
    dz.append(jnp.where(section == 1, cotangent[part:], held(arrived[1], dc)))
    last = dz[1].reshape(part * seq, width)
    dz = jnp.concatenate(dz)
    g_down = down_grad(g, dz.reshape(n, width))
    sum_down = lax.psum_scatter(g_down, "dp", scatter_dimension=0, tiled=True)
    dc, keep_u, send_u, bup_u = mlp_grad(last, gp, wup, wdown, du, c, order, dc, (g_down,))
    dc = dc.reshape(tokens.shape)
    if by_hand:
        got_u = hop(send_u, "core")
        half = ff // 2
        rest = keep_u.shape[0] // 2
        mine_a, mine_b = [(keep_u[:rest, at], got_u[:rest, at]) for at in (slice(0, half), slice(half, ff))]
        send_a = both(keep_u[rest:, :half], got_u[rest:, :half])
        got_a = hop(send_a, "y")
        send_b = both(held(keep_u, send_a)[rest:, half:], held(got_u, send_a)[rest:, half:])
        got_b = hop(send_b, "y")
        back = attn_bwd(dc, dz, m, h, qkv, e, o, inv, proj, vec, 0, 1, True, (), (got_u,))
        terms_a = z_step(mine_a, held(got_a, back[3]))
        wait = (got_a,)
    else:
        back = attn_bwd(dc, dz, m, h, qkv, e, o, inv, proj, vec, 0, 1, True)
        wait = ()
    dh, dr, dqkv, smalls = back
    g_bup = bup_u[0].reshape(width, per_row).T
    keep_p, send_p = proj_grad(
        a.reshape(n, width), dqkv.reshape(n, 3 * width), o.reshape(n, width), dr.reshape(n, width), smalls, g_bup, order, wait)
    if by_hand:
        terms_b = z_step(mine_b, got_b)
        sum_up = jnp.concatenate([total(terms_a), total(terms_b)], axis=1)
        core_p = hop(held(send_p, got_b, *terms_a[3:]), "core")
        mine_p, got_p = y_step(keep_p, core_p)
        pieces = z_step(mine_p, held(got_p, *terms_b))[3:]
        *rest, sum_down = finish((keep_p, core_p, got_p), pieces, sum_down, shard, per_row)
    else:
        scatter = lambda *halves: lax.psum_scatter(jnp.concatenate(halves), "dp", scatter_dimension=0, tiled=True).astype(F32)
        sum_up = scatter(keep_u, send_u)
        sum_proj = scatter(keep_p, send_p)
        sum_down = sum_down[None].astype(F32)
        vectors = sum_proj[:, 4 * width:4 * width + 8].T
        rest = (
            sum_proj[None, :, :3 * width],
            sum_proj[None, :, 3 * width:4 * width],
            vectors[None, 0:2],
            vectors[None, 2:4],
            vectors[None, 4:8],
            sum_proj[:, 4 * width + 8:4 * width + used].reshape(1, -1),
        )
    return (y.reshape((1,) + tokens.shape), dh[None], rest[0], rest[1], sum_up[None], sum_down, *rest[2:])


def solution(mesh):
    sharded = [P("section", "dp", None)] * 4 + [P("section", None, "dp")] * 3 + [P("section", "dp")]
    windows = P("dp", None, None)
    out = P("section", "dp", None, None)
    return jax.shard_map(
        on_device, mesh=mesh, in_specs=(windows, P("dp"), windows, *sharded), out_specs=(out, out, *sharded), check_vma=False
    )
```

```python
import jax
import jax.numpy as jnp
from jax import lax
from jax.experimental import pallas as pl
from jax.experimental.pallas import tpu as pltpu
from jax.sharding import PartitionSpec as P

HEADS = 20
HEAD_DIM = 32
GROUP = 128 // HEAD_DIM
SCALE = HEAD_DIM ** -0.5
LOG2E = 1.4426950408889634
VMEM_LIMIT = 56 * 1024 * 1024
F32 = jnp.float32
BF16 = jnp.bfloat16


def cost(us):
    return pl.CostEstimate(flops=int(us * 1.1e9), bytes_accessed=1024, transcendentals=0)


def tied(count):
    return [pl.BlockSpec(memory_space=pl.ANY)] * count


def dot(a, b, dims=((1,), (0,))):
    return lax.dot_general(a, b, (dims, ((), ())), preferred_element_type=F32)


def gelu_pair(u):
    below = 0.5 + 0.5 * lax.erf(u * 0.7071067811865476)
    return u * below, below + (0.3989422804014327 * u) * jnp.exp(-0.5 * (u * u))


def normed(v, gain, shift):
    centered = v - jnp.mean(v, axis=-1, keepdims=True)
    spread = jnp.mean(centered * centered, axis=-1, keepdims=True)
    hat = centered * lax.rsqrt(spread + 1e-05)
    return hat * gain + shift


def norm_back(v, gain, grad):
    centered = v - jnp.mean(v, axis=-1, keepdims=True)
    spread = jnp.mean(centered * centered, axis=-1, keepdims=True)
    inv = lax.rsqrt(spread + 1e-05)
    hat = centered * inv
    g = grad * gain
    back = inv * (g - jnp.mean(g, axis=-1, keepdims=True) - hat * jnp.mean(g * hat, axis=-1, keepdims=True))
    return back, jnp.sum(grad * hat, axis=0, keepdims=True), jnp.sum(grad, axis=0, keepdims=True)


def attn_fwd_body(save, first_window, len_ref, h_ref, *rest):
    if save:
        arrived_ref, wqkv_ref, vec_ref, m_ref, c_ref, qkv_ref, e_ref, o_ref, a_ref, inv_ref, taken_ref = rest
    else:
        wqkv_ref, m_ref, c_ref = rest
    width = h_ref.shape[2]
    seq = h_ref.shape[1]
    length = len_ref[pl.program_id(0) + first_window]
    if save:
        taken = jnp.where(len_ref[len_ref.shape[0] - 1] == 0, h_ref[0], arrived_ref[0])
        taken_ref[0] = taken
        h = taken.astype(F32)
        vec = vec_ref[...]
    else:
        h = h_ref[0].astype(F32)
        vec = wqkv_ref[:, 4 * width:].astype(F32).T
    a = normed(h, vec[0:1], vec[2:3]).astype(BF16)
    q_all = (dot(a, wqkv_ref[:, :width]) + vec[4:5]).astype(BF16)
    k_all = dot(a, wqkv_ref[:, width:2 * width]).astype(BF16)
    v_all = (dot(a, wqkv_ref[:, 2 * width:3 * width]) + vec[5:6]).astype(BF16)
    if save:
        a_ref[0] = a
        qkv_ref[0, :, :width] = q_all
        qkv_ref[0, :, width:2 * width] = k_all
        qkv_ref[0, :, 2 * width:] = v_all
    head_of = lax.broadcasted_iota(jnp.int32, (1, 128), 1) // HEAD_DIM
    key_at = lax.broadcasted_iota(jnp.int32, (seq, 128), 0)
    lane = lax.broadcasted_iota(jnp.int32, (seq, 128), 1)
    past = jnp.where((lane == 0) & (key_at >= length), -1e30, 0.0).astype(BF16)
    first = jnp.where(lane == 0, 1.0, 0.0).astype(BF16)
    ones = jnp.ones((seq, 128), BF16)
    zero = jnp.zeros((seq, 128), BF16)
    mixed = []
    for g in range(width // 128):
        at = slice(128 * g, 128 * g + 128)
        q, v = q_all[:, at], v_all[:, at]
        k = jnp.concatenate([k_all[:, at], past], axis=1)
        acc, inv = None, None
        stacked = dot(jnp.concatenate([jnp.concatenate([jnp.where(head_of == j, q, zero), first], axis=1) for j in range(GROUP)], axis=0), k, ((1,), (1,)))
        for j in range(GROUP):
            mine = head_of == j
            s = stacked[seq * j:seq * j + seq]
            e = jnp.exp2((s - jnp.max(s, axis=1, keepdims=True)) * (SCALE * LOG2E)).astype(BF16)
            if save:
                e_ref[0, GROUP * g + j] = e
            both_parts = dot(e, jnp.concatenate([jnp.where(mine, v, zero), ones], axis=1))
            one_over = 1.0 / both_parts[:, 128:]
            part = both_parts[:, :128] * one_over
            acc = part if acc is None else acc + part
            inv = one_over if inv is None else jnp.where(mine, one_over, inv)
        mixed.append(acc.astype(BF16))
        if save:
            inv_ref[0, :, at] = inv
    o = jnp.concatenate(mixed, axis=1)
    if save:
        o_ref[0] = o
    m = h + dot(o, wqkv_ref[:, 3 * width:4 * width]) + vec[6:7]
    m_ref[0] = m
    c_ref[0] = normed(m, vec[1:2], vec[3:4]).astype(BF16)


def whole(shape):
    return pl.BlockSpec(shape, lambda *_: (0,) * len(shape))


def attn_fwd(h, lengths, proj, save, at=0, parts=1, arrived=None, vec=None, earlier=(), after=()):
    n, seq, width = h.shape
    count = n // parts
    row = lambda *tail: pl.BlockSpec((1,) + tail, lambda i, *_: (i + at * count,) + (0,) * len(tail))
    shapes = [((seq, width), F32), ((seq, width), BF16)]
    args, in_specs = [h], [row(seq, width)]
    if save:
        shapes += [((seq, 3 * width), BF16), ((HEADS, seq, seq), BF16), ((seq, width), BF16), ((seq, width), BF16), ((seq, width), F32), ((seq, width), BF16)]
        args += [arrived, proj, vec]
        in_specs += [pl.BlockSpec((1, seq, width), lambda i, *_: (i, 0, 0)), whole(proj.shape), whole(vec.shape)]
    else:
        args += [proj]
        in_specs += [whole(proj.shape)]
    used, waits = 1 + len(args), len(earlier) + len(after)
    return pl.pallas_call(
        lambda *refs: attn_fwd_body(save, at * count, *refs[:used], *refs[used + waits:]),
        grid_spec=pltpu.PrefetchScalarGridSpec(
            num_scalar_prefetch=1,
            grid=(count,),
            in_specs=in_specs + tied(waits),
            out_specs=[row(*s) for s, _ in shapes],
        ),
        out_shape=[jax.ShapeDtypeStruct((n,) + s, d) for s, d in shapes],
        input_output_aliases={used + i: i for i in range(len(earlier))},
        compiler_params=pltpu.CompilerParams(vmem_limit_bytes=VMEM_LIMIT),
        cost_estimate=cost(4.5 * count),
        name="attention_forward",
    )(lengths, *args, *earlier, *after)


def mlp_fwd_body(save, rows, c_ref, m_ref, wup_ref, wdown_ref, bup_ref, vec_ref, *outs):
    if save:
        y_ref, g_ref, gp_ref, acc_ref = outs
    else:
        y_ref, acc_ref = outs
    step = pl.program_id(0)

    @pl.when(step == 0)
    def _():
        acc_ref[...] = m_ref[...] + vec_ref[7:8]

    for r in range(c_ref.shape[0] // rows):
        at = slice(r * rows, r * rows + rows)
        u = dot(c_ref[at], wup_ref[...]) + bup_ref[...]
        act, slope = gelu_pair(u)
        act = act.astype(BF16)
        if save:
            g_ref[at] = act
            gp_ref[at] = slope.astype(BF16)
        acc_ref[at] += dot(act, wdown_ref[...])

    @pl.when(step == pl.num_programs(0) - 1)
    def _():
        y_ref[...] = acc_ref[...].astype(BF16)


def mlp_fwd(c, m, wup, wdown, bup, vec, save, at=0, parts=1, after=(), chunk=1280, rows=256):
    n, width = c.shape
    n //= parts
    waits = len(after)
    part = pl.BlockSpec((n, width), lambda i: (at, 0))
    ff = wup.shape[1]
    outs = [jax.ShapeDtypeStruct((n, width), BF16)]
    specs = [whole((n, width))]
    if save:
        outs += [jax.ShapeDtypeStruct((n, ff), BF16)] * 2
        specs += [pl.BlockSpec((n, chunk), lambda i: (0, i))] * 2
    return pl.pallas_call(
        lambda *refs: mlp_fwd_body(save, rows, *refs[:6], *refs[6 + waits:]),
        grid=(ff // chunk,),
        in_specs=[part, part, pl.BlockSpec((width, chunk), lambda i: (0, i)),
                  pl.BlockSpec((chunk, width), lambda i: (i, 0)), pl.BlockSpec((1, chunk), lambda i: (0, i)), whole(vec.shape)] + tied(waits),
        out_specs=specs,
        out_shape=outs,
        scratch_shapes=[pltpu.VMEM((n, width), F32)],
        compiler_params=pltpu.CompilerParams(vmem_limit_bytes=VMEM_LIMIT),
        cost_estimate=cost(26),
        name="feed_forward",
    )(c, m, wup, wdown, bup, vec, *after)


def mlp_both_body(rows, c_ref, m_ref, dz_ref, wup_ref, wdown_ref, bup_ref, vec_ref, y_ref, g_ref, gp_ref, dc_ref, acc_ref):
    step = pl.program_id(0)

    @pl.when(step == 0)
    def _():
        acc_ref[...] = m_ref[...] + vec_ref[7:8]
        dc_ref[...] = jnp.zeros_like(dc_ref)

    for r in range(c_ref.shape[0] // rows):
        at = slice(r * rows, r * rows + rows)
        u = dot(c_ref[at], wup_ref[...]) + bup_ref[...]
        dg = dot(dz_ref[at], wdown_ref[...], ((1,), (1,)))
        act, slope = gelu_pair(u)
        act, slope = act.astype(BF16), slope.astype(BF16)
        g_ref[at] = act
        gp_ref[at] = slope
        acc_ref[at] += dot(act, wdown_ref[...])
        dc_ref[at] += dot((dg * slope.astype(F32)).astype(BF16), wup_ref[...], ((1,), (1,)))

    @pl.when(step == pl.num_programs(0) - 1)
    def _():
        y_ref[...] = acc_ref[...].astype(BF16)


def mlp_both(c, m, dz, wup, wdown, bup, vec, chunk=1280, rows=256):
    n, width = c.shape
    ff = wup.shape[1]
    column = pl.BlockSpec((n, chunk), lambda i: (0, i))
    return pl.pallas_call(
        lambda *refs: mlp_both_body(rows, *refs),
        grid=(ff // chunk,),
        in_specs=[whole(c.shape), whole(m.shape), whole(dz.shape), pl.BlockSpec((width, chunk), lambda i: (0, i)),
                  pl.BlockSpec((chunk, width), lambda i: (i, 0)), pl.BlockSpec((1, chunk), lambda i: (0, i)), whole(vec.shape)],
        out_specs=[whole((n, width)), column, column, whole((n, width))],
        out_shape=[jax.ShapeDtypeStruct((n, width), BF16), jax.ShapeDtypeStruct((n, ff), BF16), jax.ShapeDtypeStruct((n, ff), BF16),
                   jax.ShapeDtypeStruct((n, width), F32)],
        scratch_shapes=[pltpu.VMEM((n, width), F32)],
        compiler_params=pltpu.CompilerParams(vmem_limit_bytes=VMEM_LIMIT),
        cost_estimate=cost(42),
        name="feed_forward_both",
    )(c, m, dz, wup, wdown, bup, vec)


def mlp_up_body(rows, c_ref, wup_ref, bup_ref, g_ref):
    for r in range(c_ref.shape[0] // rows):
        at = slice(r * rows, r * rows + rows)
        g_ref[at] = gelu_pair(dot(c_ref[at], wup_ref[...]) + bup_ref[...])[0].astype(BF16)


def mlp_up(c, wup, bup, at=0, parts=1, after=(), chunk=1280, rows=256):
    n, width = c.shape
    n //= parts
    ff = wup.shape[1]
    waits = len(after)
    return pl.pallas_call(
        lambda *refs: mlp_up_body(rows, *refs[:3], *refs[3 + waits:]),
        grid=(ff // chunk,),
        in_specs=[pl.BlockSpec((n, width), lambda i: (at, 0)), pl.BlockSpec((width, chunk), lambda i: (0, i)), pl.BlockSpec((1, chunk), lambda i: (0, i))] + tied(waits),
        out_specs=pl.BlockSpec((n, chunk), lambda i: (0, i)),
        out_shape=jax.ShapeDtypeStruct((n, ff), BF16),
        compiler_params=pltpu.CompilerParams(vmem_limit_bytes=VMEM_LIMIT),
        cost_estimate=cost(0.0125 * n),
        name="feed_forward_up",
    )(c, wup, bup, *after)


def mlp_down_body(g_ref, m_ref, wdown_ref, vec_ref, y_ref, acc_ref):
    step = pl.program_id(0)

    @pl.when(step == 0)
    def _():
        acc_ref[...] = m_ref[...] + vec_ref[7:8]

    acc_ref[...] += dot(g_ref[...], wdown_ref[...])

    @pl.when(step == pl.num_programs(0) - 1)
    def _():
        y_ref[...] = acc_ref[...].astype(BF16)


def mlp_down(g, m, wdown, vec, at, parts, after=(), chunk=1280):
    ff, width = wdown.shape
    rows = g.shape[0] // parts
    waits = len(after)
    return pl.pallas_call(
        lambda *refs: mlp_down_body(*refs[:4], *refs[4 + waits:]),
        grid=(ff // chunk,),
        in_specs=[pl.BlockSpec((rows, chunk), lambda i: (at, i)), pl.BlockSpec((rows, width), lambda i: (at, 0)),
                  pl.BlockSpec((chunk, width), lambda i: (i, 0)), whole(vec.shape)] + tied(waits),
        out_specs=whole((rows, width)),
        out_shape=jax.ShapeDtypeStruct((rows, width), BF16),
        scratch_shapes=[pltpu.VMEM((rows, width), F32)],
        compiler_params=pltpu.CompilerParams(vmem_limit_bytes=VMEM_LIMIT),
        cost_estimate=cost(0.017 * rows),
        name="feed_forward_down",
    )(g, m, wdown, vec, *after)


def mlp_bwd_body(save, rows, dz_ref, gp_ref, wup_ref, wdown_ref, dc_ref, *outs):
    @pl.when(pl.program_id(0) == 0)
    def _():
        dc_ref[...] = jnp.zeros_like(dc_ref)

    for r in range(dz_ref.shape[0] // rows):
        at = slice(r * rows, r * rows + rows)
        dg = dot(dz_ref[at], wdown_ref[...], ((1,), (1,)))
        du = (dg * gp_ref[at].astype(F32)).astype(BF16)
        if save:
            outs[0][at] = du
        dc_ref[at] += dot(du, wup_ref[...], ((1,), (1,)))


def mlp_bwd(dz, gp, wup, wdown, save, at=0, parts=1, earlier=(), after=(), chunk=1280, rows=256):
    n, width = dz.shape
    ff = wup.shape[1]
    args = [dz, gp, wup, wdown, *earlier, *after]
    outs = [jax.ShapeDtypeStruct((n * parts, width), F32)]
    specs = [pl.BlockSpec((n, width), lambda i: (at, 0))]
    if save:
        outs += [jax.ShapeDtypeStruct((n, ff), BF16)]
        specs += [pl.BlockSpec((n, chunk), lambda i: (0, i))]
    return pl.pallas_call(
        lambda *refs: mlp_bwd_body(save, rows, *refs[:4], *refs[len(args):]),
        grid=(ff // chunk,),
        in_specs=[whole(dz.shape), pl.BlockSpec((n, chunk), lambda i: (at, i)), pl.BlockSpec((width, chunk), lambda i: (0, i)),
                  pl.BlockSpec((chunk, width), lambda i: (i, 0))] + tied(len(args) - 4),
        out_specs=specs,
        out_shape=outs,
        input_output_aliases={4 + i: i for i in range(len(earlier))},
        compiler_params=pltpu.CompilerParams(vmem_limit_bytes=VMEM_LIMIT),
        cost_estimate=cost(22 / parts),
        name="feed_forward_back",
    )(*args)


def up_grad_body(c_ref, order_ref, du_ref, keep_ref, send_ref, sum_ref, ct_ref):
    half = keep_ref.shape[0]

    @pl.when(pl.program_id(0) == 0)
    def _():
        ct_ref[:2 * half] = dot(order_ref[...], c_ref[...], ((1,), (1,))).astype(BF16)
        ct_ref[2 * half:] = jnp.ones_like(ct_ref[2 * half:])

    grad = dot(ct_ref[...], du_ref[...])
    keep_ref[...] = grad[:half].astype(BF16)
    send_ref[...] = grad[half:2 * half].astype(BF16)
    sum_ref[...] = grad[2 * half:2 * half + 8]


def up_grad(c, order, du, at, parts, after=(), chunk=1280):
    n, width = c.shape
    ff = du.shape[1] // parts
    first = at * ff // chunk
    waits = len(after)
    column = lambda rows: pl.BlockSpec((rows, chunk), lambda i: (0, i))
    return pl.pallas_call(
        lambda *refs: up_grad_body(*refs[:3], *refs[3 + waits:]),
        grid=(ff // chunk,),
        in_specs=[whole(c.shape), whole(order.shape), pl.BlockSpec((n, chunk), lambda i: (0, i + first))] + tied(waits),
        out_specs=[column(width // 2), column(width // 2), column(8)],
        out_shape=[jax.ShapeDtypeStruct((width // 2, ff), BF16)] * 2 + [jax.ShapeDtypeStruct((8, ff), F32)],
        scratch_shapes=[pltpu.VMEM((width + 16, n), BF16)],
        compiler_params=pltpu.CompilerParams(vmem_limit_bytes=VMEM_LIMIT),
        cost_estimate=cost(13 / parts),
        name="up_gradient",
    )(c, order, du, *after)


def mlp_grad_body(rows, dz_ref, gp_ref, wup_ref, wdown_ref, early_ref, c_ref, order_ref, dc_ref, keep_ref, send_ref, sum_ref, du_ref, ct_ref):
    half = keep_ref.shape[0]
    count = early_ref.shape[0]

    @pl.when(pl.program_id(0) == 0)
    def _():
        dc_ref[...] = jnp.zeros_like(dc_ref)
        ct_ref[:2 * half] = dot(order_ref[...], c_ref[...], ((1,), (1,))).astype(BF16)
        ct_ref[2 * half:] = jnp.ones_like(ct_ref[2 * half:])

    for r in range(dz_ref.shape[0] // rows):
        at = slice(r * rows, r * rows + rows)
        dg = dot(dz_ref[at], wdown_ref[...], ((1,), (1,)))
        du = (dg * gp_ref[at].astype(F32)).astype(BF16)
        du_ref[at] = du
        dc_ref[at] += dot(du, wup_ref[...], ((1,), (1,)))
    grad = dot(ct_ref[:, :count], early_ref[...]) + dot(ct_ref[:, count:], du_ref[...])
    keep_ref[...] = grad[:half].astype(BF16)
    send_ref[...] = grad[half:2 * half].astype(BF16)
    sum_ref[...] = grad[2 * half:2 * half + 8]


def mlp_grad(dz, gp, wup, wdown, early, c, order, dc, after=(), chunk=1280, rows=256):
    count, width = dz.shape
    n, ff = gp.shape
    at = n // count - 1
    waits = 1 + len(after)
    column = lambda rows: pl.BlockSpec((rows, chunk), lambda i: (0, i))
    return pl.pallas_call(
        lambda *refs: mlp_grad_body(rows, *refs[:7], *refs[7 + waits:]),
        grid=(ff // chunk,),
        in_specs=[whole(dz.shape), pl.BlockSpec((count, chunk), lambda i: (at, i)), column(width), pl.BlockSpec((chunk, width), lambda i: (i, 0)),
                  column(n - count), whole(c.shape), whole(order.shape)] + tied(waits),
        out_specs=[pl.BlockSpec((count, width), lambda i: (at, 0)), column(width // 2), column(width // 2), column(8)],
        out_shape=[jax.ShapeDtypeStruct((n, width), F32)] + [jax.ShapeDtypeStruct((width // 2, ff), BF16)] * 2 + [jax.ShapeDtypeStruct((8, ff), F32)],
        scratch_shapes=[pltpu.VMEM((count, chunk), BF16), pltpu.VMEM((width + 16, n), BF16)],
        input_output_aliases={7: 0},
        compiler_params=pltpu.CompilerParams(vmem_limit_bytes=VMEM_LIMIT),
        cost_estimate=cost(21),
        name="feed_forward_gradients",
    )(dz, gp, wup, wdown, early, c, order, dc, *after)


def down_grad_body(g_ref, dz_ref, out_ref):
    out_ref[...] = dot(g_ref[...], dz_ref[...], ((0,), (0,))).astype(BF16)


def down_grad(g, dz, after=(), chunk=1280):
    n, ff = g.shape
    width = dz.shape[1]
    waits = len(after)
    return pl.pallas_call(
        lambda *refs: down_grad_body(*refs[:2], *refs[2 + waits:]),
        grid=(ff // chunk,),
        in_specs=[pl.BlockSpec((n, chunk), lambda i: (0, i)), whole(dz.shape)] + tied(waits),
        out_specs=pl.BlockSpec((chunk, width), lambda i: (i, 0)),
        out_shape=jax.ShapeDtypeStruct((ff, width), BF16),
        compiler_params=pltpu.CompilerParams(vmem_limit_bytes=VMEM_LIMIT),
        cost_estimate=cost(12),
        name="down_gradient",
    )(g, dz, *after)


def attn_bwd_body(grads, base_ref, dc_ref, dz_ref, m_ref, h_ref, qkv_ref, e_ref, o_ref, inv_ref, proj_ref, vec_ref, dh_ref, *outs):
    if grads:
        dr_ref, dqkv_ref, small_ref = outs
    width = h_ref.shape[2]
    vec = vec_ref[...]

    if grads:
        @pl.when(pl.program_id(0) == 0)
        def _():
            small_ref[...] = jnp.zeros_like(small_ref) if base_ref is None else base_ref[...]

    dz = dz_ref[0].astype(F32)
    back, g_gain1, g_shift1 = norm_back(m_ref[0], vec[1:2], dc_ref[0])
    dm = dz + back
    dr = dm.astype(BF16)
    if grads:
        dr_ref[0] = dr
    do_all = dot(dr, proj_ref[:, 3 * width:4 * width], ((1,), (1,))).astype(BF16)
    seq = h_ref.shape[1]
    head_of = lax.broadcasted_iota(jnp.int32, (1, 128), 1) // HEAD_DIM
    ones = jnp.ones((seq, 128), BF16)
    zero = jnp.zeros((seq, 128), BF16)
    dq_all, dk_all, dv_all = [], [], []
    for g in range(width // 128):
        at = slice(128 * g, 128 * g + 128)
        q = qkv_ref[0, :, 128 * g:128 * g + 128]
        k = qkv_ref[0, :, width + 128 * g:width + 128 * g + 128]
        v = jnp.concatenate([qkv_ref[0, :, 2 * width + 128 * g:2 * width + 128 * g + 128], ones], axis=1)
        scaled = do_all[:, at].astype(F32) * (inv_ref[0, :, at] * SCALE)
        do = scaled.astype(BF16)
        less = (-scaled * o_ref[0, :, at].astype(F32)).astype(BF16)
        do_t, q_t = do.T, q.T
        dq = None
        dk_t, dv_t = [], []
        stacked = dot(jnp.concatenate([jnp.concatenate([jnp.where(head_of == j, do, zero), jnp.where(head_of == j, less, zero)], axis=1)
                                       for j in range(GROUP)], axis=0), v, ((1,), (1,)))
        for j in range(GROUP):
            mine = head_of == j
            e = e_ref[0, GROUP * g + j]
            rows = slice(HEAD_DIM * j, HEAD_DIM * j + HEAD_DIM)
            dv_t.append(dot(do_t[rows], e))
            dp = stacked[seq * j:seq * j + seq]
            ds = (e.astype(F32) * dp).astype(BF16)
            part = dot(ds, jnp.where(mine, k, zero))
            dq = part if dq is None else dq + part
            dk_t.append(dot(q_t[rows], ds))
        dq_all.append(dq.astype(BF16))
        dk_all.append(jnp.concatenate(dk_t, axis=0).astype(BF16).T)
        dv_all.append((jnp.concatenate(dv_t, axis=0) * (1.0 / SCALE)).astype(BF16).T)
    dqkv = jnp.concatenate(dq_all + dk_all + dv_all, axis=1)
    if grads:
        dqkv_ref[0] = dqkv
    da = dot(dqkv, proj_ref[:, :3 * width], ((1,), (1,)))
    back, g_gain0, g_shift0 = norm_back(h_ref[0].astype(F32), vec[0:1], da)
    dh_ref[0] = (dm + back).astype(dh_ref.dtype)
    if not grads:
        return
    total = lambda x: jnp.sum(x.astype(F32), axis=0, keepdims=True)
    small_ref[...] += jnp.concatenate(
        [g_gain0, g_gain1, g_shift0, g_shift1, total(dqkv[:, :width]), total(dqkv[:, 2 * width:]), total(dr), total(dz)], axis=0)


def attn_bwd(dc, dz, m, h, qkv, e, o, inv, proj, vec, at, parts, grads, earlier=(), after=()):
    n, seq, width = h.shape
    count = n // parts
    row = lambda *tail: pl.BlockSpec((1,) + tail, lambda i: (i + at * count,) + (0,) * len(tail))
    if grads:
        shapes = [((seq, width), F32), ((seq, width), BF16), ((seq, 3 * width), BF16)]
        specs = [row(*s) for s, _ in shapes] + [whole((8, width))]
        results = [jax.ShapeDtypeStruct((n,) + s, d) for s, d in shapes] + [jax.ShapeDtypeStruct((8, width), F32)]
    else:
        specs = [pl.BlockSpec((1, seq, width), lambda i: (i, 0, 0))]
        results = [jax.ShapeDtypeStruct((count, seq, width), BF16)]
    args = [dc, dz, m, h, qkv, e, o, inv, proj, vec]
    in_specs = [row(seq, width), row(seq, width), row(seq, width), row(seq, width), row(seq, 3 * width), row(HEADS, seq, seq),
                row(seq, width), row(seq, width), whole(proj.shape), whole(vec.shape)]
    base = len(args)
    if earlier:
        args += [earlier[3], *earlier[:3]]
        in_specs += [whole(earlier[3].shape)] + tied(3)
    aliases = {base + 1 + i: i for i in range(3)} if earlier else {}
    args += after
    in_specs += tied(len(after))
    used = len(args)

    def body(*refs):
        attn_bwd_body(grads, refs[base] if earlier else None, *refs[:base], *refs[used:])

    return pl.pallas_call(
        body,
        grid=(count,),
        in_specs=in_specs,
        out_specs=specs,
        out_shape=results,
        input_output_aliases=aliases,
        compiler_params=pltpu.CompilerParams(vmem_limit_bytes=VMEM_LIMIT),
        cost_estimate=cost(7 * count),
        name="attention_back",
    )(*args)


def proj_grad_body(a_ref, dqkv_ref, o_ref, dr_ref, small_ref, bias_ref, order_ref, keep_ref, send_ref, at_ref):
    step = pl.program_id(0)
    width = a_ref.shape[1]
    half = width // 2
    order = order_ref[...]

    def put(at, value):
        keep_ref[:, at] = value[:half].astype(BF16)
        send_ref[:, at] = value[half:].astype(BF16)

    @pl.when(step == 0)
    def _():
        at_ref[...] = dot(order, a_ref[...], ((1,), (1,))).astype(BF16)
        put(slice(3 * width, 4 * width), dot(dot(order, o_ref[...], ((1,), (1,))).astype(BF16), dr_ref[...]))
        table = jnp.concatenate([small_ref[...], bias_ref[...], jnp.zeros((112, width), F32)], axis=0).astype(BF16)
        put(slice(4 * width, None), dot(order, table, ((1,), (1,))))

    put(pl.ds(pl.multiple_of(step * width, 128), width), dot(at_ref[...], dqkv_ref[...]))


def proj_grad(a, dqkv, o, dr, small, bias, order, after=()):
    n, width = a.shape
    waits = len(after)
    shape = (width // 2, 4 * width + 128)
    return pl.pallas_call(
        lambda *refs: proj_grad_body(*refs[:7], *refs[7 + waits:]),
        grid=(3,),
        in_specs=[whole(a.shape), pl.BlockSpec((n, width), lambda i: (0, i)), whole(o.shape), whole(dr.shape), whole(small.shape), whole(bias.shape),
                  whole(order.shape)] + tied(waits),
        out_specs=[whole(shape)] * 2,
        out_shape=[jax.ShapeDtypeStruct(shape, BF16)] * 2,
        scratch_shapes=[pltpu.VMEM((width, n), BF16)],
        compiler_params=pltpu.CompilerParams(vmem_limit_bytes=VMEM_LIMIT),
        cost_estimate=cost(9),
        name="projection_gradients",
    )(a, dqkv, o, dr, small, bias, order, *after)


def place_body(count, to_ref, *refs):
    pieces, out_ref, sems = refs[:count], refs[count], refs[count + 1]
    copies = [pltpu.make_async_copy(piece, out_ref.at[to_ref[i]], sems.at[i]) for i, piece in enumerate(pieces)]
    for copy in copies:
        copy.start()
    for copy in copies:
        copy.wait()


def place(pieces, to, after=()):
    rows, columns = pieces[0].shape
    count, waits = len(pieces), len(after)
    out = pl.pallas_call(
        lambda *refs: place_body(count, *refs[:count + 1], *refs[count + 1 + waits:]),
        in_specs=[pl.BlockSpec(memory_space=pltpu.SMEM)] + [pl.BlockSpec(memory_space=pl.ANY)] * count + tied(waits),
        out_specs=pl.BlockSpec(memory_space=pltpu.VMEM),
        out_shape=jax.ShapeDtypeStruct((count, rows, columns), BF16),
        scratch_shapes=[pltpu.SemaphoreType.DMA((count,))],
        compiler_params=pltpu.CompilerParams(vmem_limit_bytes=VMEM_LIMIT),
        cost_estimate=cost(4),
        name="place_pieces",
    )(to, *pieces, *after)
    return out.reshape(count * rows, columns)


def place_down_body(count, to_ref, g_ref, m_ref, vec_ref, *refs):
    pieces, (w_ref, y_ref), (held_ref, act_ref, sems, act_sem, out_sem) = refs[:count], refs[count:count + 2], refs[count + 2:]
    rows = pieces[0].shape[0]
    copies = [pltpu.make_async_copy(piece, held_ref.at[pl.ds(pl.multiple_of(to_ref[i] * rows, rows), rows)], sems.at[i])
              for i, piece in enumerate(pieces)]
    copies.append(pltpu.make_async_copy(g_ref.at[pl.ds(0, act_ref.shape[0])], act_ref, act_sem))
    for copy in copies:
        copy.start()
    for copy in copies:
        copy.wait()
    out = pltpu.make_async_copy(held_ref, w_ref, out_sem)
    out.start()
    y_ref[...] = (m_ref[...] + vec_ref[7:8] + dot(act_ref[...], held_ref[...])).astype(BF16)
    out.wait()


def place_down(pieces, to, g, m, vec):
    rows, width = pieces[0].shape
    count = len(pieces)
    ff = count * rows
    n = g.shape[0]
    return pl.pallas_call(
        lambda *refs: place_down_body(count, *refs),
        grid=(1,),
        in_specs=[pl.BlockSpec(memory_space=pltpu.SMEM)] + tied(1) + [whole((n, width)), whole(vec.shape)] + tied(count),
        out_specs=[pl.BlockSpec(memory_space=pl.ANY), whole((n, width))],
        out_shape=[jax.ShapeDtypeStruct((ff, width), BF16), jax.ShapeDtypeStruct((n, width), BF16)],
        scratch_shapes=[pltpu.VMEM((ff, width), BF16), pltpu.VMEM((n, ff), BF16), pltpu.SemaphoreType.DMA((count,)),
                        pltpu.SemaphoreType.DMA(()), pltpu.SemaphoreType.DMA(())],
        compiler_params=pltpu.CompilerParams(vmem_limit_bytes=VMEM_LIMIT),
        cost_estimate=cost(10),
        name="place_and_feed_forward_down",
    )(to, g, m, vec, *pieces)


def finish_body(rows, per_row, width, *refs):
    *terms, down_ref, qkv_ref, out_ref, gain_ref, shift_ref, bias_ref, up_ref, wide_ref = refs
    wide_ref[0] = down_ref[...].astype(F32)
    total = terms[0][:rows].astype(F32)
    for term in terms[1:]:
        total = total + term[:rows].astype(F32)
    qkv_ref[0] = total[:, :3 * width]
    out_ref[0] = total[:, 3 * width:4 * width]
    small = total[:, 4 * width:]
    vectors = small.T
    gain_ref[0] = vectors[0:2]
    shift_ref[0] = vectors[2:4]
    bias_ref[0] = vectors[4:8]
    flat = rows * per_row
    spread = lax.broadcasted_iota(jnp.int32, (128, flat), 1) % per_row + 8 == lax.broadcasted_iota(jnp.int32, (128, flat), 0)
    wide = lax.dot_general(small, spread.astype(F32), (((1,), (0,)), ((), ())), precision=lax.Precision.HIGHEST, preferred_element_type=F32)
    here = lax.broadcasted_iota(jnp.int32, (rows, flat), 1) // per_row == lax.broadcasted_iota(jnp.int32, (rows, flat), 0)
    up_ref[...] = jnp.sum(jnp.where(here, wide, 0.0), axis=0, keepdims=True)


def finish(large, pieces, down, rows, per_row):
    columns = large[0].shape[1]
    width = (columns - 128) // 4
    shapes = [(1, rows, 3 * width), (1, rows, width), (1, 2, rows), (1, 2, rows), (1, 4, rows), (1, rows * per_row), (1, *down.shape)]
    return pl.pallas_call(
        lambda *refs: finish_body(rows, per_row, width, *refs),
        grid=(1,),
        in_specs=[pl.BlockSpec((2 * rows, columns), lambda i: (0, 0))] * len(large) + [whole(piece.shape) for piece in (*pieces, down)],
        out_specs=[whole(s) for s in shapes],
        out_shape=[jax.ShapeDtypeStruct(s, F32) for s in shapes],
        compiler_params=pltpu.CompilerParams(vmem_limit_bytes=VMEM_LIMIT),
        cost_estimate=cost(2),
        name="gather_projection_gradients",
    )(*large, *pieces, down)


def places(count):
    return count // 4, 2, 2


def hop(value, kind, step=1):
    zs, ys, cores = places(lax.axis_size("dp"))
    pairs = []
    for z in range(zs):
        for y in range(ys):
            for c in range(cores):
                to = {"core": (z, y, c ^ 1), "y": (z, y ^ 1, c), "z": ((z + step) % zs, y, c)}[kind]
                pairs.append(((z * ys + y) * cores + c, (to[0] * ys + to[1]) * cores + to[2]))
    return lax.ppermute(value, "dp", pairs)


def behind_me():
    zs, ys, cores = places(lax.axis_size("dp"))
    me = lax.axis_index("dp")
    return me // (cores * ys), (me // cores) % ys, me % cores


def along_line(shard):
    return [shard] + [hop(shard, "z", step) for step in range(1, places(lax.axis_size("dp"))[0])]


def both(mine, got):
    return (mine.astype(F32) + got.astype(F32)).astype(BF16)


def scatter_order(shard):
    zs, ys, cores = places(lax.axis_size("dp"))
    z, y, c = behind_me()
    row = jnp.arange(zs * ys * cores * shard)
    block = row // shard
    to = (((z + block % zs) % zs) * ys + (y ^ (block // zs % ys))) * cores + (c ^ (block // (zs * ys)))
    return (jnp.arange(zs * ys * cores * shard)[None, :] == (to * shard + row % shard)[:, None]).astype(BF16)


def y_step(mine, got):
    half = mine.shape[0] // 2
    return (mine[:half], got[:half]), hop(both(mine[half:], got[half:]), "y")


def z_step(mine, got):
    zs, _, _ = places(lax.axis_size("dp"))
    rows = got.shape[0] // zs
    terms = [[term[k * rows:k * rows + rows] for term in (*mine, got)] for k in range(zs)]
    return terms[0] + [hop(total(terms[k]).astype(BF16), "z", k) for k in range(1, zs)]


def total(terms):
    out = terms[0].astype(F32)
    for term in terms[1:]:
        out = out + term.astype(F32)
    return out


def held(value, *after):
    return lax.optimization_barrier((value, *after))[0]


def siblings(pieces, *after):
    return [hop(held(piece, *after), "core") for piece in pieces]


def places_of_pieces():
    zs, ys, cores = places(lax.axis_size("dp"))
    z, y, c = behind_me()
    to = []
    for core in (c, 1 - c):
        for row in (y, 1 - y):
            to += [(((z + zs - step) % zs) * ys + row) * cores + core for step in range(zs)]
    return jnp.stack(to).astype(jnp.int32)


def on_device(tokens, lengths, cotangent, w_qkv, w_out, w_up, w_down, norm_gain, norm_bias, bias_vec, up_bias):
    section = lax.axis_index("section")
    windows, seq, width = tokens.shape
    n = windows * seq
    shard = w_qkv.shape[1]
    per_row = up_bias.shape[1] // shard
    ff = w_up.shape[2]
    parts = 2
    part = windows // parts
    by_hand = lax.axis_size("dp") == 16
    table = jnp.concatenate([norm_gain[0], norm_bias[0], bias_vec[0]], axis=0).T
    table = jnp.concatenate([table, up_bias.reshape(shard, per_row)], axis=1)
    used = table.shape[1]
    table = jnp.pad(table, ((0, 0), (0, 128 - used)))
    packed = jnp.concatenate([w_qkv[0], w_out[0], table], axis=1)
    if by_hand:
        down = w_down[0]
        order, to = scatter_order(shard), places_of_pieces()
        wup = lax.all_gather(w_up[0], "dp", axis=0, tiled=True)
        proj_1, proj_3 = hop(packed, "z", 1), hop(packed, "z", 3)
        proj_y0, down_y0 = hop(packed, "y"), hop(down, "y")
        now = (proj_1, proj_3, proj_y0, order)
        proj_2, down_1 = hop(held(packed, *now), "z", 2), hop(held(down, *now), "z", 1)
        proj_y1, proj_y3 = hop(held(proj_1, *now), "y"), hop(held(proj_3, *now), "y")
        now = (proj_2, proj_y1, proj_y3, down_y0, down_1)
        down_3 = hop(held(down, *now), "z", 3)
        proj_y2, down_y1 = hop(held(proj_2, *now), "y"), hop(held(down_1, *now), "y")
        now = (down_3, proj_y2, down_y1)
        pieces = [packed, proj_1, proj_2, proj_3, proj_y0, proj_y1, proj_y2, proj_y3]
        proj = place(pieces + siblings(pieces, proj_y2), to)
        down_2 = hop(held(down, *now), "z", 2)
        down_y3 = hop(held(down_3, *now), "y")
    else:
        order = (jnp.arange(width)[None, :] == jnp.arange(width)[:, None]).astype(BF16)
        proj = lax.all_gather(packed, "dp", axis=0, tiled=True)
        wup = lax.all_gather(w_up[0], "dp", axis=0, tiled=True)
        wdown = lax.all_gather(w_down[0], "dp", axis=0, tiled=True)
    small = proj[:, 4 * width:4 * width + used]
    vec = small[:, :8].T.astype(F32)
    bup = small[:, 8:].reshape(1, ff).astype(F32)

    lengths = jnp.append(lengths, section)
    mid, c = attn_fwd(tokens, lengths, proj, False, after=(vec, bup))
    c = c.reshape(n, width)
    mid = mid.reshape(n, width)
    if by_hand:
        now = (down_2, down_y3, c)
        down_y2 = hop(held(down_2, *now), "y")
    act = mlp_up(c, wup, bup, 0, parts)
    if by_hand:
        pieces = [down, down_1, down_2, down_3, down_y0, down_y1, down_y2, down_y3]
        wdown, y_a = place_down(pieces + siblings(pieces, act), to, act, mid, vec)
    else:
        y_a, = mlp_fwd(c, mid, wup, wdown, bup, vec, False, 0, parts)
    y_b, = mlp_fwd(c, mid, wup, wdown, bup, vec, False, 1, parts, (y_a,))
    kept = ()
    arrived = [lax.ppermute(y.reshape(part, seq, width), "section", [(0, 1)]) for y in (y_a, y_b)]
    for at in range(parts):
        kept = attn_fwd(tokens, lengths, proj, True, at, parts, held(arrived[at], *kept[:1]), vec, kept)
    m, c, qkv, e, o, a, inv, h = kept
    c = c.reshape(n, width)
    y, g, gp, dc = mlp_both(c, m.reshape(n, width), cotangent.reshape(n, width), wup, wdown, bup, vec)
    dc = dc.reshape(tokens.shape)
    arrived = []
    for at in range(parts):
        back, = attn_bwd(dc, cotangent, m, h, qkv, e, o, inv, proj, vec, at, parts, False)
        arrived.append(lax.ppermute(back, "section", [(1, 0)]))
    dz = [jnp.where(section == 1, cotangent[:part], arrived[0])]
    dc, du = mlp_bwd(dz[0].reshape(part * seq, width), gp, wup, wdown, True, 0, parts)
    dz.append(jnp.where(section == 1, cotangent[part:], held(arrived[1], dc)))
    last = dz[1].reshape(part * seq, width)
    dz = jnp.concatenate(dz)
    g_down = down_grad(g, dz.reshape(n, width))
    sum_down = lax.psum_scatter(g_down, "dp", scatter_dimension=0, tiled=True)
    dc, keep_u, send_u, bup_u = mlp_grad(last, gp, wup, wdown, du, c, order, dc, (g_down,))
    dc = dc.reshape(tokens.shape)
    if by_hand:
        got_u = hop(send_u, "core")
        half = ff // 2
        rest = keep_u.shape[0] // 2
        mine_a, mine_b = [(keep_u[:rest, at], got_u[:rest, at]) for at in (slice(0, half), slice(half, ff))]
        send_a = both(keep_u[rest:, :half], got_u[rest:, :half])
        got_a = hop(send_a, "y")
        send_b = both(held(keep_u, send_a)[rest:, half:], held(got_u, send_a)[rest:, half:])
        got_b = hop(send_b, "y")
        back = attn_bwd(dc, dz, m, h, qkv, e, o, inv, proj, vec, 0, 1, True, (), (got_u,))
        terms_a = z_step(mine_a, held(got_a, back[3]))
        wait = (got_a,)
    else:
        back = attn_bwd(dc, dz, m, h, qkv, e, o, inv, proj, vec, 0, 1, True)
        wait = ()
    dh, dr, dqkv, smalls = back
    g_bup = bup_u[0].reshape(width, per_row).T
    keep_p, send_p = proj_grad(
        a.reshape(n, width), dqkv.reshape(n, 3 * width), o.reshape(n, width), dr.reshape(n, width), smalls, g_bup, order, wait)
    if by_hand:
        terms_b = z_step(mine_b, got_b)
        sum_up = jnp.concatenate([total(terms_a), total(terms_b)], axis=1)
        core_p = hop(held(send_p, got_b, *terms_a[3:]), "core")
        mine_p, got_p = y_step(keep_p, core_p)
        pieces = z_step(mine_p, held(got_p, *terms_b))[3:]
        *rest, sum_down = finish((keep_p, core_p, got_p), pieces, sum_down, shard, per_row)
    else:
        scatter = lambda *halves: lax.psum_scatter(jnp.concatenate(halves), "dp", scatter_dimension=0, tiled=True).astype(F32)
        sum_up = scatter(keep_u, send_u)
        sum_proj = scatter(keep_p, send_p)
        sum_down = sum_down[None].astype(F32)
        vectors = sum_proj[:, 4 * width:4 * width + 8].T
        rest = (
            sum_proj[None, :, :3 * width],
            sum_proj[None, :, 3 * width:4 * width],
            vectors[None, 0:2],
            vectors[None, 2:4],
            vectors[None, 4:8],
            sum_proj[:, 4 * width + 8:4 * width + used].reshape(1, -1),
        )
    return (y.reshape((1,) + tokens.shape), dh[None], rest[0], rest[1], sum_up[None], sum_down, *rest[2:])


def solution(mesh):
    sharded = [P("section", "dp", None)] * 4 + [P("section", None, "dp")] * 3 + [P("section", "dp")]
    windows = P("dp", None, None)
    out = P("section", "dp", None, None)
    return jax.shard_map(
        on_device, mesh=mesh, in_specs=(windows, P("dp"), windows, *sharded), out_specs=(out, out, *sharded), check_vma=False
    )
```

```python
import jax
import jax.numpy as jnp
from jax import lax
from jax.experimental import pallas as pl
from jax.experimental.pallas import tpu as pltpu
from jax.sharding import PartitionSpec as P

HEADS = 20
HEAD_DIM = 32
GROUP = 128 // HEAD_DIM
SCALE = HEAD_DIM ** -0.5
LOG2E = 1.4426950408889634
VMEM_LIMIT = 56 * 1024 * 1024
F32 = jnp.float32
BF16 = jnp.bfloat16


def cost(us):
    return pl.CostEstimate(flops=int(us * 1.1e9), bytes_accessed=1024, transcendentals=0)


def tied(count):
    return [pl.BlockSpec(memory_space=pl.ANY)] * count


def dot(a, b, dims=((1,), (0,))):
    return lax.dot_general(a, b, (dims, ((), ())), preferred_element_type=F32)


def gelu_pair(u):
    below = 0.5 + 0.5 * lax.erf(u * 0.7071067811865476)
    return u * below, below + (0.3989422804014327 * u) * jnp.exp(-0.5 * (u * u))


def normed(v, gain, shift):
    centered = v - jnp.mean(v, axis=-1, keepdims=True)
    spread = jnp.mean(centered * centered, axis=-1, keepdims=True)
    hat = centered * lax.rsqrt(spread + 1e-05)
    return hat * gain + shift


def norm_back(v, gain, grad):
    centered = v - jnp.mean(v, axis=-1, keepdims=True)
    spread = jnp.mean(centered * centered, axis=-1, keepdims=True)
    inv = lax.rsqrt(spread + 1e-05)
    hat = centered * inv
    g = grad * gain
    back = inv * (g - jnp.mean(g, axis=-1, keepdims=True) - hat * jnp.mean(g * hat, axis=-1, keepdims=True))
    return back, jnp.sum(grad * hat, axis=0, keepdims=True), jnp.sum(grad, axis=0, keepdims=True)


def attn_fwd_body(save, first_window, len_ref, h_ref, *rest):
    if save:
        arrived_ref, wqkv_ref, vec_ref, m_ref, c_ref, qkv_ref, e_ref, o_ref, a_ref, inv_ref, taken_ref = rest
    else:
        wqkv_ref, m_ref, c_ref = rest
    width = h_ref.shape[2]
    seq = h_ref.shape[1]
    length = len_ref[pl.program_id(0) + first_window]
    if save:
        taken = jnp.where(len_ref[len_ref.shape[0] - 1] == 0, h_ref[0], arrived_ref[0])
        taken_ref[0] = taken
        h = taken.astype(F32)
        vec = vec_ref[...]
    else:
        h = h_ref[0].astype(F32)
        vec = wqkv_ref[:, 4 * width:].astype(F32).T
    a = normed(h, vec[0:1], vec[2:3]).astype(BF16)
    q_all = (dot(a, wqkv_ref[:, :width]) + vec[4:5]).astype(BF16)
    k_all = dot(a, wqkv_ref[:, width:2 * width]).astype(BF16)
    v_all = (dot(a, wqkv_ref[:, 2 * width:3 * width]) + vec[5:6]).astype(BF16)
    if save:
        a_ref[0] = a
        qkv_ref[0, :, :width] = q_all
        qkv_ref[0, :, width:2 * width] = k_all
        qkv_ref[0, :, 2 * width:] = v_all
    head_of = lax.broadcasted_iota(jnp.int32, (1, 128), 1) // HEAD_DIM
    key_at = lax.broadcasted_iota(jnp.int32, (seq, 128), 0)
    lane = lax.broadcasted_iota(jnp.int32, (seq, 128), 1)
    past = jnp.where((lane == 0) & (key_at >= length), -1e30, 0.0).astype(BF16)
    first = jnp.where(lane == 0, 1.0, 0.0).astype(BF16)
    ones = jnp.ones((seq, 128), BF16)
    zero = jnp.zeros((seq, 128), BF16)
    mixed = []
    for g in range(width // 128):
        at = slice(128 * g, 128 * g + 128)
        q, v = q_all[:, at], v_all[:, at]
        k = jnp.concatenate([k_all[:, at], past], axis=1)
        acc, inv = None, None
        stacked = dot(jnp.concatenate([jnp.concatenate([jnp.where(head_of == j, q, zero), first], axis=1) for j in range(GROUP)], axis=0), k, ((1,), (1,)))
        for j in range(GROUP):
            mine = head_of == j
            s = stacked[seq * j:seq * j + seq]
            e = jnp.exp2((s - jnp.max(s, axis=1, keepdims=True)) * (SCALE * LOG2E)).astype(BF16)
            if save:
                e_ref[0, GROUP * g + j] = e
            both_parts = dot(e, jnp.concatenate([jnp.where(mine, v, zero), ones], axis=1))
            one_over = 1.0 / both_parts[:, 128:]
            part = both_parts[:, :128] * one_over
            acc = part if acc is None else acc + part
            inv = one_over if inv is None else jnp.where(mine, one_over, inv)
        mixed.append(acc.astype(BF16))
        if save:
            inv_ref[0, :, at] = inv
    o = jnp.concatenate(mixed, axis=1)
    if save:
        o_ref[0] = o
    m = h + dot(o, wqkv_ref[:, 3 * width:4 * width]) + vec[6:7]
    m_ref[0] = m
    c_ref[0] = normed(m, vec[1:2], vec[3:4]).astype(BF16)


def whole(shape):
    return pl.BlockSpec(shape, lambda *_: (0,) * len(shape))


def attn_fwd(h, lengths, proj, save, at=0, parts=1, arrived=None, vec=None, earlier=(), after=()):
    n, seq, width = h.shape
    count = n // parts
    row = lambda *tail: pl.BlockSpec((1,) + tail, lambda i, *_: (i + at * count,) + (0,) * len(tail))
    shapes = [((seq, width), F32), ((seq, width), BF16)]
    args, in_specs = [h], [row(seq, width)]
    if save:
        shapes += [((seq, 3 * width), BF16), ((HEADS, seq, seq), BF16), ((seq, width), BF16), ((seq, width), BF16), ((seq, width), F32), ((seq, width), BF16)]
        args += [arrived, proj, vec]
        in_specs += [pl.BlockSpec((1, seq, width), lambda i, *_: (i, 0, 0)), whole(proj.shape), whole(vec.shape)]
    else:
        args += [proj]
        in_specs += [whole(proj.shape)]
    used, waits = 1 + len(args), len(earlier) + len(after)
    return pl.pallas_call(
        lambda *refs: attn_fwd_body(save, at * count, *refs[:used], *refs[used + waits:]),
        grid_spec=pltpu.PrefetchScalarGridSpec(
            num_scalar_prefetch=1,
            grid=(count,),
            in_specs=in_specs + tied(waits),
            out_specs=[row(*s) for s, _ in shapes],
        ),
        out_shape=[jax.ShapeDtypeStruct((n,) + s, d) for s, d in shapes],
        input_output_aliases={used + i: i for i in range(len(earlier))},
        compiler_params=pltpu.CompilerParams(vmem_limit_bytes=VMEM_LIMIT),
        cost_estimate=cost(4.5 * count),
        name="attention_forward",
    )(lengths, *args, *earlier, *after)


def mlp_fwd_body(save, rows, c_ref, m_ref, wup_ref, wdown_ref, bup_ref, vec_ref, *outs):
    if save:
        y_ref, g_ref, gp_ref, acc_ref = outs
    else:
        y_ref, acc_ref = outs
    step = pl.program_id(0)

    @pl.when(step == 0)
    def _():
        acc_ref[...] = m_ref[...] + vec_ref[7:8]

    for r in range(c_ref.shape[0] // rows):
        at = slice(r * rows, r * rows + rows)
        u = dot(c_ref[at], wup_ref[...]) + bup_ref[...]
        act, slope = gelu_pair(u)
        act = act.astype(BF16)
        if save:
            g_ref[at] = act
            gp_ref[at] = slope.astype(BF16)
        acc_ref[at] += dot(act, wdown_ref[...])

    @pl.when(step == pl.num_programs(0) - 1)
    def _():
        y_ref[...] = acc_ref[...].astype(BF16)


def mlp_fwd(c, m, wup, wdown, bup, vec, at, parts, flag, after=(), chunk=1280, rows=256):
    n, width = c.shape
    n //= parts
    ff = wup.shape[1]
    waits = len(after)
    part = pl.BlockSpec((n, width), lambda i, flag: (at, 0))
    here = lambda i, flag: i * (1 - flag[0])

    def body(flag_ref, *refs):
        @pl.when(flag_ref[0] == 0)
        def _():
            mlp_fwd_body(False, rows, *refs[:6], *refs[6 + waits:])

    return pl.pallas_call(
        body,
        grid_spec=pltpu.PrefetchScalarGridSpec(
            num_scalar_prefetch=1,
            grid=(ff // chunk,),
            in_specs=[part, part, pl.BlockSpec((width, chunk), lambda i, flag: (0, here(i, flag))),
                      pl.BlockSpec((chunk, width), lambda i, flag: (here(i, flag), 0)),
                      pl.BlockSpec((1, chunk), lambda i, flag: (0, here(i, flag))), whole(vec.shape)] + tied(waits),
            out_specs=whole((n, width)),
            scratch_shapes=[pltpu.VMEM((n, width), F32)],
        ),
        out_shape=jax.ShapeDtypeStruct((n, width), BF16),
        compiler_params=pltpu.CompilerParams(vmem_limit_bytes=VMEM_LIMIT),
        cost_estimate=cost(13),
        name="feed_forward",
    )(flag, c, m, wup, wdown, bup, vec, *after)


def pre_grad_body(flag_ref, dz_ref, wdown_ref, dg_ref):
    @pl.when(flag_ref[0] > 0)
    def _():
        dg_ref[...] = dot(dz_ref[...], wdown_ref[...], ((1,), (1,))).astype(BF16)


def pre_grad(dz, wdown, flag, after, chunk=1280):
    n, width = dz.shape
    ff = wdown.shape[0]
    return pl.pallas_call(
        lambda *refs: pre_grad_body(*refs[:3], *refs[3 + len(after):]),
        grid_spec=pltpu.PrefetchScalarGridSpec(
            num_scalar_prefetch=1,
            grid=(ff // chunk,),
            in_specs=[pl.BlockSpec(dz.shape, lambda i, flag: (0, 0)), pl.BlockSpec((chunk, width), lambda i, flag: (i * flag[0], 0))] + tied(len(after)),
            out_specs=pl.BlockSpec((n, chunk), lambda i, flag: (0, i * flag[0])),
        ),
        out_shape=jax.ShapeDtypeStruct((n, ff), BF16),
        compiler_params=pltpu.CompilerParams(vmem_limit_bytes=VMEM_LIMIT),
        cost_estimate=cost(11),
        name="feed_forward_early_gradient",
    )(flag, dz, wdown, *after)


def mlp_both_body(rows, c_ref, m_ref, dg_ref, wup_ref, wdown_ref, bup_ref, vec_ref, y_ref, g_ref, gp_ref, dc_ref, acc_ref):
    step = pl.program_id(0)

    @pl.when(step == 0)
    def _():
        acc_ref[...] = m_ref[...] + vec_ref[7:8]
        dc_ref[...] = jnp.zeros_like(dc_ref)

    for r in range(c_ref.shape[0] // rows):
        at = slice(r * rows, r * rows + rows)
        u = dot(c_ref[at], wup_ref[...]) + bup_ref[...]
        act, slope = gelu_pair(u)
        act, slope = act.astype(BF16), slope.astype(BF16)
        g_ref[at] = act
        gp_ref[at] = slope
        acc_ref[at] += dot(act, wdown_ref[...])
        dc_ref[at] += dot((dg_ref[at].astype(F32) * slope.astype(F32)).astype(BF16), wup_ref[...], ((1,), (1,)))

    @pl.when(step == pl.num_programs(0) - 1)
    def _():
        y_ref[...] = acc_ref[...].astype(BF16)


def mlp_both(c, m, dg, wup, wdown, bup, vec, chunk=1280, rows=256):
    n, width = c.shape
    ff = wup.shape[1]
    column = pl.BlockSpec((n, chunk), lambda i: (0, i))
    return pl.pallas_call(
        lambda *refs: mlp_both_body(rows, *refs),
        grid=(ff // chunk,),
        in_specs=[whole(c.shape), whole(m.shape), column, pl.BlockSpec((width, chunk), lambda i: (0, i)),
                  pl.BlockSpec((chunk, width), lambda i: (i, 0)), pl.BlockSpec((1, chunk), lambda i: (0, i)), whole(vec.shape)],
        out_specs=[whole((n, width)), column, column, whole((n, width))],
        out_shape=[jax.ShapeDtypeStruct((n, width), BF16), jax.ShapeDtypeStruct((n, ff), BF16), jax.ShapeDtypeStruct((n, ff), BF16),
                   jax.ShapeDtypeStruct((n, width), F32)],
        scratch_shapes=[pltpu.VMEM((n, width), F32)],
        compiler_params=pltpu.CompilerParams(vmem_limit_bytes=VMEM_LIMIT),
        cost_estimate=cost(36),
        name="feed_forward_both",
    )(c, m, dg, wup, wdown, bup, vec)


def mlp_up_body(rows, c_ref, wup_ref, bup_ref, g_ref):
    for r in range(c_ref.shape[0] // rows):
        at = slice(r * rows, r * rows + rows)
        g_ref[at] = gelu_pair(dot(c_ref[at], wup_ref[...]) + bup_ref[...])[0].astype(BF16)


def mlp_up(c, wup, bup, at=0, parts=1, after=(), chunk=1280, rows=256):
    n, width = c.shape
    n //= parts
    ff = wup.shape[1]
    waits = len(after)
    return pl.pallas_call(
        lambda *refs: mlp_up_body(rows, *refs[:3], *refs[3 + waits:]),
        grid=(ff // chunk,),
        in_specs=[pl.BlockSpec((n, width), lambda i: (at, 0)), pl.BlockSpec((width, chunk), lambda i: (0, i)), pl.BlockSpec((1, chunk), lambda i: (0, i))] + tied(waits),
        out_specs=pl.BlockSpec((n, chunk), lambda i: (0, i)),
        out_shape=jax.ShapeDtypeStruct((n, ff), BF16),
        compiler_params=pltpu.CompilerParams(vmem_limit_bytes=VMEM_LIMIT),
        cost_estimate=cost(0.0125 * n),
        name="feed_forward_up",
    )(c, wup, bup, *after)


def mlp_down_body(g_ref, m_ref, wdown_ref, vec_ref, y_ref, acc_ref):
    step = pl.program_id(0)

    @pl.when(step == 0)
    def _():
        acc_ref[...] = m_ref[...] + vec_ref[7:8]

    acc_ref[...] += dot(g_ref[...], wdown_ref[...])

    @pl.when(step == pl.num_programs(0) - 1)
    def _():
        y_ref[...] = acc_ref[...].astype(BF16)


def mlp_down(g, m, wdown, vec, at, parts, after=(), chunk=1280):
    ff, width = wdown.shape
    rows = g.shape[0] // parts
    waits = len(after)
    return pl.pallas_call(
        lambda *refs: mlp_down_body(*refs[:4], *refs[4 + waits:]),
        grid=(ff // chunk,),
        in_specs=[pl.BlockSpec((rows, chunk), lambda i: (at, i)), pl.BlockSpec((rows, width), lambda i: (at, 0)),
                  pl.BlockSpec((chunk, width), lambda i: (i, 0)), whole(vec.shape)] + tied(waits),
        out_specs=whole((rows, width)),
        out_shape=jax.ShapeDtypeStruct((rows, width), BF16),
        scratch_shapes=[pltpu.VMEM((rows, width), F32)],
        compiler_params=pltpu.CompilerParams(vmem_limit_bytes=VMEM_LIMIT),
        cost_estimate=cost(0.017 * rows),
        name="feed_forward_down",
    )(g, m, wdown, vec, *after)


def mlp_bwd_body(save, rows, dz_ref, gp_ref, wup_ref, wdown_ref, dc_ref, *outs):
    @pl.when(pl.program_id(0) == 0)
    def _():
        dc_ref[...] = jnp.zeros_like(dc_ref)

    for r in range(dz_ref.shape[0] // rows):
        at = slice(r * rows, r * rows + rows)
        dg = dot(dz_ref[at], wdown_ref[...], ((1,), (1,)))
        du = (dg * gp_ref[at].astype(F32)).astype(BF16)
        if save:
            outs[0][at] = du
        dc_ref[at] += dot(du, wup_ref[...], ((1,), (1,)))


def mlp_bwd(dz, gp, wup, wdown, save, at=0, parts=1, earlier=(), after=(), chunk=1280, rows=256):
    n, width = dz.shape
    ff = wup.shape[1]
    args = [dz, gp, wup, wdown, *earlier, *after]
    outs = [jax.ShapeDtypeStruct((n * parts, width), F32)]
    specs = [pl.BlockSpec((n, width), lambda i: (at, 0))]
    if save:
        outs += [jax.ShapeDtypeStruct((n, ff), BF16)]
        specs += [pl.BlockSpec((n, chunk), lambda i: (0, i))]
    return pl.pallas_call(
        lambda *refs: mlp_bwd_body(save, rows, *refs[:4], *refs[len(args):]),
        grid=(ff // chunk,),
        in_specs=[whole(dz.shape), pl.BlockSpec((n, chunk), lambda i: (at, i)), pl.BlockSpec((width, chunk), lambda i: (0, i)),
                  pl.BlockSpec((chunk, width), lambda i: (i, 0))] + tied(len(args) - 4),
        out_specs=specs,
        out_shape=outs,
        input_output_aliases={4 + i: i for i in range(len(earlier))},
        compiler_params=pltpu.CompilerParams(vmem_limit_bytes=VMEM_LIMIT),
        cost_estimate=cost(22 / parts),
        name="feed_forward_back",
    )(*args)


def up_grad_body(c_ref, order_ref, du_ref, keep_ref, send_ref, sum_ref, ct_ref):
    half = keep_ref.shape[0]

    @pl.when(pl.program_id(0) == 0)
    def _():
        ct_ref[:2 * half] = dot(order_ref[...], c_ref[...], ((1,), (1,))).astype(BF16)
        ct_ref[2 * half:] = jnp.ones_like(ct_ref[2 * half:])

    grad = dot(ct_ref[...], du_ref[...])
    keep_ref[...] = grad[:half].astype(BF16)
    send_ref[...] = grad[half:2 * half].astype(BF16)
    sum_ref[...] = grad[2 * half:2 * half + 8]


def up_grad(c, order, du, at, parts, after=(), chunk=1280):
    n, width = c.shape
    ff = du.shape[1] // parts
    first = at * ff // chunk
    waits = len(after)
    column = lambda rows: pl.BlockSpec((rows, chunk), lambda i: (0, i))
    return pl.pallas_call(
        lambda *refs: up_grad_body(*refs[:3], *refs[3 + waits:]),
        grid=(ff // chunk,),
        in_specs=[whole(c.shape), whole(order.shape), pl.BlockSpec((n, chunk), lambda i: (0, i + first))] + tied(waits),
        out_specs=[column(width // 2), column(width // 2), column(8)],
        out_shape=[jax.ShapeDtypeStruct((width // 2, ff), BF16)] * 2 + [jax.ShapeDtypeStruct((8, ff), F32)],
        scratch_shapes=[pltpu.VMEM((width + 16, n), BF16)],
        compiler_params=pltpu.CompilerParams(vmem_limit_bytes=VMEM_LIMIT),
        cost_estimate=cost(13 / parts),
        name="up_gradient",
    )(c, order, du, *after)


def mlp_grad_body(rows, dz_ref, gp_ref, wup_ref, wdown_ref, early_ref, c_ref, order_ref, dc_ref, keep_ref, send_ref, sum_ref, du_ref, ct_ref):
    half = keep_ref.shape[0]
    count = early_ref.shape[0]

    @pl.when(pl.program_id(0) == 0)
    def _():
        dc_ref[...] = jnp.zeros_like(dc_ref)
        ct_ref[:2 * half] = dot(order_ref[...], c_ref[...], ((1,), (1,))).astype(BF16)
        ct_ref[2 * half:] = jnp.ones_like(ct_ref[2 * half:])

    for r in range(dz_ref.shape[0] // rows):
        at = slice(r * rows, r * rows + rows)
        dg = dot(dz_ref[at], wdown_ref[...], ((1,), (1,)))
        du = (dg * gp_ref[at].astype(F32)).astype(BF16)
        du_ref[at] = du
        dc_ref[at] += dot(du, wup_ref[...], ((1,), (1,)))
    grad = dot(ct_ref[:, :count], early_ref[...]) + dot(ct_ref[:, count:], du_ref[...])
    keep_ref[...] = grad[:half].astype(BF16)
    send_ref[...] = grad[half:2 * half].astype(BF16)
    sum_ref[...] = grad[2 * half:2 * half + 8]


def mlp_grad(dz, gp, wup, wdown, early, c, order, dc, after=(), chunk=1280, rows=256):
    count, width = dz.shape
    n, ff = gp.shape
    at = n // count - 1
    waits = 1 + len(after)
    column = lambda rows: pl.BlockSpec((rows, chunk), lambda i: (0, i))
    return pl.pallas_call(
        lambda *refs: mlp_grad_body(rows, *refs[:7], *refs[7 + waits:]),
        grid=(ff // chunk,),
        in_specs=[whole(dz.shape), pl.BlockSpec((count, chunk), lambda i: (at, i)), column(width), pl.BlockSpec((chunk, width), lambda i: (i, 0)),
                  column(n - count), whole(c.shape), whole(order.shape)] + tied(waits),
        out_specs=[pl.BlockSpec((count, width), lambda i: (at, 0)), column(width // 2), column(width // 2), column(8)],
        out_shape=[jax.ShapeDtypeStruct((n, width), F32)] + [jax.ShapeDtypeStruct((width // 2, ff), BF16)] * 2 + [jax.ShapeDtypeStruct((8, ff), F32)],
        scratch_shapes=[pltpu.VMEM((count, chunk), BF16), pltpu.VMEM((width + 16, n), BF16)],
        input_output_aliases={7: 0},
        compiler_params=pltpu.CompilerParams(vmem_limit_bytes=VMEM_LIMIT),
        cost_estimate=cost(21),
        name="feed_forward_gradients",
    )(dz, gp, wup, wdown, early, c, order, dc, *after)


def down_grad_body(g_ref, dz_ref, out_ref):
    out_ref[...] = dot(g_ref[...], dz_ref[...], ((0,), (0,))).astype(BF16)


def down_grad(g, dz, after=(), chunk=1280):
    n, ff = g.shape
    width = dz.shape[1]
    waits = len(after)
    return pl.pallas_call(
        lambda *refs: down_grad_body(*refs[:2], *refs[2 + waits:]),
        grid=(ff // chunk,),
        in_specs=[pl.BlockSpec((n, chunk), lambda i: (0, i)), whole(dz.shape)] + tied(waits),
        out_specs=pl.BlockSpec((chunk, width), lambda i: (i, 0)),
        out_shape=jax.ShapeDtypeStruct((ff, width), BF16),
        compiler_params=pltpu.CompilerParams(vmem_limit_bytes=VMEM_LIMIT),
        cost_estimate=cost(12),
        name="down_gradient",
    )(g, dz, *after)


def attn_bwd_body(grads, base_ref, dc_ref, dz_ref, m_ref, h_ref, qkv_ref, e_ref, o_ref, inv_ref, proj_ref, vec_ref, dh_ref, *outs):
    if grads:
        dr_ref, dqkv_ref, small_ref = outs
    width = h_ref.shape[2]
    vec = vec_ref[...]

    if grads:
        @pl.when(pl.program_id(0) == 0)
        def _():
            small_ref[...] = jnp.zeros_like(small_ref) if base_ref is None else base_ref[...]

    dz = dz_ref[0].astype(F32)
    back, g_gain1, g_shift1 = norm_back(m_ref[0], vec[1:2], dc_ref[0])
    dm = dz + back
    dr = dm.astype(BF16)
    if grads:
        dr_ref[0] = dr
    do_all = dot(dr, proj_ref[:, 3 * width:4 * width], ((1,), (1,))).astype(BF16)
    seq = h_ref.shape[1]
    head_of = lax.broadcasted_iota(jnp.int32, (1, 128), 1) // HEAD_DIM
    ones = jnp.ones((seq, 128), BF16)
    zero = jnp.zeros((seq, 128), BF16)
    dq_all, dk_all, dv_all = [], [], []
    for g in range(width // 128):
        at = slice(128 * g, 128 * g + 128)
        q = qkv_ref[0, :, 128 * g:128 * g + 128]
        k = qkv_ref[0, :, width + 128 * g:width + 128 * g + 128]
        v = jnp.concatenate([qkv_ref[0, :, 2 * width + 128 * g:2 * width + 128 * g + 128], ones], axis=1)
        scaled = do_all[:, at].astype(F32) * (inv_ref[0, :, at] * SCALE)
        do = scaled.astype(BF16)
        less = (-scaled * o_ref[0, :, at].astype(F32)).astype(BF16)
        do_t, q_t = do.T, q.T
        dq = None
        dk_t, dv_t = [], []
        stacked = dot(jnp.concatenate([jnp.concatenate([jnp.where(head_of == j, do, zero), jnp.where(head_of == j, less, zero)], axis=1)
                                       for j in range(GROUP)], axis=0), v, ((1,), (1,)))
        for j in range(GROUP):
            mine = head_of == j
            e = e_ref[0, GROUP * g + j]
            rows = slice(HEAD_DIM * j, HEAD_DIM * j + HEAD_DIM)
            dv_t.append(dot(do_t[rows], e))
            dp = stacked[seq * j:seq * j + seq]
            ds = (e.astype(F32) * dp).astype(BF16)
            part = dot(ds, jnp.where(mine, k, zero))
            dq = part if dq is None else dq + part
            dk_t.append(dot(q_t[rows], ds))
        dq_all.append(dq.astype(BF16))
        dk_all.append(jnp.concatenate(dk_t, axis=0).astype(BF16).T)
        dv_all.append((jnp.concatenate(dv_t, axis=0) * (1.0 / SCALE)).astype(BF16).T)
    dqkv = jnp.concatenate(dq_all + dk_all + dv_all, axis=1)
    if grads:
        dqkv_ref[0] = dqkv
    da = dot(dqkv, proj_ref[:, :3 * width], ((1,), (1,)))
    back, g_gain0, g_shift0 = norm_back(h_ref[0].astype(F32), vec[0:1], da)
    dh_ref[0] = (dm + back).astype(dh_ref.dtype)
    if not grads:
        return
    total = lambda x: jnp.sum(x.astype(F32), axis=0, keepdims=True)
    small_ref[...] += jnp.concatenate(
        [g_gain0, g_gain1, g_shift0, g_shift1, total(dqkv[:, :width]), total(dqkv[:, 2 * width:]), total(dr), total(dz)], axis=0)


def attn_bwd(dc, dz, m, h, qkv, e, o, inv, proj, vec, at, parts, grads, earlier=(), after=(), flag=None):
    n, seq, width = h.shape
    count = n // parts
    row = lambda *tail: pl.BlockSpec((1,) + tail, lambda i: (i + at * count,) + (0,) * len(tail))
    if grads:
        shapes = [((seq, width), F32), ((seq, width), BF16), ((seq, 3 * width), BF16)]
        specs = [row(*s) for s, _ in shapes] + [whole((8, width))]
        results = [jax.ShapeDtypeStruct((n,) + s, d) for s, d in shapes] + [jax.ShapeDtypeStruct((8, width), F32)]
    else:
        specs = [pl.BlockSpec((1, seq, width), lambda i: (i, 0, 0))]
        results = [jax.ShapeDtypeStruct((count, seq, width), BF16)]
    args = [dc, dz, m, h, qkv, e, o, inv, proj, vec]
    in_specs = [row(seq, width), row(seq, width), row(seq, width), row(seq, width), row(seq, 3 * width), row(HEADS, seq, seq),
                row(seq, width), row(seq, width), whole(proj.shape), whole(vec.shape)]
    base = len(args)
    if earlier:
        args += [earlier[3], *earlier[:3]]
        in_specs += [whole(earlier[3].shape)] + tied(3)
    aliases = {base + 1 + i: i for i in range(3)} if earlier else {}
    if flag is not None:
        args += [flag]
        in_specs += [pl.BlockSpec(memory_space=pltpu.SMEM)]
    args += after
    in_specs += tied(len(after))
    used = len(args)

    def body(*refs):
        run = lambda: attn_bwd_body(grads, refs[base] if earlier else None, *refs[:base], *refs[used:])
        if flag is None:
            run()
        else:
            pl.when(refs[base][0] > 0)(run)

    return pl.pallas_call(
        body,
        grid=(count,),
        in_specs=in_specs,
        out_specs=specs,
        out_shape=results,
        input_output_aliases=aliases,
        compiler_params=pltpu.CompilerParams(vmem_limit_bytes=VMEM_LIMIT),
        cost_estimate=cost(7 * count),
        name="attention_back",
    )(*args)


def proj_grad_body(a_ref, dqkv_ref, o_ref, dr_ref, small_ref, bias_ref, order_ref, keep_ref, send_ref, at_ref):
    step = pl.program_id(0)
    width = a_ref.shape[1]
    half = width // 2
    order = order_ref[...]

    def put(at, value):
        keep_ref[:, at] = value[:half].astype(BF16)
        send_ref[:, at] = value[half:].astype(BF16)

    @pl.when(step == 0)
    def _():
        at_ref[...] = dot(order, a_ref[...], ((1,), (1,))).astype(BF16)
        put(slice(3 * width, 4 * width), dot(dot(order, o_ref[...], ((1,), (1,))).astype(BF16), dr_ref[...]))
        table = jnp.concatenate([small_ref[...], bias_ref[...], jnp.zeros((112, width), F32)], axis=0).astype(BF16)
        put(slice(4 * width, None), dot(order, table, ((1,), (1,))))

    put(pl.ds(pl.multiple_of(step * width, 128), width), dot(at_ref[...], dqkv_ref[...]))


def proj_grad(a, dqkv, o, dr, small, bias, order, after=()):
    n, width = a.shape
    waits = len(after)
    shape = (width // 2, 4 * width + 128)
    return pl.pallas_call(
        lambda *refs: proj_grad_body(*refs[:7], *refs[7 + waits:]),
        grid=(3,),
        in_specs=[whole(a.shape), pl.BlockSpec((n, width), lambda i: (0, i)), whole(o.shape), whole(dr.shape), whole(small.shape), whole(bias.shape),
                  whole(order.shape)] + tied(waits),
        out_specs=[whole(shape)] * 2,
        out_shape=[jax.ShapeDtypeStruct(shape, BF16)] * 2,
        scratch_shapes=[pltpu.VMEM((width, n), BF16)],
        compiler_params=pltpu.CompilerParams(vmem_limit_bytes=VMEM_LIMIT),
        cost_estimate=cost(9),
        name="projection_gradients",
    )(a, dqkv, o, dr, small, bias, order, *after)


def place_body(count, to_ref, *refs):
    pieces, out_ref, sems = refs[:count], refs[count], refs[count + 1]
    copies = [pltpu.make_async_copy(piece, out_ref.at[to_ref[i]], sems.at[i]) for i, piece in enumerate(pieces)]
    for copy in copies:
        copy.start()
    for copy in copies:
        copy.wait()


def place(pieces, to, after=()):
    rows, columns = pieces[0].shape
    count, waits = len(pieces), len(after)
    out = pl.pallas_call(
        lambda *refs: place_body(count, *refs[:count + 1], *refs[count + 1 + waits:]),
        in_specs=[pl.BlockSpec(memory_space=pltpu.SMEM)] + [pl.BlockSpec(memory_space=pl.ANY)] * count + tied(waits),
        out_specs=pl.BlockSpec(memory_space=pltpu.VMEM),
        out_shape=jax.ShapeDtypeStruct((count, rows, columns), BF16),
        scratch_shapes=[pltpu.SemaphoreType.DMA((count,))],
        compiler_params=pltpu.CompilerParams(vmem_limit_bytes=VMEM_LIMIT),
        cost_estimate=cost(4),
        name="place_pieces",
    )(to, *pieces, *after)
    return out.reshape(count * rows, columns)


def place_down_body(count, to_ref, g_ref, m_ref, vec_ref, *refs):
    pieces, (w_ref, y_ref), (held_ref, act_ref, sems, act_sem, out_sem) = refs[:count], refs[count:count + 2], refs[count + 2:]
    rows = pieces[0].shape[0]
    copies = [pltpu.make_async_copy(piece, held_ref.at[pl.ds(pl.multiple_of(to_ref[i] * rows, rows), rows)], sems.at[i])
              for i, piece in enumerate(pieces)]
    copies.append(pltpu.make_async_copy(g_ref.at[pl.ds(0, act_ref.shape[0])], act_ref, act_sem))
    for copy in copies:
        copy.start()
    for copy in copies:
        copy.wait()
    out = pltpu.make_async_copy(held_ref, w_ref, out_sem)
    out.start()
    y_ref[...] = (m_ref[...] + vec_ref[7:8] + dot(act_ref[...], held_ref[...])).astype(BF16)
    out.wait()


def place_down(pieces, to, g, m, vec):
    rows, width = pieces[0].shape
    count = len(pieces)
    ff = count * rows
    n = g.shape[0]
    return pl.pallas_call(
        lambda *refs: place_down_body(count, *refs),
        grid=(1,),
        in_specs=[pl.BlockSpec(memory_space=pltpu.SMEM)] + tied(1) + [whole((n, width)), whole(vec.shape)] + tied(count),
        out_specs=[pl.BlockSpec(memory_space=pl.ANY), whole((n, width))],
        out_shape=[jax.ShapeDtypeStruct((ff, width), BF16), jax.ShapeDtypeStruct((n, width), BF16)],
        scratch_shapes=[pltpu.VMEM((ff, width), BF16), pltpu.VMEM((n, ff), BF16), pltpu.SemaphoreType.DMA((count,)),
                        pltpu.SemaphoreType.DMA(()), pltpu.SemaphoreType.DMA(())],
        compiler_params=pltpu.CompilerParams(vmem_limit_bytes=VMEM_LIMIT),
        cost_estimate=cost(10),
        name="place_and_feed_forward_down",
    )(to, g, m, vec, *pieces)


def finish_body(rows, per_row, width, *refs):
    *terms, down_ref, qkv_ref, out_ref, gain_ref, shift_ref, bias_ref, up_ref, wide_ref = refs
    wide_ref[0] = down_ref[...].astype(F32)
    total = terms[0][:rows].astype(F32)
    for term in terms[1:]:
        total = total + term[:rows].astype(F32)
    qkv_ref[0] = total[:, :3 * width]
    out_ref[0] = total[:, 3 * width:4 * width]
    small = total[:, 4 * width:]
    vectors = small.T
    gain_ref[0] = vectors[0:2]
    shift_ref[0] = vectors[2:4]
    bias_ref[0] = vectors[4:8]
    flat = rows * per_row
    spread = lax.broadcasted_iota(jnp.int32, (128, flat), 1) % per_row + 8 == lax.broadcasted_iota(jnp.int32, (128, flat), 0)
    wide = lax.dot_general(small, spread.astype(F32), (((1,), (0,)), ((), ())), precision=lax.Precision.HIGHEST, preferred_element_type=F32)
    here = lax.broadcasted_iota(jnp.int32, (rows, flat), 1) // per_row == lax.broadcasted_iota(jnp.int32, (rows, flat), 0)
    up_ref[...] = jnp.sum(jnp.where(here, wide, 0.0), axis=0, keepdims=True)


def finish(large, pieces, down, rows, per_row):
    columns = large[0].shape[1]
    width = (columns - 128) // 4
    shapes = [(1, rows, 3 * width), (1, rows, width), (1, 2, rows), (1, 2, rows), (1, 4, rows), (1, rows * per_row), (1, *down.shape)]
    return pl.pallas_call(
        lambda *refs: finish_body(rows, per_row, width, *refs),
        grid=(1,),
        in_specs=[pl.BlockSpec((2 * rows, columns), lambda i: (0, 0))] * len(large) + [whole(piece.shape) for piece in (*pieces, down)],
        out_specs=[whole(s) for s in shapes],
        out_shape=[jax.ShapeDtypeStruct(s, F32) for s in shapes],
        compiler_params=pltpu.CompilerParams(vmem_limit_bytes=VMEM_LIMIT),
        cost_estimate=cost(2),
        name="gather_projection_gradients",
    )(*large, *pieces, down)


def places(count):
    return count // 4, 2, 2


def hop(value, kind, step=1):
    zs, ys, cores = places(lax.axis_size("dp"))
    pairs = []
    for z in range(zs):
        for y in range(ys):
            for c in range(cores):
                to = {"core": (z, y, c ^ 1), "y": (z, y ^ 1, c), "z": ((z + step) % zs, y, c)}[kind]
                pairs.append(((z * ys + y) * cores + c, (to[0] * ys + to[1]) * cores + to[2]))
    return lax.ppermute(value, "dp", pairs)


def behind_me():
    zs, ys, cores = places(lax.axis_size("dp"))
    me = lax.axis_index("dp")
    return me // (cores * ys), (me // cores) % ys, me % cores


def along_line(shard):
    return [shard] + [hop(shard, "z", step) for step in range(1, places(lax.axis_size("dp"))[0])]


def both(mine, got):
    return (mine.astype(F32) + got.astype(F32)).astype(BF16)


def scatter_order(shard):
    zs, ys, cores = places(lax.axis_size("dp"))
    z, y, c = behind_me()
    row = jnp.arange(zs * ys * cores * shard)
    block = row // shard
    to = (((z + block % zs) % zs) * ys + (y ^ (block // zs % ys))) * cores + (c ^ (block // (zs * ys)))
    return (jnp.arange(zs * ys * cores * shard)[None, :] == (to * shard + row % shard)[:, None]).astype(BF16)


def y_step(mine, got):
    half = mine.shape[0] // 2
    return (mine[:half], got[:half]), hop(both(mine[half:], got[half:]), "y")


def z_step(mine, got):
    zs, _, _ = places(lax.axis_size("dp"))
    rows = got.shape[0] // zs
    terms = [[term[k * rows:k * rows + rows] for term in (*mine, got)] for k in range(zs)]
    return terms[0] + [hop(total(terms[k]).astype(BF16), "z", k) for k in range(1, zs)]


def total(terms):
    out = terms[0].astype(F32)
    for term in terms[1:]:
        out = out + term.astype(F32)
    return out


def held(value, *after):
    return lax.optimization_barrier((value, *after))[0]


def siblings(pieces, *after):
    return [hop(held(piece, *after), "core") for piece in pieces]


def places_of_pieces():
    zs, ys, cores = places(lax.axis_size("dp"))
    z, y, c = behind_me()
    to = []
    for core in (c, 1 - c):
        for row in (y, 1 - y):
            to += [(((z + zs - step) % zs) * ys + row) * cores + core for step in range(zs)]
    return jnp.stack(to).astype(jnp.int32)


def on_device(tokens, lengths, cotangent, w_qkv, w_out, w_up, w_down, norm_gain, norm_bias, bias_vec, up_bias):
    section = lax.axis_index("section")
    windows, seq, width = tokens.shape
    n = windows * seq
    shard = w_qkv.shape[1]
    per_row = up_bias.shape[1] // shard
    ff = w_up.shape[2]
    parts = 2
    part = windows // parts
    by_hand = lax.axis_size("dp") == 16
    table = jnp.concatenate([norm_gain[0], norm_bias[0], bias_vec[0]], axis=0).T
    table = jnp.concatenate([table, up_bias.reshape(shard, per_row)], axis=1)
    used = table.shape[1]
    table = jnp.pad(table, ((0, 0), (0, 128 - used)))
    packed = jnp.concatenate([w_qkv[0], w_out[0], table], axis=1)
    if by_hand:
        down = w_down[0]
        order, to = scatter_order(shard), places_of_pieces()
        wup = lax.all_gather(w_up[0], "dp", axis=0, tiled=True)
        proj_1, proj_3 = hop(packed, "z", 1), hop(packed, "z", 3)
        proj_y0, down_y0 = hop(packed, "y"), hop(down, "y")
        now = (proj_1, proj_3, proj_y0, order)
        proj_2, down_1 = hop(held(packed, *now), "z", 2), hop(held(down, *now), "z", 1)
        proj_y1, proj_y3 = hop(held(proj_1, *now), "y"), hop(held(proj_3, *now), "y")
        now = (proj_2, proj_y1, proj_y3, down_y0, down_1)
        down_3 = hop(held(down, *now), "z", 3)
        proj_y2, down_y1 = hop(held(proj_2, *now), "y"), hop(held(down_1, *now), "y")
        now = (down_3, proj_y2, down_y1)
        pieces = [packed, proj_1, proj_2, proj_3, proj_y0, proj_y1, proj_y2, proj_y3]
        proj = place(pieces + siblings(pieces, proj_y2), to)
        down_2 = hop(held(down, *now), "z", 2)
        down_y3 = hop(held(down_3, *now), "y")
    else:
        order = (jnp.arange(width)[None, :] == jnp.arange(width)[:, None]).astype(BF16)
        proj = lax.all_gather(packed, "dp", axis=0, tiled=True)
        wup = lax.all_gather(w_up[0], "dp", axis=0, tiled=True)
        wdown = lax.all_gather(w_down[0], "dp", axis=0, tiled=True)
    small = proj[:, 4 * width:4 * width + used]
    vec = small[:, :8].T.astype(F32)
    bup = small[:, 8:].reshape(1, ff).astype(F32)

    lengths = jnp.append(lengths, section)
    mid, c = attn_fwd(tokens, lengths, proj, False, after=(vec, bup))
    c = c.reshape(n, width)
    mid = mid.reshape(n, width)
    if by_hand:
        now = (down_2, down_y3, c)
        down_y2 = hop(held(down_2, *now), "y")
    act = mlp_up(c, wup, bup, 0, parts)
    if by_hand:
        pieces = [down, down_1, down_2, down_3, down_y0, down_y1, down_y2, down_y3]
        wdown, y_a = place_down(pieces + siblings(pieces, act), to, act, mid, vec)
    else:
        y_a = mlp_down(act, mid[:n // parts], wdown, vec, 0, 1)
    flag = section.reshape(1).astype(jnp.int32)
    early = pre_grad(cotangent.reshape(n, width), wdown, flag, (y_a,))
    y_b = mlp_fwd(c, mid, wup, wdown, bup, vec, 1, parts, flag, (early,))
    kept = ()
    arrived = [lax.ppermute(y.reshape(part, seq, width), "section", [(0, 1)]) for y in (y_a, y_b)]
    for at in range(parts):
        kept = attn_fwd(tokens, lengths, proj, True, at, parts, held(arrived[at], *kept[:1]), vec, kept)
    m, c, qkv, e, o, a, inv, h = kept
    c = c.reshape(n, width)
    y, g, gp, dc = mlp_both(c, m.reshape(n, width), early, wup, wdown, bup, vec)
    dc = dc.reshape(tokens.shape)
    arrived = []
    for at in range(parts):
        back, = attn_bwd(dc, cotangent, m, h, qkv, e, o, inv, proj, vec, at, parts, False, flag=flag)
        arrived.append(lax.ppermute(back, "section", [(1, 0)]))
    dz = [jnp.where(section == 1, cotangent[:part], arrived[0])]
    dc, du = mlp_bwd(dz[0].reshape(part * seq, width), gp, wup, wdown, True, 0, parts)
    dz.append(jnp.where(section == 1, cotangent[part:], held(arrived[1], dc)))
    last = dz[1].reshape(part * seq, width)
    dz = jnp.concatenate(dz)
    g_down = down_grad(g, dz.reshape(n, width))
    sum_down = lax.psum_scatter(g_down, "dp", scatter_dimension=0, tiled=True)
    dc, keep_u, send_u, bup_u = mlp_grad(last, gp, wup, wdown, du, c, order, dc, (g_down,))
    dc = dc.reshape(tokens.shape)
    if by_hand:
        got_u = hop(send_u, "core")
        half = ff // 2
        rest = keep_u.shape[0] // 2
        mine_a, mine_b = [(keep_u[:rest, at], got_u[:rest, at]) for at in (slice(0, half), slice(half, ff))]
        send_a = both(keep_u[rest:, :half], got_u[rest:, :half])
        got_a = hop(send_a, "y")
        send_b = both(held(keep_u, send_a)[rest:, half:], held(got_u, send_a)[rest:, half:])
        got_b = hop(send_b, "y")
        back = attn_bwd(dc, dz, m, h, qkv, e, o, inv, proj, vec, 0, 1, True, (), (got_u,))
        terms_a = z_step(mine_a, held(got_a, back[3]))
        wait = (got_a,)
    else:
        back = attn_bwd(dc, dz, m, h, qkv, e, o, inv, proj, vec, 0, 1, True)
        wait = ()
    dh, dr, dqkv, smalls = back
    g_bup = bup_u[0].reshape(width, per_row).T
    keep_p, send_p = proj_grad(
        a.reshape(n, width), dqkv.reshape(n, 3 * width), o.reshape(n, width), dr.reshape(n, width), smalls, g_bup, order, wait)
    if by_hand:
        terms_b = z_step(mine_b, got_b)
        sum_up = jnp.concatenate([total(terms_a), total(terms_b)], axis=1)
        core_p = hop(held(send_p, got_b, *terms_a[3:]), "core")
        mine_p, got_p = y_step(keep_p, core_p)
        pieces = z_step(mine_p, held(got_p, *terms_b))[3:]
        *rest, sum_down = finish((keep_p, core_p, got_p), pieces, sum_down, shard, per_row)
    else:
        scatter = lambda *halves: lax.psum_scatter(jnp.concatenate(halves), "dp", scatter_dimension=0, tiled=True).astype(F32)
        sum_up = scatter(keep_u, send_u)
        sum_proj = scatter(keep_p, send_p)
        sum_down = sum_down[None].astype(F32)
        vectors = sum_proj[:, 4 * width:4 * width + 8].T
        rest = (
            sum_proj[None, :, :3 * width],
            sum_proj[None, :, 3 * width:4 * width],
            vectors[None, 0:2],
            vectors[None, 2:4],
            vectors[None, 4:8],
            sum_proj[:, 4 * width + 8:4 * width + used].reshape(1, -1),
        )
    return (y.reshape((1,) + tokens.shape), dh[None], rest[0], rest[1], sum_up[None], sum_down, *rest[2:])


def solution(mesh):
    sharded = [P("section", "dp", None)] * 4 + [P("section", None, "dp")] * 3 + [P("section", "dp")]
    windows = P("dp", None, None)
    out = P("section", "dp", None, None)
    return jax.shard_map(
        on_device, mesh=mesh, in_specs=(windows, P("dp"), windows, *sharded), out_specs=(out, out, *sharded), check_vma=False
    )
```

```python
import jax
import jax.numpy as jnp
from jax import lax
from jax.experimental import pallas as pl
from jax.experimental.pallas import tpu as pltpu
from jax.sharding import PartitionSpec as P

HEADS = 20
HEAD_DIM = 32
GROUP = 128 // HEAD_DIM
SCALE = HEAD_DIM ** -0.5
LOG2E = 1.4426950408889634
VMEM_LIMIT = 56 * 1024 * 1024
F32 = jnp.float32
BF16 = jnp.bfloat16


def cost(us):
    return pl.CostEstimate(flops=int(us * 1.1e9), bytes_accessed=1024, transcendentals=0)


def tied(count):
    return [pl.BlockSpec(memory_space=pl.ANY)] * count


def dot(a, b, dims=((1,), (0,))):
    return lax.dot_general(a, b, (dims, ((), ())), preferred_element_type=F32)


def gelu_pair(u):
    below = 0.5 + 0.5 * lax.erf(u * 0.7071067811865476)
    return u * below, below + (0.3989422804014327 * u) * jnp.exp(-0.5 * (u * u))


def normed(v, gain, shift):
    centered = v - jnp.mean(v, axis=-1, keepdims=True)
    spread = jnp.mean(centered * centered, axis=-1, keepdims=True)
    hat = centered * lax.rsqrt(spread + 1e-05)
    return hat * gain + shift


def norm_back(v, gain, grad):
    centered = v - jnp.mean(v, axis=-1, keepdims=True)
    spread = jnp.mean(centered * centered, axis=-1, keepdims=True)
    inv = lax.rsqrt(spread + 1e-05)
    hat = centered * inv
    g = grad * gain
    back = inv * (g - jnp.mean(g, axis=-1, keepdims=True) - hat * jnp.mean(g * hat, axis=-1, keepdims=True))
    return back, jnp.sum(grad * hat, axis=0, keepdims=True), jnp.sum(grad, axis=0, keepdims=True)


def attn_fwd_body(save, first_window, len_ref, h_ref, *rest):
    if save:
        arrived_ref, wqkv_ref, vec_ref, m_ref, c_ref, qkv_ref, e_ref, o_ref, a_ref, inv_ref, taken_ref = rest
    else:
        wqkv_ref, m_ref, c_ref = rest
    width = h_ref.shape[2]
    seq = h_ref.shape[1]
    length = len_ref[pl.program_id(0) + first_window]
    if save:
        taken = jnp.where(len_ref[len_ref.shape[0] - 1] == 0, h_ref[0], arrived_ref[0])
        taken_ref[0] = taken
        h = taken.astype(F32)
        vec = vec_ref[...]
    else:
        h = h_ref[0].astype(F32)
        vec = wqkv_ref[:, 4 * width:].astype(F32).T
    a = normed(h, vec[0:1], vec[2:3]).astype(BF16)
    q_all = (dot(a, wqkv_ref[:, :width]) + vec[4:5]).astype(BF16)
    k_all = dot(a, wqkv_ref[:, width:2 * width]).astype(BF16)
    v_all = (dot(a, wqkv_ref[:, 2 * width:3 * width]) + vec[5:6]).astype(BF16)
    if save:
        a_ref[0] = a
        qkv_ref[0, :, :width] = q_all
        qkv_ref[0, :, width:2 * width] = k_all
        qkv_ref[0, :, 2 * width:] = v_all
    head_of = lax.broadcasted_iota(jnp.int32, (1, 128), 1) // HEAD_DIM
    key_at = lax.broadcasted_iota(jnp.int32, (seq, 128), 0)
    lane = lax.broadcasted_iota(jnp.int32, (seq, 128), 1)
    past = jnp.where((lane == 0) & (key_at >= length), -1e30, 0.0).astype(BF16)
    first = jnp.where(lane == 0, 1.0, 0.0).astype(BF16)
    ones = jnp.ones((seq, 128), BF16)
    zero = jnp.zeros((seq, 128), BF16)
    mixed = []
    for g in range(width // 128):
        at = slice(128 * g, 128 * g + 128)
        q, v = q_all[:, at], v_all[:, at]
        k = jnp.concatenate([k_all[:, at], past], axis=1)
        acc, inv = None, None
        stacked = dot(jnp.concatenate([jnp.concatenate([jnp.where(head_of == j, q, zero), first], axis=1) for j in range(GROUP)], axis=0), k, ((1,), (1,)))
        for j in range(GROUP):
            mine = head_of == j
            s = stacked[seq * j:seq * j + seq]
            e = jnp.exp2((s - jnp.max(s, axis=1, keepdims=True)) * (SCALE * LOG2E)).astype(BF16)
            if save:
                e_ref[0, GROUP * g + j] = e
            both_parts = dot(e, jnp.concatenate([jnp.where(mine, v, zero), ones], axis=1))
            one_over = 1.0 / both_parts[:, 128:]
            part = both_parts[:, :128] * one_over
            acc = part if acc is None else acc + part
            inv = one_over if inv is None else jnp.where(mine, one_over, inv)
        mixed.append(acc.astype(BF16))
        if save:
            inv_ref[0, :, at] = inv
    o = jnp.concatenate(mixed, axis=1)
    if save:
        o_ref[0] = o
    m = h + dot(o, wqkv_ref[:, 3 * width:4 * width]) + vec[6:7]
    m_ref[0] = m
    c_ref[0] = normed(m, vec[1:2], vec[3:4]).astype(BF16)


def whole(shape):
    return pl.BlockSpec(shape, lambda *_: (0,) * len(shape))


def attn_fwd(h, lengths, proj, save, at=0, parts=1, arrived=None, vec=None, earlier=(), after=()):
    n, seq, width = h.shape
    count = n // parts
    row = lambda *tail: pl.BlockSpec((1,) + tail, lambda i, *_: (i + at * count,) + (0,) * len(tail))
    shapes = [((seq, width), F32), ((seq, width), BF16)]
    args, in_specs = [h], [row(seq, width)]
    if save:
        shapes += [((seq, 3 * width), BF16), ((HEADS, seq, seq), BF16), ((seq, width), BF16), ((seq, width), BF16), ((seq, width), F32), ((seq, width), BF16)]
        args += [arrived, proj, vec]
        in_specs += [pl.BlockSpec((1, seq, width), lambda i, *_: (i, 0, 0)), whole(proj.shape), whole(vec.shape)]
    else:
        args += [proj]
        in_specs += [whole(proj.shape)]
    used, waits = 1 + len(args), len(earlier) + len(after)
    return pl.pallas_call(
        lambda *refs: attn_fwd_body(save, at * count, *refs[:used], *refs[used + waits:]),
        grid_spec=pltpu.PrefetchScalarGridSpec(
            num_scalar_prefetch=1,
            grid=(count,),
            in_specs=in_specs + tied(waits),
            out_specs=[row(*s) for s, _ in shapes],
        ),
        out_shape=[jax.ShapeDtypeStruct((n,) + s, d) for s, d in shapes],
        input_output_aliases={used + i: i for i in range(len(earlier))},
        compiler_params=pltpu.CompilerParams(vmem_limit_bytes=VMEM_LIMIT),
        cost_estimate=cost(4.5 * count),
        name="attention_forward",
    )(lengths, *args, *earlier, *after)


def mlp_fwd_body(save, rows, c_ref, m_ref, wup_ref, wdown_ref, bup_ref, vec_ref, *outs):
    if save:
        y_ref, g_ref, gp_ref, acc_ref = outs
    else:
        y_ref, acc_ref = outs
    step = pl.program_id(0)

    @pl.when(step == 0)
    def _():
        acc_ref[...] = m_ref[...] + vec_ref[7:8]

    for r in range(c_ref.shape[0] // rows):
        at = slice(r * rows, r * rows + rows)
        u = dot(c_ref[at], wup_ref[...]) + bup_ref[...]
        act, slope = gelu_pair(u)
        act = act.astype(BF16)
        if save:
            g_ref[at] = act
            gp_ref[at] = slope.astype(BF16)
        acc_ref[at] += dot(act, wdown_ref[...])

    @pl.when(step == pl.num_programs(0) - 1)
    def _():
        y_ref[...] = acc_ref[...].astype(BF16)


def mlp_fwd_skip_body(chunk, rows, flag_ref, c_ref, m_ref, vec_ref, wup_ref, wdown_ref, bup_ref, y_ref, acc_ref):
    def block(wup, wdown, bup):
        for r in range(c_ref.shape[0] // rows):
            at = slice(r * rows, r * rows + rows)
            act = gelu_pair(dot(c_ref[at], wup[...]) + bup[...])[0].astype(BF16)
            acc_ref[at] += dot(act, wdown[...])

    @pl.when(flag_ref[0] == 0)
    def _():
        width, ff = wup_ref.shape
        acc_ref[...] = m_ref[...] + vec_ref[7:8]
        pltpu.emit_pipeline(
            block,
            grid=(ff // chunk,),
            in_specs=[pl.BlockSpec((width, chunk), lambda i: (0, i)), pl.BlockSpec((chunk, width), lambda i: (i, 0)),
                      pl.BlockSpec((1, chunk), lambda i: (0, i))],
        )(wup_ref, wdown_ref, bup_ref)
        y_ref[...] = acc_ref[...].astype(BF16)


def mlp_fwd(c, m, wup, wdown, bup, vec, at, parts, flag, after=(), chunk=1280, rows=256):
    n, width = c.shape
    n //= parts
    part = pl.BlockSpec((n, width), lambda i: (at, 0))
    return pl.pallas_call(
        lambda *refs: mlp_fwd_skip_body(chunk, rows, *refs[:7], *refs[7 + len(after):]),
        grid=(1,),
        in_specs=[pl.BlockSpec(memory_space=pltpu.SMEM), part, part, whole(vec.shape)] + tied(3 + len(after)),
        out_specs=whole((n, width)),
        out_shape=jax.ShapeDtypeStruct((n, width), BF16),
        scratch_shapes=[pltpu.VMEM((n, width), F32)],
        compiler_params=pltpu.CompilerParams(vmem_limit_bytes=VMEM_LIMIT),
        cost_estimate=cost(13),
        name="feed_forward",
    )(flag, c, m, vec, wup, wdown, bup, *after)


def pre_grad_body(chunk, flag_ref, dz_ref, wdown_ref, dg_ref):
    def block(dz, weights, out):
        out[...] = dot(dz[...], weights[...], ((1,), (1,))).astype(BF16)

    @pl.when(flag_ref[0] > 0)
    def _():
        n, width = dz_ref.shape
        pltpu.emit_pipeline(
            block,
            grid=(wdown_ref.shape[0] // chunk,),
            in_specs=[pl.BlockSpec((n, width), lambda i: (0, 0)), pl.BlockSpec((chunk, width), lambda i: (i, 0))],
            out_specs=[pl.BlockSpec((n, chunk), lambda i: (0, i))],
        )(dz_ref, wdown_ref, dg_ref)


def pre_grad(dz, wdown, flag, after, chunk=1280):
    n, width = dz.shape
    ff = wdown.shape[0]
    return pl.pallas_call(
        lambda *refs: pre_grad_body(chunk, *refs[:3], *refs[3 + len(after):]),
        in_specs=[pl.BlockSpec(memory_space=pltpu.SMEM)] + tied(2 + len(after)),
        out_specs=pl.BlockSpec(memory_space=pl.ANY),
        out_shape=jax.ShapeDtypeStruct((n, ff), BF16),
        compiler_params=pltpu.CompilerParams(vmem_limit_bytes=VMEM_LIMIT),
        cost_estimate=cost(11),
        name="feed_forward_early_gradient",
    )(flag, dz, wdown, *after)


def mlp_both_body(rows, c_ref, m_ref, dg_ref, wup_ref, wdown_ref, bup_ref, vec_ref, y_ref, g_ref, gp_ref, dc_ref, acc_ref):
    step = pl.program_id(0)

    @pl.when(step == 0)
    def _():
        acc_ref[...] = m_ref[...] + vec_ref[7:8]
        dc_ref[...] = jnp.zeros_like(dc_ref)

    for r in range(c_ref.shape[0] // rows):
        at = slice(r * rows, r * rows + rows)
        u = dot(c_ref[at], wup_ref[...]) + bup_ref[...]
        act, slope = gelu_pair(u)
        act, slope = act.astype(BF16), slope.astype(BF16)
        g_ref[at] = act
        gp_ref[at] = slope
        acc_ref[at] += dot(act, wdown_ref[...])
        dc_ref[at] += dot((dg_ref[at].astype(F32) * slope.astype(F32)).astype(BF16), wup_ref[...], ((1,), (1,)))

    @pl.when(step == pl.num_programs(0) - 1)
    def _():
        y_ref[...] = acc_ref[...].astype(BF16)


def mlp_both(c, m, dg, wup, wdown, bup, vec, chunk=1280, rows=256):
    n, width = c.shape
    ff = wup.shape[1]
    column = pl.BlockSpec((n, chunk), lambda i: (0, i))
    return pl.pallas_call(
        lambda *refs: mlp_both_body(rows, *refs),
        grid=(ff // chunk,),
        in_specs=[whole(c.shape), whole(m.shape), column, pl.BlockSpec((width, chunk), lambda i: (0, i)),
                  pl.BlockSpec((chunk, width), lambda i: (i, 0)), pl.BlockSpec((1, chunk), lambda i: (0, i)), whole(vec.shape)],
        out_specs=[whole((n, width)), column, column, whole((n, width))],
        out_shape=[jax.ShapeDtypeStruct((n, width), BF16), jax.ShapeDtypeStruct((n, ff), BF16), jax.ShapeDtypeStruct((n, ff), BF16),
                   jax.ShapeDtypeStruct((n, width), F32)],
        scratch_shapes=[pltpu.VMEM((n, width), F32)],
        compiler_params=pltpu.CompilerParams(vmem_limit_bytes=VMEM_LIMIT),
        cost_estimate=cost(36),
        name="feed_forward_both",
    )(c, m, dg, wup, wdown, bup, vec)


def mlp_up_body(rows, c_ref, wup_ref, bup_ref, g_ref):
    for r in range(c_ref.shape[0] // rows):
        at = slice(r * rows, r * rows + rows)
        g_ref[at] = gelu_pair(dot(c_ref[at], wup_ref[...]) + bup_ref[...])[0].astype(BF16)


def mlp_up(c, wup, bup, at=0, parts=1, after=(), chunk=1280, rows=256):
    n, width = c.shape
    n //= parts
    ff = wup.shape[1]
    waits = len(after)
    return pl.pallas_call(
        lambda *refs: mlp_up_body(rows, *refs[:3], *refs[3 + waits:]),
        grid=(ff // chunk,),
        in_specs=[pl.BlockSpec((n, width), lambda i: (at, 0)), pl.BlockSpec((width, chunk), lambda i: (0, i)), pl.BlockSpec((1, chunk), lambda i: (0, i))] + tied(waits),
        out_specs=pl.BlockSpec((n, chunk), lambda i: (0, i)),
        out_shape=jax.ShapeDtypeStruct((n, ff), BF16),
        compiler_params=pltpu.CompilerParams(vmem_limit_bytes=VMEM_LIMIT),
        cost_estimate=cost(0.0125 * n),
        name="feed_forward_up",
    )(c, wup, bup, *after)


def mlp_down_body(g_ref, m_ref, wdown_ref, vec_ref, y_ref, acc_ref):
    step = pl.program_id(0)

    @pl.when(step == 0)
    def _():
        acc_ref[...] = m_ref[...] + vec_ref[7:8]

    acc_ref[...] += dot(g_ref[...], wdown_ref[...])

    @pl.when(step == pl.num_programs(0) - 1)
    def _():
        y_ref[...] = acc_ref[...].astype(BF16)


def mlp_down(g, m, wdown, vec, at, parts, after=(), chunk=1280):
    ff, width = wdown.shape
    rows = g.shape[0] // parts
    waits = len(after)
    return pl.pallas_call(
        lambda *refs: mlp_down_body(*refs[:4], *refs[4 + waits:]),
        grid=(ff // chunk,),
        in_specs=[pl.BlockSpec((rows, chunk), lambda i: (at, i)), pl.BlockSpec((rows, width), lambda i: (at, 0)),
                  pl.BlockSpec((chunk, width), lambda i: (i, 0)), whole(vec.shape)] + tied(waits),
        out_specs=whole((rows, width)),
        out_shape=jax.ShapeDtypeStruct((rows, width), BF16),
        scratch_shapes=[pltpu.VMEM((rows, width), F32)],
        compiler_params=pltpu.CompilerParams(vmem_limit_bytes=VMEM_LIMIT),
        cost_estimate=cost(0.017 * rows),
        name="feed_forward_down",
    )(g, m, wdown, vec, *after)


def mlp_bwd_body(save, rows, dz_ref, gp_ref, wup_ref, wdown_ref, dc_ref, *outs):
    @pl.when(pl.program_id(0) == 0)
    def _():
        dc_ref[...] = jnp.zeros_like(dc_ref)

    for r in range(dz_ref.shape[0] // rows):
        at = slice(r * rows, r * rows + rows)
        dg = dot(dz_ref[at], wdown_ref[...], ((1,), (1,)))
        du = (dg * gp_ref[at].astype(F32)).astype(BF16)
        if save:
            outs[0][at] = du
        dc_ref[at] += dot(du, wup_ref[...], ((1,), (1,)))


def mlp_bwd(dz, gp, wup, wdown, save, at=0, parts=1, earlier=(), after=(), chunk=1280, rows=256):
    n, width = dz.shape
    ff = wup.shape[1]
    args = [dz, gp, wup, wdown, *earlier, *after]
    outs = [jax.ShapeDtypeStruct((n * parts, width), F32)]
    specs = [pl.BlockSpec((n, width), lambda i: (at, 0))]
    if save:
        outs += [jax.ShapeDtypeStruct((n, ff), BF16)]
        specs += [pl.BlockSpec((n, chunk), lambda i: (0, i))]
    return pl.pallas_call(
        lambda *refs: mlp_bwd_body(save, rows, *refs[:4], *refs[len(args):]),
        grid=(ff // chunk,),
        in_specs=[whole(dz.shape), pl.BlockSpec((n, chunk), lambda i: (at, i)), pl.BlockSpec((width, chunk), lambda i: (0, i)),
                  pl.BlockSpec((chunk, width), lambda i: (i, 0))] + tied(len(args) - 4),
        out_specs=specs,
        out_shape=outs,
        input_output_aliases={4 + i: i for i in range(len(earlier))},
        compiler_params=pltpu.CompilerParams(vmem_limit_bytes=VMEM_LIMIT),
        cost_estimate=cost(22 / parts),
        name="feed_forward_back",
    )(*args)


def up_grad_body(c_ref, order_ref, du_ref, keep_ref, send_ref, sum_ref, ct_ref):
    half = keep_ref.shape[0]

    @pl.when(pl.program_id(0) == 0)
    def _():
        ct_ref[:2 * half] = dot(order_ref[...], c_ref[...], ((1,), (1,))).astype(BF16)
        ct_ref[2 * half:] = jnp.ones_like(ct_ref[2 * half:])

    grad = dot(ct_ref[...], du_ref[...])
    keep_ref[...] = grad[:half].astype(BF16)
    send_ref[...] = grad[half:2 * half].astype(BF16)
    sum_ref[...] = grad[2 * half:2 * half + 8]


def up_grad(c, order, du, at, parts, after=(), chunk=1280):
    n, width = c.shape
    ff = du.shape[1] // parts
    first = at * ff // chunk
    waits = len(after)
    column = lambda rows: pl.BlockSpec((rows, chunk), lambda i: (0, i))
    return pl.pallas_call(
        lambda *refs: up_grad_body(*refs[:3], *refs[3 + waits:]),
        grid=(ff // chunk,),
        in_specs=[whole(c.shape), whole(order.shape), pl.BlockSpec((n, chunk), lambda i: (0, i + first))] + tied(waits),
        out_specs=[column(width // 2), column(width // 2), column(8)],
        out_shape=[jax.ShapeDtypeStruct((width // 2, ff), BF16)] * 2 + [jax.ShapeDtypeStruct((8, ff), F32)],
        scratch_shapes=[pltpu.VMEM((width + 16, n), BF16)],
        compiler_params=pltpu.CompilerParams(vmem_limit_bytes=VMEM_LIMIT),
        cost_estimate=cost(13 / parts),
        name="up_gradient",
    )(c, order, du, *after)


def mlp_grad_body(rows, dz_ref, gp_ref, wup_ref, wdown_ref, early_ref, c_ref, order_ref, dc_ref, keep_ref, send_ref, sum_ref, du_ref, ct_ref):
    half = keep_ref.shape[0]
    count = early_ref.shape[0]

    @pl.when(pl.program_id(0) == 0)
    def _():
        dc_ref[...] = jnp.zeros_like(dc_ref)
        ct_ref[:2 * half] = dot(order_ref[...], c_ref[...], ((1,), (1,))).astype(BF16)
        ct_ref[2 * half:] = jnp.ones_like(ct_ref[2 * half:])

    for r in range(dz_ref.shape[0] // rows):
        at = slice(r * rows, r * rows + rows)
        dg = dot(dz_ref[at], wdown_ref[...], ((1,), (1,)))
        du = (dg * gp_ref[at].astype(F32)).astype(BF16)
        du_ref[at] = du
        dc_ref[at] += dot(du, wup_ref[...], ((1,), (1,)))
    grad = dot(ct_ref[:, :count], early_ref[...]) + dot(ct_ref[:, count:], du_ref[...])
    keep_ref[...] = grad[:half].astype(BF16)
    send_ref[...] = grad[half:2 * half].astype(BF16)
    sum_ref[...] = grad[2 * half:2 * half + 8]


def mlp_grad(dz, gp, wup, wdown, early, c, order, dc, after=(), chunk=1280, rows=256):
    count, width = dz.shape
    n, ff = gp.shape
    at = n // count - 1
    waits = 1 + len(after)
    column = lambda rows: pl.BlockSpec((rows, chunk), lambda i: (0, i))
    return pl.pallas_call(
        lambda *refs: mlp_grad_body(rows, *refs[:7], *refs[7 + waits:]),
        grid=(ff // chunk,),
        in_specs=[whole(dz.shape), pl.BlockSpec((count, chunk), lambda i: (at, i)), column(width), pl.BlockSpec((chunk, width), lambda i: (i, 0)),
                  column(n - count), whole(c.shape), whole(order.shape)] + tied(waits),
        out_specs=[pl.BlockSpec((count, width), lambda i: (at, 0)), column(width // 2), column(width // 2), column(8)],
        out_shape=[jax.ShapeDtypeStruct((n, width), F32)] + [jax.ShapeDtypeStruct((width // 2, ff), BF16)] * 2 + [jax.ShapeDtypeStruct((8, ff), F32)],
        scratch_shapes=[pltpu.VMEM((count, chunk), BF16), pltpu.VMEM((width + 16, n), BF16)],
        input_output_aliases={7: 0},
        compiler_params=pltpu.CompilerParams(vmem_limit_bytes=VMEM_LIMIT),
        cost_estimate=cost(21),
        name="feed_forward_gradients",
    )(dz, gp, wup, wdown, early, c, order, dc, *after)


def down_grad_body(g_ref, dz_ref, out_ref):
    out_ref[...] = dot(g_ref[...], dz_ref[...], ((0,), (0,))).astype(BF16)


def down_grad(g, dz, after=(), chunk=1280):
    n, ff = g.shape
    width = dz.shape[1]
    waits = len(after)
    return pl.pallas_call(
        lambda *refs: down_grad_body(*refs[:2], *refs[2 + waits:]),
        grid=(ff // chunk,),
        in_specs=[pl.BlockSpec((n, chunk), lambda i: (0, i)), whole(dz.shape)] + tied(waits),
        out_specs=pl.BlockSpec((chunk, width), lambda i: (i, 0)),
        out_shape=jax.ShapeDtypeStruct((ff, width), BF16),
        compiler_params=pltpu.CompilerParams(vmem_limit_bytes=VMEM_LIMIT),
        cost_estimate=cost(12),
        name="down_gradient",
    )(g, dz, *after)


def attn_bwd_body(grads, base_ref, dc_ref, dz_ref, m_ref, h_ref, qkv_ref, e_ref, o_ref, inv_ref, proj_ref, vec_ref, dh_ref, *outs):
    if grads:
        dr_ref, dqkv_ref, small_ref = outs
    width = h_ref.shape[2]
    vec = vec_ref[...]

    if grads:
        @pl.when(pl.program_id(0) == 0)
        def _():
            small_ref[...] = jnp.zeros_like(small_ref) if base_ref is None else base_ref[...]

    dz = dz_ref[0].astype(F32)
    back, g_gain1, g_shift1 = norm_back(m_ref[0], vec[1:2], dc_ref[0])
    dm = dz + back
    dr = dm.astype(BF16)
    if grads:
        dr_ref[0] = dr
    do_all = dot(dr, proj_ref[:, 3 * width:4 * width], ((1,), (1,))).astype(BF16)
    seq = h_ref.shape[1]
    head_of = lax.broadcasted_iota(jnp.int32, (1, 128), 1) // HEAD_DIM
    ones = jnp.ones((seq, 128), BF16)
    zero = jnp.zeros((seq, 128), BF16)
    dq_all, dk_all, dv_all = [], [], []
    for g in range(width // 128):
        at = slice(128 * g, 128 * g + 128)
        q = qkv_ref[0, :, 128 * g:128 * g + 128]
        k = qkv_ref[0, :, width + 128 * g:width + 128 * g + 128]
        v = jnp.concatenate([qkv_ref[0, :, 2 * width + 128 * g:2 * width + 128 * g + 128], ones], axis=1)
        scaled = do_all[:, at].astype(F32) * (inv_ref[0, :, at] * SCALE)
        do = scaled.astype(BF16)
        less = (-scaled * o_ref[0, :, at].astype(F32)).astype(BF16)
        do_t, q_t = do.T, q.T
        dq = None
        dk_t, dv_t = [], []
        stacked = dot(jnp.concatenate([jnp.concatenate([jnp.where(head_of == j, do, zero), jnp.where(head_of == j, less, zero)], axis=1)
                                       for j in range(GROUP)], axis=0), v, ((1,), (1,)))
        for j in range(GROUP):
            mine = head_of == j
            e = e_ref[0, GROUP * g + j]
            rows = slice(HEAD_DIM * j, HEAD_DIM * j + HEAD_DIM)
            dv_t.append(dot(do_t[rows], e))
            dp = stacked[seq * j:seq * j + seq]
            ds = (e.astype(F32) * dp).astype(BF16)
            part = dot(ds, jnp.where(mine, k, zero))
            dq = part if dq is None else dq + part
            dk_t.append(dot(q_t[rows], ds))
        dq_all.append(dq.astype(BF16))
        dk_all.append(jnp.concatenate(dk_t, axis=0).astype(BF16).T)
        dv_all.append((jnp.concatenate(dv_t, axis=0) * (1.0 / SCALE)).astype(BF16).T)
    dqkv = jnp.concatenate(dq_all + dk_all + dv_all, axis=1)
    if grads:
        dqkv_ref[0] = dqkv
    da = dot(dqkv, proj_ref[:, :3 * width], ((1,), (1,)))
    back, g_gain0, g_shift0 = norm_back(h_ref[0].astype(F32), vec[0:1], da)
    dh_ref[0] = (dm + back).astype(dh_ref.dtype)
    if not grads:
        return
    total = lambda x: jnp.sum(x.astype(F32), axis=0, keepdims=True)
    small_ref[...] += jnp.concatenate(
        [g_gain0, g_gain1, g_shift0, g_shift1, total(dqkv[:, :width]), total(dqkv[:, 2 * width:]), total(dr), total(dz)], axis=0)


def attn_bwd(dc, dz, m, h, qkv, e, o, inv, proj, vec, at, parts, grads, earlier=(), after=(), flag=None):
    n, seq, width = h.shape
    count = n // parts
    row = lambda *tail: pl.BlockSpec((1,) + tail, lambda i: (i + at * count,) + (0,) * len(tail))
    if grads:
        shapes = [((seq, width), F32), ((seq, width), BF16), ((seq, 3 * width), BF16)]
        specs = [row(*s) for s, _ in shapes] + [whole((8, width))]
        results = [jax.ShapeDtypeStruct((n,) + s, d) for s, d in shapes] + [jax.ShapeDtypeStruct((8, width), F32)]
    else:
        specs = [pl.BlockSpec((1, seq, width), lambda i: (i, 0, 0))]
        results = [jax.ShapeDtypeStruct((count, seq, width), BF16)]
    args = [dc, dz, m, h, qkv, e, o, inv, proj, vec]
    in_specs = [row(seq, width), row(seq, width), row(seq, width), row(seq, width), row(seq, 3 * width), row(HEADS, seq, seq),
                row(seq, width), row(seq, width), whole(proj.shape), whole(vec.shape)]
    base = len(args)
    if earlier:
        args += [earlier[3], *earlier[:3]]
        in_specs += [whole(earlier[3].shape)] + tied(3)
    aliases = {base + 1 + i: i for i in range(3)} if earlier else {}
    if flag is not None:
        args += [flag]
        in_specs += [pl.BlockSpec(memory_space=pltpu.SMEM)]
    args += after
    in_specs += tied(len(after))
    used = len(args)

    def body(*refs):
        run = lambda: attn_bwd_body(grads, refs[base] if earlier else None, *refs[:base], *refs[used:])
        if flag is None:
            run()
        else:
            pl.when(refs[base][0] > 0)(run)

    return pl.pallas_call(
        body,
        grid=(count,),
        in_specs=in_specs,
        out_specs=specs,
        out_shape=results,
        input_output_aliases=aliases,
        compiler_params=pltpu.CompilerParams(vmem_limit_bytes=VMEM_LIMIT),
        cost_estimate=cost(7 * count),
        name="attention_back",
    )(*args)


def proj_grad_body(a_ref, dqkv_ref, o_ref, dr_ref, small_ref, bias_ref, order_ref, keep_ref, send_ref, at_ref):
    step = pl.program_id(0)
    width = a_ref.shape[1]
    half = width // 2
    order = order_ref[...]

    def put(at, value):
        keep_ref[:, at] = value[:half].astype(BF16)
        send_ref[:, at] = value[half:].astype(BF16)

    @pl.when(step == 0)
    def _():
        at_ref[...] = dot(order, a_ref[...], ((1,), (1,))).astype(BF16)
        put(slice(3 * width, 4 * width), dot(dot(order, o_ref[...], ((1,), (1,))).astype(BF16), dr_ref[...]))
        table = jnp.concatenate([small_ref[...], bias_ref[...], jnp.zeros((112, width), F32)], axis=0).astype(BF16)
        put(slice(4 * width, None), dot(order, table, ((1,), (1,))))

    put(pl.ds(pl.multiple_of(step * width, 128), width), dot(at_ref[...], dqkv_ref[...]))


def proj_grad(a, dqkv, o, dr, small, bias, order, after=()):
    n, width = a.shape
    waits = len(after)
    shape = (width // 2, 4 * width + 128)
    return pl.pallas_call(
        lambda *refs: proj_grad_body(*refs[:7], *refs[7 + waits:]),
        grid=(3,),
        in_specs=[whole(a.shape), pl.BlockSpec((n, width), lambda i: (0, i)), whole(o.shape), whole(dr.shape), whole(small.shape), whole(bias.shape),
                  whole(order.shape)] + tied(waits),
        out_specs=[whole(shape)] * 2,
        out_shape=[jax.ShapeDtypeStruct(shape, BF16)] * 2,
        scratch_shapes=[pltpu.VMEM((width, n), BF16)],
        compiler_params=pltpu.CompilerParams(vmem_limit_bytes=VMEM_LIMIT),
        cost_estimate=cost(9),
        name="projection_gradients",
    )(a, dqkv, o, dr, small, bias, order, *after)


def place_body(count, to_ref, *refs):
    pieces, out_ref, sems = refs[:count], refs[count], refs[count + 1]
    copies = [pltpu.make_async_copy(piece, out_ref.at[to_ref[i]], sems.at[i]) for i, piece in enumerate(pieces)]
    for copy in copies:
        copy.start()
    for copy in copies:
        copy.wait()


def place(pieces, to, after=()):
    rows, columns = pieces[0].shape
    count, waits = len(pieces), len(after)
    out = pl.pallas_call(
        lambda *refs: place_body(count, *refs[:count + 1], *refs[count + 1 + waits:]),
        in_specs=[pl.BlockSpec(memory_space=pltpu.SMEM)] + [pl.BlockSpec(memory_space=pl.ANY)] * count + tied(waits),
        out_specs=pl.BlockSpec(memory_space=pltpu.VMEM),
        out_shape=jax.ShapeDtypeStruct((count, rows, columns), BF16),
        scratch_shapes=[pltpu.SemaphoreType.DMA((count,))],
        compiler_params=pltpu.CompilerParams(vmem_limit_bytes=VMEM_LIMIT),
        cost_estimate=cost(4),
        name="place_pieces",
    )(to, *pieces, *after)
    return out.reshape(count * rows, columns)


def place_down_body(count, to_ref, g_ref, m_ref, vec_ref, *refs):
    pieces, (w_ref, y_ref), (held_ref, act_ref, sems, act_sem, out_sem) = refs[:count], refs[count:count + 2], refs[count + 2:]
    rows = pieces[0].shape[0]
    copies = [pltpu.make_async_copy(piece, held_ref.at[pl.ds(pl.multiple_of(to_ref[i] * rows, rows), rows)], sems.at[i])
              for i, piece in enumerate(pieces)]
    copies.append(pltpu.make_async_copy(g_ref.at[pl.ds(0, act_ref.shape[0])], act_ref, act_sem))
    for copy in copies:
        copy.start()
    for copy in copies:
        copy.wait()
    out = pltpu.make_async_copy(held_ref, w_ref, out_sem)
    out.start()
    y_ref[...] = (m_ref[...] + vec_ref[7:8] + dot(act_ref[...], held_ref[...])).astype(BF16)
    out.wait()


def place_down(pieces, to, g, m, vec):
    rows, width = pieces[0].shape
    count = len(pieces)
    ff = count * rows
    n = g.shape[0]
    return pl.pallas_call(
        lambda *refs: place_down_body(count, *refs),
        grid=(1,),
        in_specs=[pl.BlockSpec(memory_space=pltpu.SMEM)] + tied(1) + [whole((n, width)), whole(vec.shape)] + tied(count),
        out_specs=[pl.BlockSpec(memory_space=pl.ANY), whole((n, width))],
        out_shape=[jax.ShapeDtypeStruct((ff, width), BF16), jax.ShapeDtypeStruct((n, width), BF16)],
        scratch_shapes=[pltpu.VMEM((ff, width), BF16), pltpu.VMEM((n, ff), BF16), pltpu.SemaphoreType.DMA((count,)),
                        pltpu.SemaphoreType.DMA(()), pltpu.SemaphoreType.DMA(())],
        compiler_params=pltpu.CompilerParams(vmem_limit_bytes=VMEM_LIMIT),
        cost_estimate=cost(10),
        name="place_and_feed_forward_down",
    )(to, g, m, vec, *pieces)


def finish_body(rows, per_row, width, *refs):
    *terms, down_ref, qkv_ref, out_ref, gain_ref, shift_ref, bias_ref, up_ref, wide_ref = refs
    wide_ref[0] = down_ref[...].astype(F32)
    total = terms[0][:rows].astype(F32)
    for term in terms[1:]:
        total = total + term[:rows].astype(F32)
    qkv_ref[0] = total[:, :3 * width]
    out_ref[0] = total[:, 3 * width:4 * width]
    small = total[:, 4 * width:]
    vectors = small.T
    gain_ref[0] = vectors[0:2]
    shift_ref[0] = vectors[2:4]
    bias_ref[0] = vectors[4:8]
    flat = rows * per_row
    spread = lax.broadcasted_iota(jnp.int32, (128, flat), 1) % per_row + 8 == lax.broadcasted_iota(jnp.int32, (128, flat), 0)
    wide = lax.dot_general(small, spread.astype(F32), (((1,), (0,)), ((), ())), precision=lax.Precision.HIGHEST, preferred_element_type=F32)
    here = lax.broadcasted_iota(jnp.int32, (rows, flat), 1) // per_row == lax.broadcasted_iota(jnp.int32, (rows, flat), 0)
    up_ref[...] = jnp.sum(jnp.where(here, wide, 0.0), axis=0, keepdims=True)


def finish(large, pieces, down, rows, per_row):
    columns = large[0].shape[1]
    width = (columns - 128) // 4
    shapes = [(1, rows, 3 * width), (1, rows, width), (1, 2, rows), (1, 2, rows), (1, 4, rows), (1, rows * per_row), (1, *down.shape)]
    return pl.pallas_call(
        lambda *refs: finish_body(rows, per_row, width, *refs),
        grid=(1,),
        in_specs=[pl.BlockSpec((2 * rows, columns), lambda i: (0, 0))] * len(large) + [whole(piece.shape) for piece in (*pieces, down)],
        out_specs=[whole(s) for s in shapes],
        out_shape=[jax.ShapeDtypeStruct(s, F32) for s in shapes],
        compiler_params=pltpu.CompilerParams(vmem_limit_bytes=VMEM_LIMIT),
        cost_estimate=cost(2),
        name="gather_projection_gradients",
    )(*large, *pieces, down)


def places(count):
    return count // 4, 2, 2


def hop(value, kind, step=1):
    zs, ys, cores = places(lax.axis_size("dp"))
    pairs = []
    for z in range(zs):
        for y in range(ys):
            for c in range(cores):
                to = {"core": (z, y, c ^ 1), "y": (z, y ^ 1, c), "z": ((z + step) % zs, y, c)}[kind]
                pairs.append(((z * ys + y) * cores + c, (to[0] * ys + to[1]) * cores + to[2]))
    return lax.ppermute(value, "dp", pairs)


def behind_me():
    zs, ys, cores = places(lax.axis_size("dp"))
    me = lax.axis_index("dp")
    return me // (cores * ys), (me // cores) % ys, me % cores


def along_line(shard):
    return [shard] + [hop(shard, "z", step) for step in range(1, places(lax.axis_size("dp"))[0])]


def both(mine, got):
    return (mine.astype(F32) + got.astype(F32)).astype(BF16)


def scatter_order(shard):
    zs, ys, cores = places(lax.axis_size("dp"))
    z, y, c = behind_me()
    row = jnp.arange(zs * ys * cores * shard)
    block = row // shard
    to = (((z + block % zs) % zs) * ys + (y ^ (block // zs % ys))) * cores + (c ^ (block // (zs * ys)))
    return (jnp.arange(zs * ys * cores * shard)[None, :] == (to * shard + row % shard)[:, None]).astype(BF16)


def y_step(mine, got):
    half = mine.shape[0] // 2
    return (mine[:half], got[:half]), hop(both(mine[half:], got[half:]), "y")


def z_step(mine, got):
    zs, _, _ = places(lax.axis_size("dp"))
    rows = got.shape[0] // zs
    terms = [[term[k * rows:k * rows + rows] for term in (*mine, got)] for k in range(zs)]
    return terms[0] + [hop(total(terms[k]).astype(BF16), "z", k) for k in range(1, zs)]


def total(terms):
    out = terms[0].astype(F32)
    for term in terms[1:]:
        out = out + term.astype(F32)
    return out


def held(value, *after):
    return lax.optimization_barrier((value, *after))[0]


def siblings(pieces, *after):
    return [hop(held(piece, *after), "core") for piece in pieces]


def places_of_pieces():
    zs, ys, cores = places(lax.axis_size("dp"))
    z, y, c = behind_me()
    to = []
    for core in (c, 1 - c):
        for row in (y, 1 - y):
            to += [(((z + zs - step) % zs) * ys + row) * cores + core for step in range(zs)]
    return jnp.stack(to).astype(jnp.int32)


def on_device(tokens, lengths, cotangent, w_qkv, w_out, w_up, w_down, norm_gain, norm_bias, bias_vec, up_bias):
    section = lax.axis_index("section")
    windows, seq, width = tokens.shape
    n = windows * seq
    shard = w_qkv.shape[1]
    per_row = up_bias.shape[1] // shard
    ff = w_up.shape[2]
    parts = 2
    part = windows // parts
    by_hand = lax.axis_size("dp") == 16
    table = jnp.concatenate([norm_gain[0], norm_bias[0], bias_vec[0]], axis=0).T
    table = jnp.concatenate([table, up_bias.reshape(shard, per_row)], axis=1)
    used = table.shape[1]
    table = jnp.pad(table, ((0, 0), (0, 128 - used)))
    packed = jnp.concatenate([w_qkv[0], w_out[0], table], axis=1)
    if by_hand:
        down = w_down[0]
        order, to = scatter_order(shard), places_of_pieces()
        wup = lax.all_gather(w_up[0], "dp", axis=0, tiled=True)
        proj_1, proj_3 = hop(packed, "z", 1), hop(packed, "z", 3)
        proj_y0, down_y0 = hop(packed, "y"), hop(down, "y")
        now = (proj_1, proj_3, proj_y0, order)
        proj_2, down_1 = hop(held(packed, *now), "z", 2), hop(held(down, *now), "z", 1)
        proj_y1, proj_y3 = hop(held(proj_1, *now), "y"), hop(held(proj_3, *now), "y")
        now = (proj_2, proj_y1, proj_y3, down_y0, down_1)
        down_3 = hop(held(down, *now), "z", 3)
        proj_y2, down_y1 = hop(held(proj_2, *now), "y"), hop(held(down_1, *now), "y")
        now = (down_3, proj_y2, down_y1)
        pieces = [packed, proj_1, proj_2, proj_3, proj_y0, proj_y1, proj_y2, proj_y3]
        proj = place(pieces + siblings(pieces, proj_y2), to)
        down_2 = hop(held(down, *now), "z", 2)
        down_y3 = hop(held(down_3, *now), "y")
    else:
        order = (jnp.arange(width)[None, :] == jnp.arange(width)[:, None]).astype(BF16)
        proj = lax.all_gather(packed, "dp", axis=0, tiled=True)
        wup = lax.all_gather(w_up[0], "dp", axis=0, tiled=True)
        wdown = lax.all_gather(w_down[0], "dp", axis=0, tiled=True)
    small = proj[:, 4 * width:4 * width + used]
    vec = small[:, :8].T.astype(F32)
    bup = small[:, 8:].reshape(1, ff).astype(F32)

    lengths = jnp.append(lengths, section)
    mid, c = attn_fwd(tokens, lengths, proj, False, after=(vec, bup))
    c = c.reshape(n, width)
    mid = mid.reshape(n, width)
    if by_hand:
        now = (down_2, down_y3, c)
        down_y2 = hop(held(down_2, *now), "y")
    act = mlp_up(c, wup, bup, 0, parts)
    if by_hand:
        pieces = [down, down_1, down_2, down_3, down_y0, down_y1, down_y2, down_y3]
        wdown, y_a = place_down(pieces + siblings(pieces, act), to, act, mid, vec)
    else:
        y_a = mlp_down(act, mid[:n // parts], wdown, vec, 0, 1)
    flag = section.reshape(1).astype(jnp.int32)
    early = pre_grad(cotangent.reshape(n, width), wdown, flag, (y_a,))
    y_b = mlp_fwd(c, mid, wup, wdown, bup, vec, 1, parts, flag, (early,))
    kept = ()
    arrived = [lax.ppermute(y.reshape(part, seq, width), "section", [(0, 1)]) for y in (y_a, y_b)]
    for at in range(parts):
        kept = attn_fwd(tokens, lengths, proj, True, at, parts, held(arrived[at], *kept[:1]), vec, kept)
    m, c, qkv, e, o, a, inv, h = kept
    c = c.reshape(n, width)
    y, g, gp, dc = mlp_both(c, m.reshape(n, width), early, wup, wdown, bup, vec)
    dc = dc.reshape(tokens.shape)
    arrived = []
    for at in range(parts):
        back, = attn_bwd(dc, cotangent, m, h, qkv, e, o, inv, proj, vec, at, parts, False, flag=flag)
        arrived.append(lax.ppermute(back, "section", [(1, 0)]))
    dz = [jnp.where(section == 1, cotangent[:part], arrived[0])]
    dc, du = mlp_bwd(dz[0].reshape(part * seq, width), gp, wup, wdown, True, 0, parts)
    dz.append(jnp.where(section == 1, cotangent[part:], held(arrived[1], dc)))
    last = dz[1].reshape(part * seq, width)
    dz = jnp.concatenate(dz)
    g_down = down_grad(g, dz.reshape(n, width))
    sum_down = lax.psum_scatter(g_down, "dp", scatter_dimension=0, tiled=True)
    dc, keep_u, send_u, bup_u = mlp_grad(last, gp, wup, wdown, du, c, order, dc, (g_down,))
    dc = dc.reshape(tokens.shape)
    if by_hand:
        got_u = hop(send_u, "core")
        half = ff // 2
        rest = keep_u.shape[0] // 2
        mine_a, mine_b = [(keep_u[:rest, at], got_u[:rest, at]) for at in (slice(0, half), slice(half, ff))]
        send_a = both(keep_u[rest:, :half], got_u[rest:, :half])
        got_a = hop(send_a, "y")
        send_b = both(held(keep_u, send_a)[rest:, half:], held(got_u, send_a)[rest:, half:])
        got_b = hop(send_b, "y")
        back = attn_bwd(dc, dz, m, h, qkv, e, o, inv, proj, vec, 0, 1, True, (), (got_u,))
        terms_a = z_step(mine_a, held(got_a, back[3]))
        wait = (got_a,)
    else:
        back = attn_bwd(dc, dz, m, h, qkv, e, o, inv, proj, vec, 0, 1, True)
        wait = ()
    dh, dr, dqkv, smalls = back
    g_bup = bup_u[0].reshape(width, per_row).T
    keep_p, send_p = proj_grad(
        a.reshape(n, width), dqkv.reshape(n, 3 * width), o.reshape(n, width), dr.reshape(n, width), smalls, g_bup, order, wait)
    if by_hand:
        terms_b = z_step(mine_b, got_b)
        sum_up = jnp.concatenate([total(terms_a), total(terms_b)], axis=1)
        core_p = hop(held(send_p, got_b, *terms_a[3:]), "core")
        mine_p, got_p = y_step(keep_p, core_p)
        pieces = z_step(mine_p, held(got_p, *terms_b))[3:]
        *rest, sum_down = finish((keep_p, core_p, got_p), pieces, sum_down, shard, per_row)
    else:
        scatter = lambda *halves: lax.psum_scatter(jnp.concatenate(halves), "dp", scatter_dimension=0, tiled=True).astype(F32)
        sum_up = scatter(keep_u, send_u)
        sum_proj = scatter(keep_p, send_p)
        sum_down = sum_down[None].astype(F32)
        vectors = sum_proj[:, 4 * width:4 * width + 8].T
        rest = (
            sum_proj[None, :, :3 * width],
            sum_proj[None, :, 3 * width:4 * width],
            vectors[None, 0:2],
            vectors[None, 2:4],
            vectors[None, 4:8],
            sum_proj[:, 4 * width + 8:4 * width + used].reshape(1, -1),
        )
    return (y.reshape((1,) + tokens.shape), dh[None], rest[0], rest[1], sum_up[None], sum_down, *rest[2:])


def solution(mesh):
    sharded = [P("section", "dp", None)] * 4 + [P("section", None, "dp")] * 3 + [P("section", "dp")]
    windows = P("dp", None, None)
    out = P("section", "dp", None, None)
    return jax.shard_map(
        on_device, mesh=mesh, in_specs=(windows, P("dp"), windows, *sharded), out_specs=(out, out, *sharded), check_vma=False
    )
```
